128 devices in a mesh: section: 8 (over z_hi, y), ep: 16 (over x, z_lo, core).
Axes of the slice: x: 4, y: 4, z: 4 (z_hi: 2, z_lo: 2; z = z_hi * 2 + z_lo), core: 2. Of those that a mesh axis runs over, the one named last changes fastest.
Arguments:
- pending: bfloat16 [8, 2048, 7168], P('section', 'ep'), may hold values from -6 to 6
- expert_ids: int32 [8, 2048, 2], P('section', 'ep'), may hold values from 0 to 3, all different within a row; in each aligned block of 128 rows (0 to 127, 128 to 255, ..., all dimensions but the last counted through in order) at most 72 rows name the same one
- route_weight: float32 [8, 2048, 2], P('section', 'ep'), may hold values from 0.1 to 0.9
- gate_saved: bfloat16 [8, 1152, 4096], P('section', None, 'ep'), may hold values from -8 to 8
- up_saved: bfloat16 [8, 1152, 4096], P('section', None, 'ep'), may hold values from -8 to 8
- w_gate: bfloat16 [8, 7168, 4096], P('section', None, 'ep'), may hold values from -0.0625 to 0.0625
- w_up: bfloat16 [8, 7168, 4096], P('section', None, 'ep'), may hold values from -0.0625 to 0.0625
- w_down: bfloat16 [8, 4096, 7168], P('section', 'ep'), may hold values from -0.1875 to 0.1875
Outputs:
- upstream: bfloat16 [8, 2048, 7168], P('section', 'ep')
- down_grad: float32 [8, 4096, 7168], P('section', 'ep')
The draws below stay inside these ranges and needn't reach their ends.
Inputs may be any that keep to these rules, and one draw needn't show every extreme that they name: `expert_ids`: each token names 2 different experts. In each aligned block of 128 tokens (the tokens of one device) no expert is named more than 72 times, and in every draw some block names some expert exactly 72 times.
All inputs are finite; a program needn't handle non-finite values.
Results may differ from the reference program's by a relative error of at most 0.006.
Values may be sent and summed in bfloat16 or wider, within the bound.
No kernel may reach another device: no remote copies, remote signals or barrier semaphores. Data moves between devices by JAX's collectives and lax.ppermute only.
A program may use at most 256 MiB of HBM per device.

```python
import math
import jax
import jax.numpy as jnp
import numpy as np
from jax import lax

D = 7168
HID = 1024
SHARDS = 4
HID_DEV = 256
TOPK = 2
TOK_DEV = 128
EXPERTS = 4
TOKENS = 2048
CAP = 72
N_SECTION = 8
N_EP = 16


def steps_of(key, dims, cuts, low, top_value):
    def one(position, shards_of):
        draws = jax.random.uniform(jax.random.fold_in(jax.random.fold_in(key, 6), position), (shards_of,), jnp.float32, low / len(cuts), top_value / len(cuts))
        return jnp.repeat(jnp.exp(draws), dims[position] // shards_of).reshape((-1,) + (1,) * (len(dims) - position - 1))

    gain = one(*cuts[0])
    for cut in cuts[1:]:
        gain = gain * one(*cut)
    return gain


def shared_out(own_key, own, number, rows, number_of, top, limit, skew):
    order = jax.random.permutation(own_key, number_of)
    crowded, common = load_shares(number_of, rows * top, limit, skew, True), load_shares(number_of, rows * top, limit, skew, False)
    places = jnp.arange(number_of)

    def named(lengths, offset_by):
        used = int((lengths > 0).sum())
        fixed = max(1, used // 4)
        shifted = fixed + (places - fixed + offset_by * (used - fixed)) % max(1, number_of - fixed)
        return jnp.zeros((number_of,), jnp.int32).at[order[jnp.where(places < fixed, places, shifted)]].set(jnp.asarray(lengths, jnp.int32))

    lengths = jnp.where(number % 4 == 0, named(crowded, number // 4), named(common, number - number // 4 - 1))
    mixed = jax.random.permutation(jax.random.fold_in(own, 3), number_of)
    donor, receiver = mixed[0:number_of // 2 * 2:2], mixed[1:number_of // 2 * 2:2]
    margin = jnp.minimum(lengths[donor] - 1, limit - lengths[receiver]) // 2
    margin = jnp.where((donor == order[0]) | (receiver == order[0]) | (lengths[receiver] == 0), 0, jnp.maximum(margin, 0))
    shifted = jax.random.randint(jax.random.fold_in(own, 4), (number_of // 2,), 0, 1 << 20) % (margin + 1)
    lengths = lengths.at[donor].add(-shifted).at[receiver].add(shifted)
    members = jnp.searchsorted(jnp.cumsum(lengths), jnp.arange(rows * top), side="right").astype(jnp.int32)
    table = members.reshape(top, rows).T
    table = table[jax.random.permutation(jax.random.fold_in(own, 1), rows)]
    offset_by = jax.random.randint(jax.random.fold_in(own, 2), (rows, 1), 0, top)
    return jnp.take_along_axis(table, (jnp.arange(top)[None, :] + offset_by) % top, axis=1)


def load_shares(amount, total, reach, skew, full):
    portions = [(1 << 20) // math.isqrt(standing ** skew) + 1 for standing in range(1, amount + 1)]
    largest = reach if full else min(reach, max(-(-total // amount), total * portions[0] // sum(portions)))
    least = 1 if total - largest >= amount - 1 else 0
    given, surplus = [largest] + [least] * (amount - 1), total - largest - least * (amount - 1)
    while surplus > 0:
        movable = [i for i in range(1, amount) if given[i] < largest] or [i for i in range(1, amount) if given[i] < reach]
        whole, remaining = sum([portions[i] for i in movable]), surplus
        for i in movable:
            addition = min(reach - given[i], max(1, remaining * portions[i] // whole), surplus)
            given[i] = given[i] + addition
            surplus = surplus - addition
    return np.array(given)


def normal_values(rng, dims, scale, reach, shards=(), kind=jnp.bfloat16):
    array = scale * jax.random.normal(rng, dims, jnp.float32)
    if shards:
        array = array * steps_of(rng, dims, shards, -0.22, 0.18)
    return jnp.clip(array, -reach, reach).astype(kind)


def setup_inputs(seed: int = 0) -> dict:
    keys = jax.random.split(jax.random.key(seed), 9)
    pending = normal_values(keys[0], (N_SECTION, TOKENS, D), 1.0, 6.0, ((0, 8), (1, 16)))
    expert_ids_keys = jax.random.split(jax.random.fold_in(keys[1], 1), N_SECTION * TOKENS // TOK_DEV)
    expert_ids_turns = jax.random.permutation(jax.random.fold_in(keys[1], 3), N_SECTION * TOKENS // TOK_DEV)
    expert_ids = jax.vmap(lambda own, number: shared_out(jax.random.fold_in(keys[1], 2), own, number, TOK_DEV, EXPERTS, TOPK, CAP, 2))(expert_ids_keys, expert_ids_turns).reshape((N_SECTION, TOKENS, TOPK))
    route_weight = jnp.clip(0.1 + 0.79999997 * jax.random.uniform(keys[2], (N_SECTION, TOKENS, TOPK), jnp.float32) ** steps_of(keys[2], (N_SECTION, TOKENS, TOPK), ((0, 8), (1, 16)), -0.2, 0.2), 0.1, 0.9)
    gate_saved = normal_values(keys[3], (N_SECTION, N_EP * CAP, EXPERTS * HID), 1.5, 8.0, ((0, 8), (2, 16)))
    up_saved = normal_values(keys[4], (N_SECTION, N_EP * CAP, EXPERTS * HID), 1.5, 8.0, ((0, 8), (2, 16)))
    w_gate = normal_values(keys[5], (N_SECTION, D, EXPERTS * HID), D ** -0.5, 0.0625, ((0, 8), (2, 16)))
    w_up = normal_values(keys[6], (N_SECTION, D, EXPERTS * HID), D ** -0.5, 0.0625, ((0, 8), (2, 16)))
    w_down = normal_values(keys[7], (N_SECTION, EXPERTS * HID, D), HID ** -0.5, 0.1875, ((0, 8), (1, 16)))
    return {"pending": pending, "expert_ids": expert_ids, "route_weight": route_weight, "gate_saved": gate_saved, "up_saved": up_saved, "w_gate": w_gate, "w_up": w_up, "w_down": w_down}


def section_backward(incoming, ids, probs, gate_saved, up_saved, w_gate, w_up, w_down):
    width = incoming.shape[1]
    blocks = ids.reshape(N_EP, TOK_DEV * TOPK)
    onehot = (blocks[:, :, None] == jnp.arange(EXPERTS, dtype=jnp.int32)[None, None, :]).astype(jnp.int32)
    ranks = jnp.sum((jnp.cumsum(onehot, axis=1) - onehot) * onehot, axis=2)
    source = jnp.arange(N_EP, dtype=jnp.int32)[:, None]
    target = (blocks * (N_EP * CAP) + source * CAP + ranks).reshape(-1).astype(jnp.int32)
    scaled = (jnp.repeat(incoming.astype(jnp.float32), TOPK, axis=0) * probs.reshape(-1)[:, None]).astype(jnp.bfloat16)
    packed = jnp.zeros((EXPERTS * N_EP * CAP, width), jnp.bfloat16).at[target].set(scaled)
    packed = packed.reshape(EXPERTS, N_EP * CAP, width)
    sums = []
    grads = []
    for expert in range(EXPERTS):
        rows = packed[expert]
        low = expert * HID
        gate = gate_saved[:, low:low + HID].astype(jnp.float32)
        upval = up_saved[:, low:low + HID].astype(jnp.float32)
        sig = jax.nn.sigmoid(gate)
        slope = jnp.dot(rows, w_down[low:low + HID].T, preferred_element_type=jnp.float32)
        dgate = (slope * upval * sig * (1.0 + gate * (1.0 - sig))).astype(jnp.bfloat16)
        dupval = (slope * gate * sig).astype(jnp.bfloat16)
        hidden = (gate * sig * upval).astype(jnp.bfloat16)
        total = jnp.zeros((N_EP * CAP, width), jnp.float32)
        for shard in range(SHARDS):
            first = shard * HID_DEV
            last = first + HID_DEV
            part = jnp.dot(dgate[:, first:last], w_gate[:, low + first:low + last].T, preferred_element_type=jnp.float32)
            part = part + jnp.dot(dupval[:, first:last], w_up[:, low + first:low + last].T, preferred_element_type=jnp.float32)
            total = total + lax.optimization_barrier(part.astype(jnp.bfloat16)).astype(jnp.float32)
        sums.append(total)
        grads.append(jnp.dot(hidden.T, rows, preferred_element_type=jnp.float32))
    flat = jnp.concatenate(sums, axis=0)
    branch = jnp.take(flat, target, axis=0).reshape(-1, TOPK, width).sum(axis=1)
    branch = lax.optimization_barrier(branch.astype(jnp.bfloat16)).astype(jnp.float32)
    grad_in = (incoming.astype(jnp.float32) + branch).astype(jnp.bfloat16)
    return grad_in, jnp.concatenate(grads, axis=0)


def reference(pending, expert_ids, route_weight, gate_saved, up_saved, w_gate, w_up, w_down):
    incoming_all = jnp.roll(pending, -1, axis=0)
    outs = []
    grads = []
    for section in range(N_SECTION):
        grad_in, grad_down = section_backward(incoming_all[section], expert_ids[section], route_weight[section], gate_saved[section], up_saved[section], w_gate[section], w_up[section], w_down[section])
        outs.append(grad_in)
        grads.append(grad_down)
    upstream = jnp.roll(jnp.stack(outs, axis=0), -1, axis=0)
    return upstream, jnp.stack(grads, axis=0)
```

```python
import functools

import jax
import jax.numpy as jnp
from jax import lax
from jax.experimental import pallas as pl
from jax.experimental.pallas import tpu as pltpu
from jax.sharding import PartitionSpec as P

NX, NZ, NC = 4, 2, 2
F32, BF16 = jnp.float32, jnp.bfloat16
PARAMS = pltpu.CompilerParams(vmem_limit_bytes=40 << 20)
CHUNKS = (("B", 7), ("A", 7), ("B", 7), ("A", 7))
CONTRACT_LAST = (((1,), (1,)), ((), ()))


def section_move(array):
    peers = lax.axis_size("section")
    return lax.ppermute(array, "section", [(i, (i - 1) % peers) for i in range(peers)])


def ep_move(array, dx=0, dz=0, dc=0):
    pairs = []
    for q in range(NX * NZ * NC):
        x, z, c = q // (NZ * NC), q // NC % NZ, q % NC
        pairs.append((q, (x + dx) % NX * NZ * NC + (z ^ dz) * NC + (c ^ dc)))
    return lax.ppermute(array, "ep", pairs)


def whole(shape):
    return pl.BlockSpec(shape, lambda *_: (0,) * len(shape))


def tile_of(columns):
    return 256 if columns % 256 == 0 else 128


def route_kernel(cap, x_ref, info_ref, place_ref, place_t_ref, weight_ref):
    tokens = info_ref.shape[1]
    row = lax.broadcasted_iota(jnp.int32, (tokens, tokens), 0)
    col = lax.broadcasted_iota(jnp.int32, (tokens, tokens), 1)
    before = (row < col).astype(F32).astype(BF16)
    slot_of = lax.broadcasted_iota(jnp.int32, (cap, tokens), 0).astype(F32)
    places, weights = [], []
    for d in range(NX):
        expert = lax.rem(x_ref[0] + d, NX).astype(F32)
        first = info_ref[0:1, :] == expert
        second = info_ref[1:2, :] == expert
        named = jnp.where(first | second, 1.0, 0.0)
        prob = jnp.where(first, info_ref[2:3, :], jnp.where(second, info_ref[3:4, :], 0.0))
        rank = jnp.dot(
            jnp.broadcast_to(named, (8, tokens)).astype(BF16), before, preferred_element_type=F32
        )[0:1]
        placed = jnp.where((slot_of == rank) & (named > 0.0), 1.0, 0.0)
        places.append(placed)
        weights.append(
            jnp.broadcast_to(jnp.sum(placed * prob, axis=1, keepdims=True), (cap, 128))
        )
    place = jnp.concatenate(places, axis=0)
    place_ref[...] = place.astype(BF16)
    weight_ref[...] = jnp.concatenate(weights, axis=0)
    eye = (row == col).astype(F32).astype(BF16)
    place_t_ref[...] = lax.dot_general(
        eye, place.astype(BF16), CONTRACT_LAST, preferred_element_type=F32
    ).astype(BF16)


def route(x, info, cap):
    tokens = info.shape[1]
    slots = NX * cap
    return pl.pallas_call(
        functools.partial(route_kernel, cap),
        in_specs=[pl.BlockSpec(memory_space=pltpu.SMEM), whole(info.shape)],
        out_specs=[whole((slots, tokens)), whole((tokens, slots)), whole((slots, 128))],
        out_shape=[
            jax.ShapeDtypeStruct((slots, tokens), BF16),
            jax.ShapeDtypeStruct((tokens, slots), BF16),
            jax.ShapeDtypeStruct((slots, 128), F32),
        ],
        grid=(1,),
        compiler_params=PARAMS,
    )(x, info)


def saved_kernel(cap, at_ref, gate_ref, up_ref, f1_ref, f2_ref, ha_ref, hb_ref, g3, u3, h3):
    g3[...] = gate_ref[...].astype(F32).reshape(g3.shape)
    u3[...] = up_ref[...].astype(F32).reshape(u3.shape)
    x, z, c = at_ref[0], at_ref[1], at_ref[2]
    for cr in range(NC):
        for zr in range(NZ):
            for d in range(NX):
                j = (cr * NZ + zr) * NX + d
                jb = (cr * NX + d) * NZ + zr
                zs = z if zr == 0 else 1 - z
                cs = c if cr == 0 else 1 - c
                q = lax.rem(x + NX - d, NX) * (NZ * NC) + zs * NC + cs
                gate, upval = g3[q], u3[q]
                sig = jax.nn.sigmoid(gate)
                f1_ref[pl.ds(j * cap, cap), :] = upval * sig * (1.0 + gate * (1.0 - sig))
                f2_ref[pl.ds(j * cap, cap), :] = gate * sig
                h3[pl.ds(j * cap, cap), :] = gate * sig * upval
    ha_ref[...] = h3[...].astype(BF16)
    reorder_to_b(cap, h3, g3)
    hb_ref[...] = g3[...].reshape(hb_ref.shape).astype(BF16)


def reorder_to_b(cap, flat, blocks):
    for cr in range(NC):
        for zr in range(NZ):
            for d in range(NX):
                j = (cr * NZ + zr) * NX + d
                blocks[(cr * NX + d) * NZ + zr] = flat[pl.ds(j * cap, cap), :]


def saved(at, gate, up, cap):
    rows, hid = gate.shape
    blocks = rows // cap
    return pl.pallas_call(
        functools.partial(saved_kernel, cap),
        in_specs=[pl.BlockSpec(memory_space=pltpu.SMEM), whole(gate.shape), whole(up.shape)],
        out_specs=[whole((rows, hid))] * 4,
        out_shape=[jax.ShapeDtypeStruct((rows, hid), t) for t in (F32, F32, BF16, BF16)],
        scratch_shapes=[
            pltpu.VMEM((blocks, cap, hid), F32),
            pltpu.VMEM((blocks, cap, hid), F32),
            pltpu.VMEM((rows, hid), F32),
        ],
        grid=(1,),
        compiler_params=PARAMS,
    )(at, gate, up)


def pack_a_kernel(cap, place_ref, weight_ref, tok_ref, *outs):
    rows = jnp.dot(place_ref[...], tok_ref[...], preferred_element_type=F32)
    rows = rows * weight_ref[:, 0:1]
    for d in range(NX):
        outs[d][...] = rows[d * cap : (d + 1) * cap].astype(BF16)


def pack_a(place, weight, tok, cap):
    tokens, columns = tok.shape
    tile = tile_of(columns)
    return pl.pallas_call(
        functools.partial(pack_a_kernel, cap),
        in_specs=[
            whole(place.shape),
            whole(weight.shape),
            pl.BlockSpec((tokens, tile), lambda j: (0, j)),
        ],
        out_specs=[pl.BlockSpec((cap, tile), lambda j: (0, j))] * NX,
        out_shape=[jax.ShapeDtypeStruct((cap, columns), BF16)] * NX,
        grid=(columns // tile,),
        compiler_params=PARAMS,
    )(place, weight, tok)


def pack_b_kernel(cap, place0_ref, weight0_ref, place1_ref, weight1_ref, tok0_ref, tok1_ref, *outs):
    rows0 = jnp.dot(place0_ref[...], tok0_ref[...], preferred_element_type=F32)
    rows0 = rows0 * weight0_ref[:, 0:1]
    rows1 = jnp.dot(place1_ref[...], tok1_ref[...], preferred_element_type=F32)
    rows1 = rows1 * weight1_ref[:, 0:1]
    for d in range(NX):
        low, high = d * cap, (d + 1) * cap
        outs[d][...] = jnp.concatenate([rows0[low:high], rows1[low:high]], axis=0).astype(BF16)


def pack_b(place0, weight0, place1, weight1, tok0, tok1, cap):
    tokens, columns = tok0.shape
    tile = tile_of(columns)
    return pl.pallas_call(
        functools.partial(pack_b_kernel, cap),
        in_specs=[
            whole(place0.shape),
            whole(weight0.shape),
            whole(place1.shape),
            whole(weight1.shape),
            pl.BlockSpec((tokens, tile), lambda j: (0, j)),
            pl.BlockSpec((tokens, tile), lambda j: (0, j)),
        ],
        out_specs=[pl.BlockSpec((NZ * cap, tile), lambda j: (0, j))] * NX,
        out_shape=[jax.ShapeDtypeStruct((NZ * cap, columns), BF16)] * NX,
        grid=(columns // tile,),
        compiler_params=PARAMS,
    )(place0, weight0, place1, weight1, tok0, tok1)


def rows_kernel(groups, with_sum, with_grad, *refs):
    rows, refs = refs[:groups], refs[groups:]
    wd_ref, hid_ref = refs[:2]
    sum_in = refs[2] if with_sum else None
    sum_ref, grad_ref = refs[2 + with_sum + with_grad :]

    @pl.when(pl.program_id(0) == 0)
    def _():
        sum_ref[...] = jnp.zeros_like(sum_ref) if sum_in is None else sum_in[...]

    wd = wd_ref[...]
    grad = None
    for g in range(groups):
        block = rows[g][...]
        many = block.shape[0]
        sum_ref[pl.ds(g * many, many), :] += lax.dot_general(
            block, wd, CONTRACT_LAST, preferred_element_type=F32
        )
        more = jnp.dot(hid_ref[g], block, preferred_element_type=F32)
        grad = more if grad is None else grad + more
    grad_ref[...] = grad


def use_rows(rows, w_down, hid_t, dh, grad, start):
    groups = len(rows)
    many, columns = rows[0].shape
    hid, width = w_down.shape
    tile = tile_of(columns)
    first = start // tile
    at = pl.BlockSpec((hid, tile), lambda j: (0, first + j))
    operands = list(rows) + [w_down, hid_t]
    specs = [pl.BlockSpec((many, tile), lambda j: (0, j))] * groups + [at, whole(hid_t.shape)]
    aliases = {}
    if dh is not None:
        operands.append(dh)
        specs.append(whole(dh.shape))
    if grad is not None:
        aliases[len(operands)] = 1
        operands.append(grad)
        specs.append(pl.BlockSpec(memory_space=pl.ANY))
    return pl.pallas_call(
        functools.partial(rows_kernel, groups, dh is not None, grad is not None),
        in_specs=specs,
        out_specs=[whole((groups * many, hid)), at],
        out_shape=[
            jax.ShapeDtypeStruct((groups * many, hid), F32),
            jax.ShapeDtypeStruct((hid, width), F32),
        ],
        grid=(columns // tile,),
        input_output_aliases=aliases,
        compiler_params=PARAMS,
    )(*operands)


def act_kernel(cap, dha_ref, dhb_ref, f1_ref, f2_ref, ga_ref, ua_ref, gb_ref, ub_ref, flat, blocks):
    b3 = dhb_ref[...].reshape(blocks.shape)
    for cr in range(NC):
        for zr in range(NZ):
            for d in range(NX):
                j = (cr * NZ + zr) * NX + d
                here = pl.ds(j * cap, cap)
                flat[here, :] = dha_ref[here, :] + b3[(cr * NX + d) * NZ + zr]
    dh = flat[...]
    dgate = dh * f1_ref[...]
    dup = dh * f2_ref[...]
    ga_ref[...] = dgate.astype(BF16)
    ua_ref[...] = dup.astype(BF16)
    flat[...] = dgate
    reorder_to_b(cap, flat, blocks)
    gb_ref[...] = blocks[...].reshape(gb_ref.shape).astype(BF16)
    flat[...] = dup
    reorder_to_b(cap, flat, blocks)
    ub_ref[...] = blocks[...].reshape(ub_ref.shape).astype(BF16)


def activations(dha, dhb, f1, f2, cap):
    rows, hid = dha.shape
    return pl.pallas_call(
        functools.partial(act_kernel, cap),
        in_specs=[whole((rows, hid))] * 4,
        out_specs=[whole((rows, hid))] * 4,
        out_shape=[jax.ShapeDtypeStruct((rows, hid), BF16)] * 4,
        scratch_shapes=[
            pltpu.VMEM((rows, hid), F32),
            pltpu.VMEM((rows // cap, cap, hid), F32),
        ],
        grid=(1,),
        compiler_params=PARAMS,
    )(dha, dhb, f1, f2)


def part_kernel(pieces, with_other, dg_ref, du_ref, wg_ref, wu_ref, *refs):
    total = lax.dot_general(dg_ref[...], wg_ref[...], CONTRACT_LAST, preferred_element_type=F32)
    total += lax.dot_general(du_ref[...], wu_ref[...], CONTRACT_LAST, preferred_element_type=F32)
    if with_other:
        total += refs[0][...].astype(F32)
    outs = refs[with_other:]
    many = total.shape[0] // pieces
    for i in range(pieces):
        outs[i][...] = total[i * many : (i + 1) * many].astype(BF16)


def parts_of(dg, du, wg, wu, start, columns, half, other, pieces):
    rows, hid = dg.shape
    many = rows // NC
    tile = tile_of(columns)
    first = start // tile
    of_half = pl.BlockSpec((many, hid), lambda j: (half, 0))
    weights = pl.BlockSpec((tile, hid), lambda j: (first + j, 0))
    operands = [dg, du, wg, wu]
    specs = [of_half, of_half, weights, weights]
    if other is not None:
        operands.append(other)
        specs.append(pl.BlockSpec((many, tile), lambda j: (0, j)))
    return pl.pallas_call(
        functools.partial(part_kernel, pieces, other is not None),
        in_specs=specs,
        out_specs=[pl.BlockSpec((many // pieces, tile), lambda j: (0, j))] * pieces,
        out_shape=[jax.ShapeDtypeStruct((many // pieces, columns), BF16)] * pieces,
        grid=(columns // tile,),
        compiler_params=PARAMS,
    )(*operands)


def sum_z_kernel(cap, a_ref, b_ref, *outs):
    total = a_ref[...].astype(F32) + b_ref[...].astype(F32)
    for d in range(NX):
        outs[d][...] = total[d * cap : (d + 1) * cap].astype(BF16)


def sum_z(a, b, cap):
    rows, columns = a.shape
    tile = tile_of(columns)
    return pl.pallas_call(
        functools.partial(sum_z_kernel, cap),
        in_specs=[pl.BlockSpec((rows, tile), lambda j: (0, j))] * 2,
        out_specs=[pl.BlockSpec((cap, tile), lambda j: (0, j))] * NX,
        out_shape=[jax.ShapeDtypeStruct((cap, columns), BF16)] * NX,
        grid=(columns // tile,),
        compiler_params=PARAMS,
    )(a, b)


def finish_a_kernel(place_t_ref, tok_ref, *refs):
    blocks, out_ref = refs[:NX], refs[NX]
    rows = jnp.concatenate([b[...].astype(F32) for b in blocks], axis=0).astype(BF16)
    branch = jnp.dot(place_t_ref[...], rows, preferred_element_type=F32).astype(BF16)
    out_ref[...] = (tok_ref[...].astype(F32) + branch.astype(F32)).astype(BF16)


def finish_a(place_t, tok, blocks):
    tokens, columns = tok.shape
    cap = blocks[0].shape[0]
    tile = tile_of(columns)
    at = pl.BlockSpec((tokens, tile), lambda j: (0, j))
    return pl.pallas_call(
        finish_a_kernel,
        in_specs=[whole(place_t.shape), at]
        + [pl.BlockSpec((cap, tile), lambda j: (0, j))] * NX,
        out_specs=at,
        out_shape=jax.ShapeDtypeStruct((tokens, columns), BF16),
        grid=(columns // tile,),
        compiler_params=PARAMS,
    )(place_t, tok, *blocks)


def combine_b_kernel(cap, place0_ref, place1_ref, *refs):
    blocks, own_ref, other_ref = refs[:NX], refs[NX], refs[NX + 1]
    wide = [b[...].astype(F32) for b in blocks]
    for zr, (place_ref, out_ref) in enumerate(((place0_ref, own_ref), (place1_ref, other_ref))):
        rows = jnp.concatenate([b[zr * cap : (zr + 1) * cap] for b in wide], axis=0).astype(BF16)
        total = jnp.dot(place_ref[...], rows, preferred_element_type=F32)
        out_ref[...] = total.astype(out_ref.dtype)


def combine_b(place0_t, place1_t, blocks):
    tokens = place0_t.shape[0]
    many, columns = blocks[0].shape
    tile = tile_of(columns)
    at = pl.BlockSpec((tokens, tile), lambda j: (0, j))
    return pl.pallas_call(
        functools.partial(combine_b_kernel, many // NZ),
        in_specs=[whole(place0_t.shape), whole(place1_t.shape)]
        + [pl.BlockSpec((many, tile), lambda j: (0, j))] * NX,
        out_specs=[at, at],
        out_shape=[
            jax.ShapeDtypeStruct((tokens, columns), F32),
            jax.ShapeDtypeStruct((tokens, columns), BF16),
        ],
        grid=(columns // tile,),
        compiler_params=PARAMS,
    )(place0_t, place1_t, *blocks)


def finish_b_kernel(own_ref, other_ref, tok_ref, out_ref):
    branch = (own_ref[...] + other_ref[...].astype(F32)).astype(BF16)
    out_ref[...] = (tok_ref[...].astype(F32) + branch.astype(F32)).astype(BF16)


def finish_b(own, other, tok):
    tokens, columns = tok.shape
    tile = tile_of(columns)
    at = pl.BlockSpec((tokens, tile), lambda j: (0, j))
    return pl.pallas_call(
        finish_b_kernel,
        in_specs=[at, at, at],
        out_specs=at,
        out_shape=jax.ShapeDtypeStruct((tokens, columns), BF16),
        grid=(columns // tile,),
        compiler_params=PARAMS,
    )(own, other, tok)


def body(pending, expert_ids, route_weight, gate_saved, up_saved, w_gate, w_up, w_down):
    own = pending[0]
    width = own.shape[1]
    rows, hid = gate_saved.shape[1:]
    cap = rows // (NX * NZ * NC)
    w_gate, w_up, w_down = w_gate[0], w_up[0], w_down[0]
    chunks, start = [], 0
    for kind, size in CHUNKS:
        columns = size * width // 28
        chunks.append((kind, start, columns))
        start += columns

    incoming = [section_move(own[:, low : low + n]) for _, low, n in chunks]
    position = lax.axis_index("ep").astype(jnp.int32)
    x, z, c = position // (NZ * NC), position // NC % NZ, position % NC
    at = jnp.stack([x, z, c])
    info = jnp.concatenate([expert_ids[0].astype(F32), route_weight[0]], axis=1).T
    place0, place0_t, weight0 = route(at, info, cap)
    place1, place1_t, weight1 = route(at, ep_move(info, dz=1), cap)
    f1, f2, hid_a, hid_b = saved(at, gate_saved[0], up_saved[0], cap)
    hid_a = hid_a.reshape(NC * NZ, -1, hid).transpose(0, 2, 1)
    hid_b = hid_b.reshape(NC, -1, hid).transpose(0, 2, 1)

    dh = {"A": None, "B": None}
    grad = None
    for (kind, low, n), tok in zip(chunks, incoming):
        if kind == "A":
            sent = pack_a(place0, weight0, tok, cap)
            got = [sent[0]] + [ep_move(sent[d], dx=d) for d in range(1, NX)]
            near = jnp.concatenate(got, axis=0)
            far = ep_move(near, dz=1)
            groups = [near, far, ep_move(near, dc=1), ep_move(far, dc=1)]
            hid_t = hid_a
        else:
            across = ep_move(tok, dz=1)
            sent = pack_b(place0, weight0, place1, weight1, tok, across, cap)
            got = [sent[0]] + [ep_move(sent[d], dx=d) for d in range(1, NX)]
            near = jnp.concatenate(got, axis=0)
            groups = [near, ep_move(near, dc=1)]
            hid_t = hid_b
        dh[kind], grad = use_rows(groups, w_down, hid_t, dh[kind], grad, low)

    dg_a, du_a, dg_b, du_b = activations(dh["A"], dh["B"], f1, f2, cap)
    outs = []
    for (kind, low, n), tok in zip(chunks, incoming):
        dg, du = (dg_a, du_a) if kind == "A" else (dg_b, du_b)
        (theirs,) = parts_of(dg, du, w_gate, w_up, low, n, 1, None, 1)
        theirs = ep_move(theirs, dc=1)
        if kind == "A":
            keep, send = parts_of(dg, du, w_gate, w_up, low, n, 0, theirs, NZ)
            pieces = sum_z(keep, ep_move(send, dz=1), cap)
            got = [pieces[0]] + [ep_move(pieces[d], dx=-d) for d in range(1, NX)]
            done = finish_a(place0_t, tok, got)
        else:
            pieces = parts_of(dg, du, w_gate, w_up, low, n, 0, theirs, NX)
            got = [pieces[0]] + [ep_move(pieces[d], dx=-d) for d in range(1, NX)]
            mine, send = combine_b(place0_t, place1_t, got)
            done = finish_b(mine, ep_move(send, dz=1), tok)
        outs.append(section_move(done))
    return (jnp.concatenate(outs, axis=1)[None], grad[None])


def solution(mesh):
    placed = (
        P("section", "ep", None),
        P("section", "ep", None),
        P("section", "ep", None),
        P("section", None, "ep"),
        P("section", None, "ep"),
        P("section", None, "ep"),
        P("section", None, "ep"),
        P("section", "ep", None),
    )
    return jax.shard_map(
        body,
        mesh=mesh,
        in_specs=placed,
        out_specs=(P("section", "ep", None), P("section", "ep", None)),
        check_vma=False,
    )
```

```python
import functools

import jax
import jax.numpy as jnp
from jax import lax
from jax.experimental import pallas as pl
from jax.experimental.pallas import tpu as pltpu
from jax.sharding import PartitionSpec as P

NX, NZ, NC = 4, 2, 2
F32, BF16 = jnp.float32, jnp.bfloat16
PARAMS = pltpu.CompilerParams(vmem_limit_bytes=28 << 20)
EARLY, LATE = (5, 5), (9, 9)
CONTRACT_LAST = (((1,), (1,)), ((), ()))


def section_move(array):
    peers = lax.axis_size("section")
    return lax.ppermute(array, "section", [(i, (i - 1) % peers) for i in range(peers)])


def ep_move(array, dx=0, dz=0, dc=0):
    pairs = []
    for q in range(NX * NZ * NC):
        x, z, c = q // (NZ * NC), q // NC % NZ, q % NC
        pairs.append((q, (x + dx) % NX * NZ * NC + (z ^ dz) * NC + (c ^ dc)))
    return lax.ppermute(array, "ep", pairs)


def x_exchange(array):
    groups = [[x * NZ * NC + i for x in range(NX)] for i in range(NZ * NC)]
    blocks = array.reshape(NX, -1, array.shape[1])
    moved = lax.all_to_all(blocks, "ep", 0, 0, axis_index_groups=groups, tiled=True)
    return moved.reshape(array.shape)


def whole(shape):
    return pl.BlockSpec(shape, lambda *_: (0,) * len(shape))


def tile_of(columns):
    return columns


def route_kernel(cap, x_ref, info_ref, place_ref, place_t_ref, weight_ref):
    tokens = info_ref.shape[1]
    row = lax.broadcasted_iota(jnp.int32, (tokens, tokens), 0)
    col = lax.broadcasted_iota(jnp.int32, (tokens, tokens), 1)
    before = (row < col).astype(F32).astype(BF16)
    slot_of = lax.broadcasted_iota(jnp.int32, (cap, tokens), 0).astype(F32)
    places, weights = [], []
    for d in range(NX):
        expert = lax.rem(x_ref[0] + d, NX).astype(F32)
        first = info_ref[0:1, :] == expert
        second = info_ref[1:2, :] == expert
        named = jnp.where(first | second, 1.0, 0.0)
        prob = jnp.where(first, info_ref[2:3, :], jnp.where(second, info_ref[3:4, :], 0.0))
        rank = jnp.dot(
            jnp.broadcast_to(named, (8, tokens)).astype(BF16), before, preferred_element_type=F32
        )[0:1]
        placed = jnp.where((slot_of == rank) & (named > 0.0), 1.0, 0.0)
        places.append(placed)
        weights.append(
            jnp.broadcast_to(jnp.sum(placed * prob, axis=1, keepdims=True), (cap, 128))
        )
    place = jnp.concatenate(places, axis=0)
    place_ref[...] = place.astype(BF16)
    weight_ref[...] = jnp.concatenate(weights, axis=0)
    eye = (row == col).astype(F32).astype(BF16)
    place_t_ref[...] = lax.dot_general(
        eye, place.astype(BF16), CONTRACT_LAST, preferred_element_type=F32
    ).astype(BF16)


def route(x, info, cap):
    tokens = info.shape[1]
    slots = NX * cap
    return pl.pallas_call(
        functools.partial(route_kernel, cap),
        in_specs=[pl.BlockSpec(memory_space=pltpu.SMEM), whole(info.shape)],
        out_specs=[whole((slots, tokens)), whole((tokens, slots)), whole((slots, 128))],
        out_shape=[
            jax.ShapeDtypeStruct((slots, tokens), BF16),
            jax.ShapeDtypeStruct((tokens, slots), BF16),
            jax.ShapeDtypeStruct((slots, 128), F32),
        ],
        grid=(1,),
        compiler_params=PARAMS,
    )(x, info)


def saved_kernel(cap, at_ref, gate_ref, up_ref, f1_ref, f2_ref, ha_ref, hb_ref, g3, u3, h3, k3):
    g3[...] = gate_ref[...].astype(F32).reshape(g3.shape)
    u3[...] = up_ref[...].astype(F32).reshape(u3.shape)
    z, c = at_ref[1], at_ref[2]
    for cr in range(NC):
        for zr in range(NZ):
            for xs in range(NX):
                j = (cr * NZ + zr) * NX + xs
                zs = z if zr == 0 else 1 - z
                cs = c if cr == 0 else 1 - c
                q = xs * (NZ * NC) + zs * NC + cs
                gate, upval = g3[q], u3[q]
                sig = jax.nn.sigmoid(gate)
                f1_ref[pl.ds(j * cap, cap), :] = upval * sig * (1.0 + gate * (1.0 - sig))
                f2_ref[pl.ds(j * cap, cap), :] = gate * sig
                h3[j] = gate * sig * upval
    ha_ref[...] = h3[...].reshape(ha_ref.shape).astype(BF16)
    a_to_b(at_ref[0], h3, k3)
    hb_ref[...] = k3[...].reshape(hb_ref.shape).astype(BF16)


def pairs_of_blocks(x):
    for cr in range(NC):
        for zr in range(NZ):
            for d in range(NX):
                yield (cr * NZ + zr) * NX + lax.rem(x + NX - d, NX), (cr * NX + d) * NZ + zr


def a_to_b(x, a3, b3):
    for ja, jb in pairs_of_blocks(x):
        b3[jb] = a3[ja]


def saved(at, gate, up, cap):
    rows, hid = gate.shape
    blocks = rows // cap
    return pl.pallas_call(
        functools.partial(saved_kernel, cap),
        in_specs=[pl.BlockSpec(memory_space=pltpu.SMEM), whole(gate.shape), whole(up.shape)],
        out_specs=[whole((rows, hid))] * 4,
        out_shape=[jax.ShapeDtypeStruct((rows, hid), t) for t in (F32, F32, BF16, BF16)],
        scratch_shapes=[pltpu.VMEM((blocks, cap, hid), F32)] * 4,
        grid=(1,),
        compiler_params=PARAMS,
    )(at, gate, up)


def pack_a_kernel(place_ref, weight_ref, tok_ref, out_ref):
    rows = jnp.dot(place_ref[...], tok_ref[...], preferred_element_type=F32)
    out_ref[...] = (rows * weight_ref[:, 0:1]).astype(BF16)


def pack_a(place, weight, tok):
    tokens, columns = tok.shape
    slots = place.shape[0]
    tile = tile_of(columns)
    return pl.pallas_call(
        pack_a_kernel,
        in_specs=[
            whole(place.shape),
            whole(weight.shape),
            pl.BlockSpec((tokens, tile), lambda j: (0, j)),
        ],
        out_specs=pl.BlockSpec((slots, tile), lambda j: (0, j)),
        out_shape=jax.ShapeDtypeStruct((slots, columns), BF16),
        grid=(columns // tile,),
        compiler_params=PARAMS,
    )(place, weight, tok)


def pack_b_kernel(cap, place0_ref, weight0_ref, place1_ref, weight1_ref, tok0_ref, tok1_ref, *outs):
    rows0 = jnp.dot(place0_ref[...], tok0_ref[...], preferred_element_type=F32)
    rows0 = rows0 * weight0_ref[:, 0:1]
    rows1 = jnp.dot(place1_ref[...], tok1_ref[...], preferred_element_type=F32)
    rows1 = rows1 * weight1_ref[:, 0:1]
    for d in range(NX):
        low, high = d * cap, (d + 1) * cap
        outs[d][...] = jnp.concatenate([rows0[low:high], rows1[low:high]], axis=0).astype(BF16)


def pack_b(place0, weight0, place1, weight1, tok0, tok1, cap):
    tokens, columns = tok0.shape
    tile = tile_of(columns)
    return pl.pallas_call(
        functools.partial(pack_b_kernel, cap),
        in_specs=[
            whole(place0.shape),
            whole(weight0.shape),
            whole(place1.shape),
            whole(weight1.shape),
            pl.BlockSpec((tokens, tile), lambda j: (0, j)),
            pl.BlockSpec((tokens, tile), lambda j: (0, j)),
        ],
        out_specs=[pl.BlockSpec((NZ * cap, tile), lambda j: (0, j))] * NX,
        out_shape=[jax.ShapeDtypeStruct((NZ * cap, columns), BF16)] * NX,
        grid=(columns // tile,),
        compiler_params=PARAMS,
    )(place0, weight0, place1, weight1, tok0, tok1)


def rows_kernel(groups, want_sum, want_grad, with_sum, with_grad, *refs):
    rows, refs = refs[:groups], list(refs[groups:])
    wd_ref = refs.pop(0) if want_sum else None
    hid_ref = refs.pop(0) if want_grad else None
    sum_in = refs.pop(0) if with_sum else None
    if with_grad:
        refs.pop(0)
    sum_ref = refs.pop(0) if want_sum else None
    grad_ref = refs.pop(0) if want_grad else None
    many = rows[0].shape[0]
    if want_sum:
        wd = wd_ref[...]
        for g in range(groups):
            here = pl.ds(g * many, many)
            more = lax.dot_general(rows[g][...], wd, CONTRACT_LAST, preferred_element_type=F32)
            sum_ref[here, :] = more if sum_in is None else sum_in[here, :] + more
    if want_grad:
        grad = None
        for g in range(groups):
            more = jnp.dot(hid_ref[g], rows[g][...], preferred_element_type=F32)
            grad = more if grad is None else grad + more
        grad_ref[...] = grad


def use_rows(rows, w_down, hid_t, dh, grad, start, want_sum, want_grad):
    groups = len(rows)
    many, columns = rows[0].shape
    hid, width = w_down.shape
    at = pl.BlockSpec((pl.Element(hid), pl.Element(columns)), lambda j: (0, start))
    operands, specs = list(rows), [whole((many, columns))] * groups
    out_specs, out_shape, aliases = [], [], {}
    if want_sum:
        operands.append(w_down)
        specs.append(at)
        out_specs.append(whole((groups * many, hid)))
        out_shape.append(jax.ShapeDtypeStruct((groups * many, hid), F32))
    if want_grad:
        operands.append(hid_t)
        specs.append(whole(hid_t.shape))
        out_specs.append(at)
        out_shape.append(jax.ShapeDtypeStruct((hid, width), F32))
    with_sum, with_grad = want_sum and dh is not None, want_grad and grad is not None
    if with_sum:
        operands.append(dh)
        specs.append(whole(dh.shape))
    if with_grad:
        aliases[len(operands)] = len(out_shape) - 1
        operands.append(grad)
        specs.append(pl.BlockSpec(memory_space=pl.ANY))
    done = pl.pallas_call(
        functools.partial(rows_kernel, groups, want_sum, want_grad, with_sum, with_grad),
        in_specs=specs,
        out_specs=out_specs,
        out_shape=out_shape,
        grid=(1,),
        input_output_aliases=aliases,
        compiler_params=PARAMS,
    )(*operands)
    return (done[0] if want_sum else dh), (done[-1] if want_grad else grad)


def act_kernel(at_ref, dha_ref, dhb_ref, f1_ref, f2_ref, ga_ref, ua_ref, gb_ref, ub_ref, one, two):
    x = at_ref[0]
    two[...] = dhb_ref[...].reshape(two.shape)
    for ja, jb in pairs_of_blocks(x):
        one[ja] = two[jb]
    dh = dha_ref[...] + one[...].reshape(dha_ref.shape)
    dgate = dh * f1_ref[...]
    dup = dh * f2_ref[...]
    ga_ref[...] = dgate.astype(BF16)
    ua_ref[...] = dup.astype(BF16)
    for value, out_ref in ((dgate, gb_ref), (dup, ub_ref)):
        one[...] = value.reshape(one.shape)
        a_to_b(x, one, two)
        out_ref[...] = two[...].reshape(out_ref.shape).astype(BF16)


def activations(at, dha, dhb, f1, f2, cap):
    rows, hid = dha.shape
    return pl.pallas_call(
        act_kernel,
        in_specs=[pl.BlockSpec(memory_space=pltpu.SMEM)] + [whole((rows, hid))] * 4,
        out_specs=[whole((rows, hid))] * 4,
        out_shape=[jax.ShapeDtypeStruct((rows, hid), BF16)] * 4,
        scratch_shapes=[pltpu.VMEM((rows // cap, cap, hid), F32)] * 2,
        grid=(1,),
        compiler_params=PARAMS,
    )(at, dha, dhb, f1, f2)


def part_kernel(pieces, with_other, dg_ref, du_ref, wg_ref, wu_ref, *refs):
    total = lax.dot_general(dg_ref[...], wg_ref[...], CONTRACT_LAST, preferred_element_type=F32)
    total += lax.dot_general(du_ref[...], wu_ref[...], CONTRACT_LAST, preferred_element_type=F32)
    if with_other:
        total += refs[0][...].astype(F32)
    outs = refs[with_other:]
    many = total.shape[0] // pieces
    for i in range(pieces):
        outs[i][...] = total[i * many : (i + 1) * many].astype(BF16)


def parts_of(dg, du, wg, wu, start, columns, half, other, pieces):
    rows, hid = dg.shape
    many = rows // NC
    tile = tile_of(columns)
    of_half = pl.BlockSpec((many, hid), lambda j: (half, 0))
    weights = pl.BlockSpec((pl.Element(tile), pl.Element(hid)), lambda j: (start, 0))
    operands = [dg, du, wg, wu]
    specs = [of_half, of_half, weights, weights]
    if other is not None:
        operands.append(other)
        specs.append(pl.BlockSpec((many, tile), lambda j: (0, j)))
    return pl.pallas_call(
        functools.partial(part_kernel, pieces, other is not None),
        in_specs=specs,
        out_specs=[pl.BlockSpec((many // pieces, tile), lambda j: (0, j))] * pieces,
        out_shape=[jax.ShapeDtypeStruct((many // pieces, columns), BF16)] * pieces,
        grid=(columns // tile,),
        compiler_params=PARAMS,
    )(*operands)


def sum_z_kernel(a_ref, b_ref, out_ref):
    out_ref[...] = (a_ref[...].astype(F32) + b_ref[...].astype(F32)).astype(BF16)


def sum_z(a, b):
    return pl.pallas_call(
        sum_z_kernel,
        in_specs=[whole(a.shape)] * 2,
        out_specs=whole(a.shape),
        out_shape=jax.ShapeDtypeStruct(a.shape, BF16),
        grid=(1,),
        compiler_params=PARAMS,
    )(a, b)


def finish_a_kernel(place_t_ref, tok_ref, rows_ref, out_ref):
    branch = jnp.dot(place_t_ref[...], rows_ref[...], preferred_element_type=F32).astype(BF16)
    out_ref[...] = (tok_ref[...].astype(F32) + branch.astype(F32)).astype(BF16)


def finish_a(place_t, tok, rows):
    return pl.pallas_call(
        finish_a_kernel,
        in_specs=[whole(place_t.shape), whole(tok.shape), whole(rows.shape)],
        out_specs=whole(tok.shape),
        out_shape=jax.ShapeDtypeStruct(tok.shape, BF16),
        grid=(1,),
        compiler_params=PARAMS,
    )(place_t, tok, rows)


def combine_b_kernel(cap, place0_ref, place1_ref, *refs):
    blocks, own_ref, other_ref = refs[:NX], refs[NX], refs[NX + 1]
    wide = [b[...].astype(F32) for b in blocks]
    for zr, (place_ref, out_ref) in enumerate(((place0_ref, own_ref), (place1_ref, other_ref))):
        rows = jnp.concatenate([b[zr * cap : (zr + 1) * cap] for b in wide], axis=0).astype(BF16)
        total = jnp.dot(place_ref[...], rows, preferred_element_type=F32)
        out_ref[...] = total.astype(out_ref.dtype)


def combine_b(place0_t, place1_t, blocks):
    tokens = place0_t.shape[0]
    many, columns = blocks[0].shape
    tile = tile_of(columns)
    at = pl.BlockSpec((tokens, tile), lambda j: (0, j))
    return pl.pallas_call(
        functools.partial(combine_b_kernel, many // NZ),
        in_specs=[whole(place0_t.shape), whole(place1_t.shape)]
        + [pl.BlockSpec((many, tile), lambda j: (0, j))] * NX,
        out_specs=[at, at],
        out_shape=[
            jax.ShapeDtypeStruct((tokens, columns), F32),
            jax.ShapeDtypeStruct((tokens, columns), BF16),
        ],
        grid=(columns // tile,),
        compiler_params=PARAMS,
    )(place0_t, place1_t, *blocks)


def finish_b_kernel(own_ref, other_ref, tok_ref, out_ref):
    branch = (own_ref[...] + other_ref[...].astype(F32)).astype(BF16)
    out_ref[...] = (tok_ref[...].astype(F32) + branch.astype(F32)).astype(BF16)


def finish_b(own, other, tok):
    tokens, columns = tok.shape
    tile = tile_of(columns)
    at = pl.BlockSpec((tokens, tile), lambda j: (0, j))
    return pl.pallas_call(
        finish_b_kernel,
        in_specs=[at, at, at],
        out_specs=at,
        out_shape=jax.ShapeDtypeStruct((tokens, columns), BF16),
        grid=(columns // tile,),
        compiler_params=PARAMS,
    )(own, other, tok)


def body(pending, expert_ids, route_weight, gate_saved, up_saved, w_gate, w_up, w_down):
    own = pending[0]
    width = own.shape[1]
    rows, hid = gate_saved.shape[1:]
    cap = rows // (NX * NZ * NC)
    w_gate, w_up, w_down = w_gate[0], w_up[0], w_down[0]
    unit = width // 28
    a0, b0, a1, b1 = EARLY[0] * unit, EARLY[1] * unit, LATE[0] * unit, LATE[1] * unit
    at_a0, at_b0, at_a1, at_b1 = 0, a0, a0 + b0, a0 + b0 + a1
    tie = lax.optimization_barrier

    tok_a0 = section_move(own[:, at_a0 : at_a0 + a0])
    tok_b0 = section_move(own[:, at_b0 : at_b0 + b0])
    tok_a1 = section_move(own[:, at_a1 : at_a1 + a1])
    tok_b1 = section_move(own[:, at_b1 : at_b1 + b1])
    position = lax.axis_index("ep").astype(jnp.int32)
    at = jnp.stack([position >> 2, (position >> 1) & 1, position & 1])
    info = jnp.concatenate([expert_ids[0].astype(F32), route_weight[0]], axis=1).T
    place, place_t, weight = route(jnp.zeros_like(at), info, cap)
    place0, place0_t, weight0 = route(at, info, cap)
    place1, place1_t, weight1 = route(at, ep_move(info, dz=1), cap)
    f1, f2, hid_a, hid_b = saved(at, gate_saved[0], up_saved[0], cap)
    hid_t = {
        "A": hid_a.reshape(NC * NZ, -1, hid).transpose(0, 2, 1),
        "B": hid_b.reshape(NC, -1, hid).transpose(0, 2, 1),
    }

    def x_moves(blocks, sign):
        return [ep_move(blocks[d], dx=sign * d) for d in range(1, NX)]

    near_a0 = x_exchange(pack_a(place, weight, tok_a0))
    near_a0, across_b0 = tie((near_a0, ep_move(tok_b0, dz=1)))
    far_a0 = ep_move(near_a0, dz=1)
    sent_b0 = pack_b(place0, weight0, place1, weight1, tok_b0, across_b0, cap)
    got_b0 = x_moves(sent_b0, 1)
    near_a1 = x_exchange(pack_a(place, weight, tok_a1))
    far_a0, got_b0, near_a1, across_b1 = tie((far_a0, got_b0, near_a1, ep_move(tok_b1, dz=1)))
    far_a1 = ep_move(near_a1, dz=1)
    sent_b1 = pack_b(place0, weight0, place1, weight1, tok_b1, across_b1, cap)
    got_b1 = x_moves(sent_b1, 1)
    near_b0 = jnp.concatenate([sent_b0[0]] + got_b0, axis=0)
    rows_b0 = [near_b0, ep_move(near_b0, dc=1)]
    rows_a0 = [near_a0, far_a0, ep_move(near_a0, dc=1), ep_move(far_a0, dc=1)]
    dh_a, grad = use_rows(rows_a0, w_down, hid_t["A"], None, None, at_a0, True, True)
    dh_b, grad = use_rows(rows_b0, w_down, hid_t["B"], None, grad, at_b0, True, True)
    near_a1_other = ep_move(near_a1, dc=1)
    far_a1, got_b1, near_a1_other, dh_a, dh_b, grad = tie(
        (far_a1, got_b1, near_a1_other, dh_a, dh_b, grad)
    )
    near_b1 = jnp.concatenate([sent_b1[0]] + got_b1, axis=0)
    rows_b1 = [near_b1, ep_move(near_b1, dc=1)]
    rows_a1 = [near_a1, far_a1, near_a1_other, ep_move(far_a1, dc=1)]
    dh_a, _ = use_rows(rows_a1, w_down, None, dh_a, None, at_a1, True, False)
    dh_b, _ = use_rows(rows_b1, w_down, None, dh_b, None, at_b1, True, False)

    dg_a, du_a, dg_b, du_b = activations(at, dh_a, dh_b, f1, f2, cap)

    def parts(kind, low, n, other, pieces):
        dg, du = (dg_a, du_a) if kind == "A" else (dg_b, du_b)
        half = 1 if other is None else 0
        return parts_of(dg, du, w_gate, w_up, low, n, half, other, pieces)

    core_b1 = ep_move(parts("B", at_b1, b1, None, 1)[0], dc=1)
    core_a1 = ep_move(parts("A", at_a1, a1, None, 1)[0], dc=1)
    part_b1 = parts("B", at_b1, b1, core_b1, NX)
    back_b1 = x_moves(part_b1, -1)
    keep_a1, send_a1 = parts("A", at_a1, a1, core_a1, NZ)
    back_a1 = ep_move(send_a1, dz=1)
    core_b0 = ep_move(parts("B", at_b0, b0, None, 1)[0], dc=1)
    core_a0 = ep_move(parts("A", at_a0, a0, None, 1)[0], dc=1)
    part_b0 = parts("B", at_b0, b0, core_b0, NX)
    keep_a0, send_a0 = parts("A", at_a0, a0, core_a0, NZ)
    back_b1, back_a1, part_b0, keep_a0, send_a0 = tie(
        (back_b1, back_a1, part_b0, keep_a0, send_a0)
    )
    mine_b1, send_b1 = combine_b(place0_t, place1_t, [part_b1[0]] + back_b1)
    cross_b1 = ep_move(send_b1, dz=1)
    own_a1 = x_exchange(sum_z(keep_a1, back_a1))
    back_b0 = x_moves(part_b0, -1)
    back_a0 = ep_move(send_a0, dz=1)
    up_b1 = section_move(finish_b(mine_b1, cross_b1, tok_b1))
    up_a1 = section_move(finish_a(place_t, tok_a1, own_a1))
    _, grad = use_rows(rows_a1, w_down, hid_t["A"], None, grad, at_a1, False, True)
    _, grad = use_rows(rows_b1, w_down, hid_t["B"], None, grad, at_b1, False, True)
    back_b0, back_a0, grad = tie((back_b0, back_a0, grad))
    mine_b0, send_b0 = combine_b(place0_t, place1_t, [part_b0[0]] + back_b0)
    cross_b0 = ep_move(send_b0, dz=1)
    own_a0 = x_exchange(sum_z(keep_a0, back_a0))
    up_b0 = section_move(finish_b(mine_b0, cross_b0, tok_b0))
    up_a0 = section_move(finish_a(place_t, tok_a0, own_a0))
    return (jnp.concatenate([up_a0, up_b0, up_a1, up_b1], axis=1)[None], grad[None])


def solution(mesh):
    placed = (
        P("section", "ep", None),
        P("section", "ep", None),
        P("section", "ep", None),
        P("section", None, "ep"),
        P("section", None, "ep"),
        P("section", None, "ep"),
        P("section", None, "ep"),
        P("section", "ep", None),
    )
    return jax.shard_map(
        body,
        mesh=mesh,
        in_specs=placed,
        out_specs=(P("section", "ep", None), P("section", "ep", None)),
        check_vma=False,
    )
```

```python
import functools

import jax
import jax.numpy as jnp
from jax import lax
from jax.experimental import pallas as pl
from jax.experimental.pallas import tpu as pltpu
from jax.sharding import PartitionSpec as P

NX, NZ, NC, NY = 4, 2, 2, 4
F32, BF16 = jnp.float32, jnp.bfloat16
PARAMS = pltpu.CompilerParams(vmem_limit_bytes=32 << 20)
EARLY, LATE = (5, 5), (9, 9)
CONTRACT_LAST = (((1,), (1,)), ((), ()))


def section_move(array, flip):
    sections, peers = lax.axis_size("section"), NX * NZ * NC
    pairs = []
    for s in range(sections):
        for q in range(peers):
            to = q ^ NC if flip(s) else q
            pairs.append((s * peers + q, (s - 1) % sections * peers + to))
    return lax.ppermute(array, ("section", "ep"), pairs)


def ep_move(array, dx=0, dz=0, dc=0):
    pairs = []
    for q in range(NX * NZ * NC):
        x, z, c = q // (NZ * NC), q // NC % NZ, q % NC
        pairs.append((q, (x + dx) % NX * NZ * NC + (z ^ dz) * NC + (c ^ dc)))
    return lax.ppermute(array, "ep", pairs)


def x_moves(blocks, sign):
    return [ep_move(blocks[d], dx=sign * d) for d in range(1, NX)]


def x_exchange(array):
    groups = [[x * NZ * NC + i for x in range(NX)] for i in range(NZ * NC)]
    blocks = array.reshape(NX, -1, array.shape[1])
    moved = lax.all_to_all(blocks, "ep", 0, 0, axis_index_groups=groups, tiled=True)
    return moved.reshape(array.shape)


def whole(shape):
    return pl.BlockSpec(shape, lambda *_: (0,) * len(shape))


def in_hbm(array):
    return pltpu.with_memory_space_constraint(array, pltpu.HBM)


def tile_of(columns):
    return max(t for t in range(128, 897, 128) if columns % t == 0)


def over_columns(compute, columns, tiled, fixed, scalars, tiled_out, fixed_out, into=None):
    tile = tile_of(columns)
    steps = columns // tile
    n_in, n_fix, n_out = len(tiled), len(fixed), len(tiled_out)

    def kernel(*refs):
        refs = list(refs)
        take = lambda n: [refs.pop(0) for _ in range(n)]
        ins, fixes = take(n_in), take(n_fix)
        scalar = take(1)[0] if scalars is not None else None
        if into is not None:
            take(1)
        outs, fix_outs = take(n_out), take(len(fixed_out))
        in_bufs, out_bufs = take(n_in), take(n_out)
        in_sems, out_sems = take(2)

        def window(ref, axis, start, t):
            here = pl.ds(start + t * tile, tile)
            return ref.at[:, here] if axis == 1 else ref.at[here, :]

        loads = [
            [
                pltpu.make_async_copy(
                    window(ins[i], axis, start, t),
                    window(in_bufs[i], axis, 0, t),
                    in_sems.at[i * steps + t],
                )
                for i, (_, axis, start) in enumerate(tiled)
            ]
            for t in range(steps)
        ]
        for t in range(steps):
            for copy in loads[t]:
                copy.start()
        stores = []
        for t in range(steps):
            for copy in loads[t]:
                copy.wait()
            values = [
                window(in_bufs[i], axis, 0, t)[...] for i, (_, axis, _) in enumerate(tiled)
            ]
            for i, value in enumerate(compute(t, values, fixes, scalar, fix_outs)):
                buf = window(out_bufs[i], 1, 0, t)
                buf[...] = value.astype(out_bufs[i].dtype)
                copy = pltpu.make_async_copy(
                    buf, window(outs[i], 1, tiled_out[i][2], t), out_sems.at[i * steps + t]
                )
                copy.start()
                stores.append(copy)
        for copy in stores:
            copy.wait()

    hbm = pl.BlockSpec(memory_space=pl.ANY)
    operands = [a for a, _, _ in tiled] + list(fixed)
    specs = [hbm] * n_in + [pl.BlockSpec(memory_space=pltpu.VMEM)] * n_fix
    if scalars is not None:
        operands.append(scalars)
        specs.append(pl.BlockSpec(memory_space=pltpu.SMEM))
    aliases = {}
    if into is not None:
        aliases[len(operands)] = 0
        operands.append(in_hbm(into))
        specs.append(hbm)
    buffers = [
        pltpu.VMEM((a.shape[0], columns) if axis == 1 else (columns, a.shape[1]), a.dtype)
        for a, axis, _ in tiled
    ] + [pltpu.VMEM((shape[0], columns), dtype) for shape, dtype, _ in tiled_out]
    return pl.pallas_call(
        kernel,
        in_specs=specs,
        out_specs=[hbm] * n_out + [pl.BlockSpec(memory_space=pltpu.VMEM)] * len(fixed_out),
        out_shape=[pltpu.HBM(shape, dtype) for shape, dtype, _ in tiled_out]
        + [jax.ShapeDtypeStruct(shape, dtype) for shape, dtype in fixed_out],
        scratch_shapes=buffers
        + [
            pltpu.SemaphoreType.DMA((max(1, n_in * steps),)),
            pltpu.SemaphoreType.DMA((max(1, n_out * steps),)),
        ],
        input_output_aliases=aliases,
        compiler_params=PARAMS,
    )(*operands)


def tables_of(cap, info_ref, first_x):
    tokens = info_ref.shape[1]
    row = lax.broadcasted_iota(jnp.int32, (tokens, tokens), 0)
    col = lax.broadcasted_iota(jnp.int32, (tokens, tokens), 1)
    before = (row < col).astype(F32).astype(BF16)
    slot_of = lax.broadcasted_iota(jnp.int32, (cap, tokens), 0).astype(F32)
    places, weights = [], []
    for d in range(NX):
        expert = lax.rem(first_x + d, NX).astype(F32)
        first = info_ref[0:1, :] == expert
        second = info_ref[1:2, :] == expert
        named = jnp.where(first | second, 1.0, 0.0)
        prob = jnp.where(first, info_ref[2:3, :], jnp.where(second, info_ref[3:4, :], 0.0))
        rank = jnp.dot(
            jnp.broadcast_to(named, (8, tokens)).astype(BF16), before, preferred_element_type=F32
        )[0:1]
        placed = jnp.where((slot_of == rank) & (named > 0.0), 1.0, 0.0)
        places.append(placed)
        weights.append(
            jnp.broadcast_to(jnp.sum(placed * prob, axis=1, keepdims=True), (cap, 128))
        )
    return places, weights


def transposed(block):
    tokens = block.shape[1]
    row = lax.broadcasted_iota(jnp.int32, (tokens, tokens), 0)
    col = lax.broadcasted_iota(jnp.int32, (tokens, tokens), 1)
    eye = (row == col).astype(F32).astype(BF16)
    return lax.dot_general(eye, block.astype(BF16), CONTRACT_LAST, preferred_element_type=F32)


def route_kernel(
    cap, at_ref, info0_ref, info1_ref, pa_ref, pat_ref, wa_ref, p0_ref, w0_ref, p1_ref, w1_ref,
    keep_ref, send_ref,
):
    x, last = at_ref[0], at_ref[4].astype(F32)
    places, weights = tables_of(cap, info0_ref, jnp.int32(0))
    pa_ref[...] = jnp.concatenate(places, axis=0).astype(BF16)
    pat_ref[...] = transposed(jnp.concatenate(places, axis=0)).astype(BF16)
    wa_ref[...] = jnp.concatenate(weights, axis=0)
    places0, weights0 = tables_of(cap, info0_ref, x)
    places1, weights1 = tables_of(cap, info1_ref, x)
    p0_ref[...] = jnp.concatenate(places0, axis=0).astype(BF16)
    w0_ref[...] = jnp.concatenate(weights0, axis=0)
    p1_ref[...] = jnp.concatenate(places1, axis=0).astype(BF16)
    w1_ref[...] = jnp.concatenate(weights1, axis=0)
    for d in range(NX):
        keep = jnp.concatenate([places0[d] * (1.0 - last), places1[d] * last], axis=0)
        send = jnp.concatenate([places0[d] * last, places1[d] * (1.0 - last)], axis=0)
        keep_ref[d] = transposed(keep).astype(BF16)
        send_ref[d] = transposed(send).astype(BF16)


def route(at, info0, info1, cap):
    tokens = info0.shape[1]
    slots = NX * cap
    place, weight = (slots, tokens), (slots, 128)
    back = (NX, tokens, NZ * cap)
    shapes = [(place, BF16), ((tokens, slots), BF16), (weight, F32), (place, BF16), (weight, F32)]
    shapes += [(place, BF16), (weight, F32), (back, BF16), (back, BF16)]
    return pl.pallas_call(
        functools.partial(route_kernel, cap),
        in_specs=[pl.BlockSpec(memory_space=pltpu.SMEM), whole(info0.shape), whole(info1.shape)],
        out_specs=[whole(s) for s, _ in shapes],
        out_shape=[pltpu.HBM(s, t) for s, t in shapes],
        grid=(1,),
        compiler_params=PARAMS,
    )(at, info0, info1)


def saved_kernel(cap, at_ref, gate_ref, up_ref, f1_ref, f2_ref, ha_ref, hb_ref, g3, u3, h3, k3):
    g3[...] = gate_ref[...].astype(F32).reshape(g3.shape)
    u3[...] = up_ref[...].astype(F32).reshape(u3.shape)
    z, c = at_ref[1], at_ref[2]
    for cr in range(NC):
        for zr in range(NZ):
            for xs in range(NX):
                j = (cr * NZ + zr) * NX + xs
                zs = z if zr == 0 else 1 - z
                cs = c if cr == 0 else 1 - c
                q = xs * (NZ * NC) + zs * NC + cs
                gate, upval = g3[q], u3[q]
                sig = jax.nn.sigmoid(gate)
                f1_ref[pl.ds(j * cap, cap), :] = upval * sig * (1.0 + gate * (1.0 - sig))
                f2_ref[pl.ds(j * cap, cap), :] = gate * sig
                h3[j] = gate * sig * upval
    ha_ref[...] = h3[...].reshape(ha_ref.shape).astype(BF16)
    a_to_b(at_ref[0], h3, k3)
    hb_ref[...] = k3[...].reshape(hb_ref.shape).astype(BF16)


def pairs_of_blocks(x):
    for cr in range(NC):
        for zr in range(NZ):
            for d in range(NX):
                yield (cr * NZ + zr) * NX + lax.rem(x + NX - d, NX), (cr * NX + d) * NZ + zr


def a_to_b(x, a3, b3):
    for ja, jb in pairs_of_blocks(x):
        b3[jb] = a3[ja]


def saved(at, gate, up, cap):
    rows, hid = gate.shape
    blocks = rows // cap
    return pl.pallas_call(
        functools.partial(saved_kernel, cap),
        in_specs=[pl.BlockSpec(memory_space=pltpu.SMEM), whole(gate.shape), whole(up.shape)],
        out_specs=[whole((rows, hid))] * 4,
        out_shape=[jax.ShapeDtypeStruct((rows, hid), t) for t in (F32, F32, BF16, BF16)],
        scratch_shapes=[pltpu.VMEM((blocks, cap, hid), F32)] * 4,
        grid=(1,),
        compiler_params=PARAMS,
    )(at, gate, up)


def pack_a(place, weight, tok, start, columns):
    def compute(t, values, fixed, scalar, outs):
        rows = jnp.dot(fixed[0][...], values[0], preferred_element_type=F32)
        return [rows * fixed[1][:, 0:1]]

    out = ((place.shape[0], columns), BF16, 0)
    return over_columns(compute, columns, [(tok, 1, start)], [place, weight], None, [out], [])[0]


def pack_b(place0, weight0, place1, weight1, tok0, start, tok1, cap):
    columns = tok1.shape[1]

    def compute(t, values, fixed, scalar, outs):
        rows0 = jnp.dot(fixed[0][...], values[0], preferred_element_type=F32) * fixed[1][:, 0:1]
        rows1 = jnp.dot(fixed[2][...], values[1], preferred_element_type=F32) * fixed[3][:, 0:1]
        cut = [slice(d * cap, (d + 1) * cap) for d in range(NX)]
        return [jnp.concatenate([rows0[i], rows1[i]], axis=0) for i in cut]

    out = ((NZ * cap, columns), BF16, 0)
    return over_columns(
        compute, columns, [(tok0, 1, start), (tok1, 1, 0)], [place0, weight0, place1, weight1],
        None, [out] * NX, [],
    )


def use_rows(groups, w_down, hid_t, dh, grad, start, want_sum, want_grad):
    hid, width = w_down.shape
    columns = groups[0][0].shape[1]
    lengths = [sum(a.shape[0] for a in g) for g in groups]
    rows = sum(lengths)
    tiled = [(a, 1, 0) for g in groups for a in g]
    fixed = []
    if want_sum:
        tiled.append((in_hbm(w_down), 1, start))
        if dh is not None:
            fixed.append(dh)
    if want_grad:
        fixed.append(hid_t)

    def compute(t, values, fixed_refs, scalar, outs):
        values, refs = list(values), list(fixed_refs)
        blocks = []
        for g in groups:
            parts = [values.pop(0) for _ in g]
            blocks.append(parts[0] if len(parts) == 1 else jnp.concatenate(parts, axis=0))
        if want_sum:
            before = refs.pop(0) if dh is not None else None
            low = 0
            for block, many in zip(blocks, lengths):
                here = pl.ds(low, many)
                more = lax.dot_general(block, values[0], CONTRACT_LAST, preferred_element_type=F32)
                if t > 0:
                    more += outs[0][here, :]
                elif before is not None:
                    more += before[here, :]
                outs[0][here, :] = more
                low += many
        if not want_grad:
            return []
        total = None
        for i, block in enumerate(blocks):
            more = jnp.dot(refs[0][i], block, preferred_element_type=F32)
            total = more if total is None else total + more
        return [total]

    done = over_columns(
        compute, columns, tiled, fixed, None,
        [((hid, width), F32, start)] if want_grad else [],
        [((rows, hid), F32)] if want_sum else [],
        grad if want_grad else None,
    )
    return (done[-1] if want_sum else dh), (done[0] if want_grad else grad)


def act_kernel(at_ref, dha_ref, dhb_ref, f1_ref, f2_ref, ga_ref, ua_ref, gb_ref, ub_ref, one, two):
    x = at_ref[0]
    two[...] = dhb_ref[...].reshape(two.shape)
    for ja, jb in pairs_of_blocks(x):
        one[ja] = two[jb]
    dh = dha_ref[...] + one[...].reshape(dha_ref.shape)
    dgate = dh * f1_ref[...]
    dup = dh * f2_ref[...]
    ga_ref[...] = dgate.astype(BF16)
    ua_ref[...] = dup.astype(BF16)
    for value, out_ref in ((dgate, gb_ref), (dup, ub_ref)):
        one[...] = value.reshape(one.shape)
        a_to_b(x, one, two)
        out_ref[...] = two[...].reshape(out_ref.shape).astype(BF16)


def activations(at, dha, dhb, f1, f2, cap):
    rows, hid = dha.shape
    return pl.pallas_call(
        act_kernel,
        in_specs=[pl.BlockSpec(memory_space=pltpu.SMEM)] + [whole((rows, hid))] * 4,
        out_specs=[whole((rows, hid))] * 4,
        out_shape=[jax.ShapeDtypeStruct((rows, hid), BF16)] * 4,
        scratch_shapes=[pltpu.VMEM((rows // cap, cap, hid), F32)] * 2,
        grid=(1,),
        compiler_params=PARAMS,
    )(at, dha, dhb, f1, f2)


def parts_of(dg, du, wg, wu, start, columns, half, other, pieces):
    many = dg.shape[0] // NC
    each = many // pieces
    tiled = [(in_hbm(wg), 0, start), (in_hbm(wu), 0, start)]
    if other is not None:
        tiled.append((other, 1, 0))

    def compute(t, values, fixed, scalar, outs):
        here = pl.ds(half * many, many)
        total = lax.dot_general(
            fixed[0][here, :], values[0], CONTRACT_LAST, preferred_element_type=F32
        )
        total += lax.dot_general(
            fixed[1][here, :], values[1], CONTRACT_LAST, preferred_element_type=F32
        )
        if other is not None:
            total += values[2].astype(F32)
        return [total[i * each : (i + 1) * each] for i in range(pieces)]

    out = ((each, columns), BF16, 0)
    return over_columns(compute, columns, tiled, [dg, du], None, [out] * pieces, [])


def sum_z(a, b):
    def compute(t, values, fixed, scalar, outs):
        return [values[0].astype(F32) + values[1].astype(F32)]

    return over_columns(
        compute, a.shape[1], [(a, 1, 0), (b, 1, 0)], [], None, [(a.shape, BF16, 0)], []
    )[0]


def finish_a(place_t, tok, start, rows):
    def compute(t, values, fixed, scalar, outs):
        branch = jnp.dot(fixed[0][...], values[1], preferred_element_type=F32).astype(BF16)
        return [values[0].astype(F32) + branch.astype(F32)]

    out = ((tok.shape[0], rows.shape[1]), BF16, 0)
    return over_columns(
        compute, rows.shape[1], [(tok, 1, start), (rows, 1, 0)], [place_t], None, [out], []
    )[0]


def combine_b(keep, send, blocks):
    columns = blocks[0].shape[1]
    tokens = keep.shape[1]

    def compute(t, values, fixed, scalar, outs):
        totals = []
        for ref in fixed:
            total = None
            for d in range(NX):
                more = jnp.dot(ref[d], values[d], preferred_element_type=F32)
                total = more if total is None else total + more
            totals.append(total)
        return totals

    outs = [((tokens, columns), F32, 0), ((tokens, columns), BF16, 0)]
    return over_columns(compute, columns, [(b, 1, 0) for b in blocks], [keep, send], None, outs, [])


def finish_b(at, own, other, tok0, start, tok1):
    columns = own.shape[1]

    def compute(t, values, fixed, scalar, outs):
        branch = (values[0] + values[1].astype(F32)).astype(BF16)
        tok = jnp.where(scalar[4] == 0, values[2].astype(F32), values[3].astype(F32))
        return [tok + branch.astype(F32)]

    tiled = [(own, 1, 0), (other, 1, 0), (tok0, 1, start), (tok1, 1, 0)]
    return over_columns(compute, columns, tiled, [], at, [(own.shape, BF16, 0)], [])[0]


def place_chunk(piece, width, start, into):
    def kernel(*refs):
        src, dst, sem = refs[0], refs[-2], refs[-1]
        copy = pltpu.make_async_copy(src, dst.at[:, pl.ds(start, piece.shape[1])], sem)
        copy.start()
        copy.wait()

    hbm = pl.BlockSpec(memory_space=pl.ANY)
    operands = [piece] if into is None else [piece, in_hbm(into)]
    return pl.pallas_call(
        kernel,
        in_specs=[hbm] * len(operands),
        out_specs=hbm,
        out_shape=pltpu.HBM((piece.shape[0], width), piece.dtype),
        scratch_shapes=[pltpu.SemaphoreType.DMA],
        input_output_aliases={} if into is None else {1: 0},
        compiler_params=PARAMS,
    )(*operands)


def body(pending, expert_ids, route_weight, gate_saved, up_saved, w_gate, w_up, w_down):
    own = pending[0]
    width = own.shape[1]
    rows, hid = gate_saved.shape[1:]
    cap = rows // (NX * NZ * NC)
    w_gate, w_up, w_down = w_gate[0], w_up[0], w_down[0]
    unit = width // 28
    a0, b0, a1, b1 = EARLY[0] * unit, EARLY[1] * unit, LATE[0] * unit, LATE[1] * unit
    early = a0 + b0
    at_a0, at_b0, at_a1, at_b1 = 0, a0, early, early + a1
    tie = lax.optimization_barrier

    def crossing(s):
        return s % NY == 0

    def swapped(s):
        return s % NY == NY - 1

    tok0 = section_move(own[:, :early], crossing)
    info = jnp.concatenate([expert_ids[0].astype(F32), route_weight[0]], axis=1).T
    info_far = ep_move(info, dz=1)
    tok1 = section_move(own[:, early:], crossing)
    section = lax.axis_index("section").astype(jnp.int32)
    position = lax.axis_index("ep").astype(jnp.int32)
    turned = (section % NY == NY - 1).astype(jnp.int32)
    last = jnp.maximum(turned, (section % NY == 0).astype(jnp.int32))
    z = (position >> 1) & 1
    at = jnp.stack([position >> 2, jnp.where(turned == 1, 1 - z, z), position & 1, turned, last])
    info0 = jnp.where(turned == 1, info_far, info)
    info1 = jnp.where(turned == 1, info, info_far)
    place, place_t, weight, place0, weight0, place1, weight1, keep_t, send_t = route(
        at, info0, info1, cap
    )
    f1, f2, hid_a, hid_b = saved(at, gate_saved[0], up_saved[0], cap)
    hid_at = hid_a.reshape(NC * NZ, -1, hid).transpose(0, 2, 1)
    hid_bt = hid_b.reshape(NC, -1, hid).transpose(0, 2, 1)

    near_a0 = x_exchange(pack_a(place, weight, tok0, 0, a0))
    near_a0, far_tok0 = tie((near_a0, ep_move(tok0[:, a0:], dz=1)))
    far_a0 = ep_move(near_a0, dz=1)
    sent_b0 = pack_b(place0, weight0, place1, weight1, tok0, a0, far_tok0, cap)
    got_b0 = x_moves(sent_b0, 1)
    near_a1 = x_exchange(pack_a(place, weight, tok1, 0, a1))
    far_a0, got_b0, near_a1, far_tok1 = tie(
        (far_a0, got_b0, near_a1, ep_move(tok1[:, a1:], dz=1))
    )
    far_a1 = ep_move(near_a1, dz=1)
    sent_b1 = pack_b(place0, weight0, place1, weight1, tok1, a1, far_tok1, cap)
    near_b0 = jnp.concatenate([sent_b0[0]] + got_b0, axis=0)
    sent_b1, near_b0, near_a0, far_a0 = tie((sent_b1, near_b0, near_a0, far_a0))
    got_b1 = x_moves(sent_b1, 1)
    rows_b0 = [[near_b0], [ep_move(near_b0, dc=1)]]
    rows_a0 = [[near_a0], [far_a0], [ep_move(near_a0, dc=1)], [ep_move(far_a0, dc=1)]]
    dh_a, grad = use_rows(rows_a0, w_down, hid_at, None, None, at_a0, True, True)
    dh_b, grad = use_rows(rows_b0, w_down, hid_bt, None, grad, at_b0, True, True)
    near_a1_other = ep_move(near_a1, dc=1)
    first_b1_other = ep_move(sent_b1[0], dc=1)
    far_a1, got_b1, near_a1_other, first_b1_other, dh_a, dh_b, grad = tie(
        (far_a1, got_b1, near_a1_other, first_b1_other, dh_a, dh_b, grad)
    )
    rows_a1 = [[near_a1], [far_a1], [near_a1_other], [ep_move(far_a1, dc=1)]]
    rows_b1 = [
        [sent_b1[0]] + got_b1,
        [first_b1_other] + [ep_move(piece, dc=1) for piece in got_b1],
    ]
    dh_a, _ = use_rows(rows_a1, w_down, None, dh_a, None, at_a1, True, False)
    dh_b, _ = use_rows(rows_b1, w_down, None, dh_b, None, at_b1, True, False)

    dg_a, du_a, dg_b, du_b = activations(at, dh_a, dh_b, f1, f2, cap)

    def parts(kind, low, n, other, pieces):
        dg, du = (dg_a, du_a) if kind == "A" else (dg_b, du_b)
        half = 1 if other is None else 0
        return parts_of(dg, du, w_gate, w_up, low, n, half, other, pieces)

    core_b1 = ep_move(parts("B", at_b1, b1, None, 1)[0], dc=1)
    core_a1 = ep_move(parts("A", at_a1, a1, None, 1)[0], dc=1)
    part_b1 = parts("B", at_b1, b1, core_b1, NX)
    back_b1 = x_moves(part_b1, -1)
    keep_a1, send_a1 = parts("A", at_a1, a1, core_a1, NZ)
    back_a1 = ep_move(send_a1, dz=1)
    core_b0 = ep_move(parts("B", at_b0, b0, None, 1)[0], dc=1)
    core_a0 = ep_move(parts("A", at_a0, a0, None, 1)[0], dc=1)
    part_b0 = parts("B", at_b0, b0, core_b0, NX)
    keep_a0, send_a0 = parts("A", at_a0, a0, core_a0, NZ)
    _, grad = use_rows(rows_a1, w_down, hid_at, None, grad, at_a1, False, True)
    _, grad = use_rows(rows_b1, w_down, hid_bt, None, grad, at_b1, False, True)
    back_b1, back_a1, part_b0, keep_a0, send_a0, grad = tie(
        (back_b1, back_a1, part_b0, keep_a0, send_a0, grad)
    )
    mine_b1, send_b1 = combine_b(keep_t, send_t, [part_b1[0]] + back_b1)
    sum_a1 = sum_z(keep_a1, back_a1)
    send_b1, sum_a1, part_b0, send_a0 = tie((send_b1, sum_a1, part_b0, send_a0))
    cross_b1 = ep_move(send_b1, dz=1)
    own_a1 = x_exchange(sum_a1)
    back_b0 = x_moves(part_b0, -1)
    back_a0 = ep_move(send_a0, dz=1)
    up_b1 = section_move(finish_b(at, mine_b1, cross_b1, tok1, a1, far_tok1), crossing)
    up_a1 = section_move(finish_a(place_t, tok1, 0, own_a1), swapped)
    back_b0, back_a0 = tie((back_b0, back_a0))
    mine_b0, send_b0 = combine_b(keep_t, send_t, [part_b0[0]] + back_b0)
    cross_b0 = ep_move(send_b0, dz=1)
    own_a0 = x_exchange(sum_z(keep_a0, back_a0))
    up_b0 = section_move(finish_b(at, mine_b0, cross_b0, tok0, a0, far_tok0), crossing)
    up_a0 = section_move(finish_a(place_t, tok0, 0, own_a0), swapped)
    out = place_chunk(up_b1, width, at_b1, None)
    out = place_chunk(up_a1, width, at_a1, out)
    out = place_chunk(up_b0, width, at_b0, out)
    out = place_chunk(up_a0, width, at_a0, out)
    return (out[None], grad[None])


def solution(mesh):
    placed = (
        P("section", "ep", None),
        P("section", "ep", None),
        P("section", "ep", None),
        P("section", None, "ep"),
        P("section", None, "ep"),
        P("section", None, "ep"),
        P("section", None, "ep"),
        P("section", "ep", None),
    )
    return jax.shard_map(
        body,
        mesh=mesh,
        in_specs=placed,
        out_specs=(P("section", "ep", None), P("section", "ep", None)),
        check_vma=False,
    )
```

```python
import functools

import jax
import jax.numpy as jnp
from jax import lax
from jax.experimental import pallas as pl
from jax.experimental.pallas import tpu as pltpu
from jax.sharding import PartitionSpec as P

NX, NZ, NC, NY = 4, 2, 2, 4
F32, BF16 = jnp.float32, jnp.bfloat16
PARAMS = pltpu.CompilerParams(vmem_limit_bytes=32 << 20)
LIGHT = pl.CostEstimate(flops=1, bytes_accessed=1, transcendentals=0)
EARLY, LATE = (5, 5), (9, 9)
CONTRACT_LAST = (((1,), (1,)), ((), ()))


def section_move(array, flip):
    sections, peers = lax.axis_size("section"), NX * NZ * NC
    pairs = []
    for s in range(sections):
        for q in range(peers):
            to = q ^ NC if flip(s) else q
            pairs.append((s * peers + q, (s - 1) % sections * peers + to))
    return lax.ppermute(array, ("section", "ep"), pairs)


def ep_move(array, dx=0, dz=0, dc=0):
    pairs = []
    for q in range(NX * NZ * NC):
        x, z, c = q // (NZ * NC), q // NC % NZ, q % NC
        pairs.append((q, (x + dx) % NX * NZ * NC + (z ^ dz) * NC + (c ^ dc)))
    return lax.ppermute(array, "ep", pairs)


def x_moves(blocks, sign):
    return [ep_move(blocks[d], dx=sign * d) for d in range(1, NX)]


def x_exchange(array):
    groups = [[x * NZ * NC + i for x in range(NX)] for i in range(NZ * NC)]
    blocks = array.reshape(NX, -1, array.shape[1])
    moved = lax.all_to_all(blocks, "ep", 0, 0, axis_index_groups=groups, tiled=True)
    return moved.reshape(array.shape)


def whole(shape):
    return pl.BlockSpec(shape, lambda *_: (0,) * len(shape))


def in_hbm(array):
    return pltpu.with_memory_space_constraint(array, pltpu.HBM)


def tile_of(columns):
    return max(t for t in range(128, 897, 128) if columns % t == 0)


def release(value, *after):
    return lax.optimization_barrier((value, after))[0]


def at_once(compute, columns, tiled, fixed, scalars, tiled_out, fixed_out):
    n_in, n_fix, n_out = len(tiled), len(fixed), len(tiled_out)

    def kernel(*refs):
        ins, fixes, outs = refs[:n_in], refs[n_in : n_in + n_fix], refs[n_in + n_fix :]
        results = compute(0, [r[...] for r in ins], fixes, None, outs[n_out:])
        for ref, value in zip(outs, results):
            ref[...] = value.astype(ref.dtype)

    operands, specs = [], []
    for array, axis, start in tiled:
        operands.append(array)
        if array.shape[axis] == columns:
            specs.append(whole(array.shape))
            continue
        shape = list(array.shape)
        shape[axis] = columns
        at = (0, start) if axis == 1 else (start, 0)
        specs.append(pl.BlockSpec(tuple(pl.Element(n) for n in shape), lambda *_, at=at: at))
    for array in fixed:
        operands.append(array)
        specs.append(whole(array.shape))
    shapes = [(shape, dtype) for shape, dtype, *_ in tiled_out] + list(fixed_out)
    return pl.pallas_call(
        kernel,
        in_specs=specs,
        out_specs=[whole(shape) for shape, _ in shapes],
        out_shape=[jax.ShapeDtypeStruct(shape, dtype) for shape, dtype in shapes],
        grid=(1,),
        compiler_params=PARAMS,
        cost_estimate=LIGHT,
    )(*operands)


def over_columns(compute, columns, tiled, fixed, scalars, tiled_out, fixed_out, into=None):
    row_windows = [entry[3] if len(entry) > 3 else None for entry in tiled]
    tiled = [entry[:3] for entry in tiled]
    tile = tile_of(columns)
    steps = columns // tile
    n_in, n_fix, n_out = len(tiled), len(fixed), len(tiled_out)

    def kernel(*refs):
        refs = list(refs)
        take = lambda n: [refs.pop(0) for _ in range(n)]
        ins, fixes = take(n_in), take(n_fix)
        scalar = take(1)[0] if scalars is not None else None
        if into is not None:
            take(1)
        outs, fix_outs = take(n_out), take(len(fixed_out))
        in_bufs, out_bufs = take(n_in), take(n_out)
        in_sems, out_sems = take(2)

        def window(ref, axis, start, t, rows=None):
            here = pl.ds(start + t * tile, tile)
            if rows is not None:
                return ref.at[pl.ds(*rows), here]
            return ref.at[:, here] if axis == 1 else ref.at[here, :]

        loads = [
            [
                pltpu.make_async_copy(
                    window(ins[i], axis, start, t, row_windows[i]),
                    window(in_bufs[i], axis, 0, t),
                    in_sems.at[i * steps + t],
                )
                for i, (_, axis, start) in enumerate(tiled)
            ]
            for t in range(steps)
        ]
        for t in range(steps):
            for copy in loads[t]:
                copy.start()
        stores = []
        for t in range(steps):
            for copy in loads[t]:
                copy.wait()
            values = [
                window(in_bufs[i], axis, 0, t)[...] for i, (_, axis, _) in enumerate(tiled)
            ]
            for i, value in enumerate(compute(t, values, fixes, scalar, fix_outs)):
                buf = window(out_bufs[i], 1, 0, t)
                buf[...] = value.astype(out_bufs[i].dtype)
                copy = pltpu.make_async_copy(
                    buf, window(outs[i], 1, tiled_out[i][2], t), out_sems.at[i * steps + t]
                )
                copy.start()
                stores.append(copy)
        for copy in stores:
            copy.wait()

    hbm = pl.BlockSpec(memory_space=pl.ANY)
    operands = [in_hbm(a) for a, _, _ in tiled] + list(fixed)
    specs = [hbm] * n_in + [pl.BlockSpec(memory_space=pltpu.VMEM)] * n_fix
    if scalars is not None:
        operands.append(scalars)
        specs.append(pl.BlockSpec(memory_space=pltpu.SMEM))
    aliases = {}
    if into is not None:
        aliases[len(operands)] = 0
        operands.append(in_hbm(into))
        specs.append(hbm)
    buffers = [
        pltpu.VMEM(
            (r[1] if r else a.shape[0], columns) if axis == 1 else (columns, a.shape[1]), a.dtype
        )
        for (a, axis, _), r in zip(tiled, row_windows)
    ] + [pltpu.VMEM((shape[0], columns), dtype) for shape, dtype, _ in tiled_out]
    return pl.pallas_call(
        kernel,
        in_specs=specs,
        out_specs=[hbm] * n_out + [pl.BlockSpec(memory_space=pltpu.VMEM)] * len(fixed_out),
        out_shape=[pltpu.HBM(shape, dtype) for shape, dtype, _ in tiled_out]
        + [jax.ShapeDtypeStruct(shape, dtype) for shape, dtype in fixed_out],
        scratch_shapes=buffers
        + [
            pltpu.SemaphoreType.DMA((max(1, n_in * steps),)),
            pltpu.SemaphoreType.DMA((max(1, n_out * steps),)),
        ],
        input_output_aliases=aliases,
        compiler_params=PARAMS,
        cost_estimate=LIGHT,
    )(*operands)


def tables_of(cap, info_ref, first_x):
    tokens = info_ref.shape[1]
    row = lax.broadcasted_iota(jnp.int32, (tokens, tokens), 0)
    col = lax.broadcasted_iota(jnp.int32, (tokens, tokens), 1)
    before = (row < col).astype(F32).astype(BF16)
    slot_of = lax.broadcasted_iota(jnp.int32, (cap, tokens), 0).astype(F32)
    places, weights = [], []
    for d in range(NX):
        expert = lax.rem(first_x + d, NX).astype(F32)
        first = info_ref[0:1, :] == expert
        second = info_ref[1:2, :] == expert
        named = jnp.where(first | second, 1.0, 0.0)
        prob = jnp.where(first, info_ref[2:3, :], jnp.where(second, info_ref[3:4, :], 0.0))
        rank = jnp.dot(
            jnp.broadcast_to(named, (8, tokens)).astype(BF16), before, preferred_element_type=F32
        )[0:1]
        placed = jnp.where((slot_of == rank) & (named > 0.0), 1.0, 0.0)
        places.append(placed)
        weights.append(
            jnp.broadcast_to(jnp.sum(placed * prob, axis=1, keepdims=True), (cap, 128))
        )
    return places, weights


def transposed(block):
    tokens = block.shape[1]
    row = lax.broadcasted_iota(jnp.int32, (tokens, tokens), 0)
    col = lax.broadcasted_iota(jnp.int32, (tokens, tokens), 1)
    eye = (row == col).astype(F32).astype(BF16)
    return lax.dot_general(eye, block.astype(BF16), CONTRACT_LAST, preferred_element_type=F32)


def route_kernel(
    cap, at_ref, info0_ref, info1_ref, pa_ref, pat_ref, wa_ref, p0_ref, w0_ref, p1_ref, w1_ref,
    keep_ref, send_ref,
):
    x, last = at_ref[0], at_ref[4].astype(F32)
    places, weights = tables_of(cap, info0_ref, jnp.int32(0))
    pa_ref[...] = jnp.concatenate(places, axis=0).astype(BF16)
    pat_ref[...] = transposed(jnp.concatenate(places, axis=0)).astype(BF16)
    wa_ref[...] = jnp.concatenate(weights, axis=0)
    places0, weights0 = tables_of(cap, info0_ref, x)
    places1, weights1 = tables_of(cap, info1_ref, x)
    p0_ref[...] = jnp.concatenate(places0, axis=0).astype(BF16)
    w0_ref[...] = jnp.concatenate(weights0, axis=0)
    p1_ref[...] = jnp.concatenate(places1, axis=0).astype(BF16)
    w1_ref[...] = jnp.concatenate(weights1, axis=0)
    for d in range(NX):
        keep = jnp.concatenate([places0[d] * (1.0 - last), places1[d] * last], axis=0)
        send = jnp.concatenate([places0[d] * last, places1[d] * (1.0 - last)], axis=0)
        keep_ref[d] = transposed(keep).astype(BF16)
        send_ref[d] = transposed(send).astype(BF16)


def route(at, info0, info1, cap):
    tokens = info0.shape[1]
    slots = NX * cap
    place, weight = (slots, tokens), (slots, 128)
    back = (NX, tokens, NZ * cap)
    shapes = [(place, BF16), ((tokens, slots), BF16), (weight, F32), (place, BF16), (weight, F32)]
    shapes += [(place, BF16), (weight, F32), (back, BF16), (back, BF16)]
    return pl.pallas_call(
        functools.partial(route_kernel, cap),
        in_specs=[pl.BlockSpec(memory_space=pltpu.SMEM), whole(info0.shape), whole(info1.shape)],
        out_specs=[whole(s) for s, _ in shapes],
        out_shape=[pltpu.HBM(s, t) for s, t in shapes],
        grid=(1,),
        compiler_params=PARAMS,
        cost_estimate=LIGHT,
    )(at, info0, info1)


def saved_kernel(cap, at_ref, gate_ref, up_ref, f1_ref, f2_ref, ha_ref, hb_ref, g3, u3, h3, k3):
    g3[...] = gate_ref[...].astype(F32).reshape(g3.shape)
    u3[...] = up_ref[...].astype(F32).reshape(u3.shape)
    z, c = at_ref[1], at_ref[2]
    for cr in range(NC):
        for zr in range(NZ):
            for xs in range(NX):
                j = (cr * NZ + zr) * NX + xs
                zs = z if zr == 0 else 1 - z
                cs = c if cr == 0 else 1 - c
                q = xs * (NZ * NC) + zs * NC + cs
                gate, upval = g3[q], u3[q]
                sig = jax.nn.sigmoid(gate)
                f1_ref[pl.ds(j * cap, cap), :] = upval * sig * (1.0 + gate * (1.0 - sig))
                f2_ref[pl.ds(j * cap, cap), :] = gate * sig
                h3[j] = gate * sig * upval
    ha_ref[...] = h3[...].reshape(ha_ref.shape).astype(BF16)
    a_to_b(at_ref[0], h3, k3)
    hb_ref[...] = k3[...].reshape(hb_ref.shape).astype(BF16)


def pairs_of_blocks(x):
    for cr in range(NC):
        for zr in range(NZ):
            for d in range(NX):
                yield (cr * NZ + zr) * NX + lax.rem(x + NX - d, NX), (cr * NX + d) * NZ + zr


def a_to_b(x, a3, b3):
    for ja, jb in pairs_of_blocks(x):
        b3[jb] = a3[ja]


def saved(at, gate, up, cap):
    rows, hid = gate.shape
    blocks = rows // cap
    return pl.pallas_call(
        functools.partial(saved_kernel, cap),
        in_specs=[pl.BlockSpec(memory_space=pltpu.SMEM), whole(gate.shape), whole(up.shape)],
        out_specs=[whole((rows, hid))] * 4,
        out_shape=[jax.ShapeDtypeStruct((rows, hid), t) for t in (F32, F32, BF16, BF16)],
        scratch_shapes=[pltpu.VMEM((blocks, cap, hid), F32)] * 4,
        grid=(1,),
        compiler_params=PARAMS,
        cost_estimate=LIGHT,
    )(at, gate, up)


def pack_a(place, weight, tok, start, columns):
    def compute(t, values, fixed, scalar, outs):
        rows = jnp.dot(fixed[0][...], values[0], preferred_element_type=F32)
        return [rows * fixed[1][:, 0:1]]

    out = ((place.shape[0], columns), BF16, 0)
    return over_columns(compute, columns, [(tok, 1, start)], [place, weight], None, [out], [])[0]


def pack_b(place0, weight0, place1, weight1, tok0, start, tok1, cap):
    columns = tok1.shape[1]

    def compute(t, values, fixed, scalar, outs):
        rows0 = jnp.dot(fixed[0][...], values[0], preferred_element_type=F32) * fixed[1][:, 0:1]
        rows1 = jnp.dot(fixed[2][...], values[1], preferred_element_type=F32) * fixed[3][:, 0:1]
        cut = [slice(d * cap, (d + 1) * cap) for d in range(NX)]
        return [jnp.concatenate([rows0[i], rows1[i]], axis=0) for i in cut]

    out = ((NZ * cap, columns), BF16, 0)
    return over_columns(
        compute, columns, [(tok0, 1, start), (tok1, 1, 0)], [place0, weight0, place1, weight1],
        None, [out] * NX, [],
    )


def use_rows(groups, w_down, hid_t, dh, grad, start, want_sum, want_grad, kernel=over_columns):
    hid, width = w_down.shape
    groups = [[e if isinstance(e, tuple) else (e, None) for e in g] for g in groups]
    columns = groups[0][0][0].shape[1]
    lengths = [sum(r[1] if r else a.shape[0] for a, r in g) for g in groups]
    rows = sum(lengths)
    tiled = [(a, 1, 0, r) if r else (a, 1, 0) for g in groups for a, r in g]
    fixed = []
    if want_sum:
        tiled.append((w_down, 1, start))
        if dh is not None:
            fixed.append(dh)
    if want_grad:
        fixed.append(hid_t)

    def compute(t, values, fixed_refs, scalar, outs):
        values, refs = list(values), list(fixed_refs)
        blocks = []
        for g in groups:
            parts = [values.pop(0) for _ in g]
            blocks.append(parts[0] if len(parts) == 1 else jnp.concatenate(parts, axis=0))
        if want_sum:
            before = refs.pop(0) if dh is not None else None
            low = 0
            for block, many in zip(blocks, lengths):
                here = pl.ds(low, many)
                more = lax.dot_general(block, values[0], CONTRACT_LAST, preferred_element_type=F32)
                if t > 0:
                    more += outs[0][here, :]
                elif before is not None:
                    more += before[here, :]
                outs[0][here, :] = more
                low += many
        if not want_grad:
            return []
        total = None
        for i, block in enumerate(blocks):
            more = jnp.dot(refs[0][i], block, preferred_element_type=F32)
            total = more if total is None else total + more
        return [total]

    sums = [((rows, hid), F32)] if want_sum else []
    if not want_grad:
        return kernel(compute, columns, tiled, fixed, None, [], sums)[0]
    done = over_columns(
        compute, columns, tiled, fixed, None, [((hid, width), F32, start)], sums, grad
    )
    return (done[1], done[0]) if want_sum else done[0]


def join(blocks):
    rows, columns = sum(b.shape[0] for b in blocks), blocks[0].shape[1]

    def kernel(*refs):
        out, sems = refs[-2], refs[-1]
        copies, low = [], 0
        for i, b in enumerate(blocks):
            here = out.at[pl.ds(low, b.shape[0]), :]
            copies.append(pltpu.make_async_copy(refs[i], here, sems.at[i]))
            low += b.shape[0]
        for copy in copies:
            copy.start()
        for copy in copies:
            copy.wait()

    return pl.pallas_call(
        kernel,
        in_specs=[pl.BlockSpec(memory_space=pl.ANY)] * len(blocks),
        out_specs=pl.BlockSpec(memory_space=pl.ANY),
        out_shape=pltpu.HBM((rows, columns), blocks[0].dtype),
        scratch_shapes=[pltpu.SemaphoreType.DMA((len(blocks),))],
        compiler_params=PARAMS,
        cost_estimate=LIGHT,
    )(*[in_hbm(b) for b in blocks])


def act_kernel(
    at_ref, near_ref, far0_ref, far1_ref, b0_ref, b1_ref, f1_ref, f2_ref,
    ga_ref, ua_ref, gb_ref, ub_ref, one, two,
):
    x = at_ref[0]
    half = two.shape[0] // NC
    two[pl.ds(0, half)] = b0_ref[...].reshape((half,) + two.shape[1:])
    two[pl.ds(half, half)] = b1_ref[...].reshape((half,) + two.shape[1:])
    for ja, jb in pairs_of_blocks(x):
        one[ja] = two[jb]
    many = far0_ref.shape[0]
    dh = jnp.concatenate(
        [near_ref[pl.ds(0, many), :], far0_ref[...], near_ref[pl.ds(many, many), :], far1_ref[...]],
        axis=0,
    ) + one[...].reshape(f1_ref.shape)
    dgate = dh * f1_ref[...]
    dup = dh * f2_ref[...]
    ga_ref[...] = dgate.astype(BF16)
    ua_ref[...] = dup.astype(BF16)
    for value, out_ref in ((dgate, gb_ref), (dup, ub_ref)):
        one[...] = value.reshape(one.shape)
        a_to_b(x, one, two)
        out_ref[...] = two[...].reshape(out_ref.shape).astype(BF16)


def activations(at, dhs, f1, f2, cap):
    rows, hid = f1.shape
    operands = list(dhs) + [f1, f2]
    return pl.pallas_call(
        act_kernel,
        in_specs=[pl.BlockSpec(memory_space=pltpu.SMEM)] + [whole(a.shape) for a in operands],
        out_specs=[whole((rows, hid))] * 4,
        out_shape=[jax.ShapeDtypeStruct((rows, hid), BF16)] * 4,
        scratch_shapes=[pltpu.VMEM((rows // cap, cap, hid), F32)] * 2,
        grid=(1,),
        compiler_params=PARAMS,
        cost_estimate=LIGHT,
    )(at, *operands)


def parts_of(dg, du, wg, wu, start, columns, half, other, pieces, kernel):
    many = dg.shape[0] // NC
    each = many // pieces
    tiled = [(wg, 0, start), (wu, 0, start)]
    if other is not None:
        tiled.append((other, 1, 0))

    def compute(t, values, fixed, scalar, outs):
        here = pl.ds(half * many, many)
        total = lax.dot_general(
            fixed[0][here, :], values[0], CONTRACT_LAST, preferred_element_type=F32
        )
        total += lax.dot_general(
            fixed[1][here, :], values[1], CONTRACT_LAST, preferred_element_type=F32
        )
        if other is not None:
            total += values[2].astype(F32)
        return [total[i * each : (i + 1) * each] for i in range(pieces)]

    out = ((each, columns), BF16, 0)
    return kernel(compute, columns, tiled, [dg, du], None, [out] * pieces, [])


def sum_z(a, b):
    def compute(t, values, fixed, scalar, outs):
        return [values[0].astype(F32) + values[1].astype(F32)]

    return over_columns(
        compute, a.shape[1], [(a, 1, 0), (b, 1, 0)], [], None, [(a.shape, BF16, 0)], []
    )[0]


def finish_a(place_t, tok, start, rows):
    def compute(t, values, fixed, scalar, outs):
        branch = jnp.dot(fixed[0][...], values[1], preferred_element_type=F32).astype(BF16)
        return [values[0].astype(F32) + branch.astype(F32)]

    out = ((tok.shape[0], rows.shape[1]), BF16, 0)
    return over_columns(
        compute, rows.shape[1], [(tok, 1, start), (rows, 1, 0)], [place_t], None, [out], []
    )[0]


def combine_b(keep, send, blocks):
    columns = blocks[0].shape[1]
    tokens = keep.shape[1]

    def compute(t, values, fixed, scalar, outs):
        totals = []
        for ref in fixed:
            total = None
            for d in range(NX):
                more = jnp.dot(ref[d], values[d], preferred_element_type=F32)
                total = more if total is None else total + more
            totals.append(total)
        return totals

    outs = [((tokens, columns), F32, 0), ((tokens, columns), BF16, 0)]
    return over_columns(compute, columns, [(b, 1, 0) for b in blocks], [keep, send], None, outs, [])


def finish_b(at, own, other, tok0, start, tok1):
    columns = own.shape[1]

    def compute(t, values, fixed, scalar, outs):
        branch = (values[0] + values[1].astype(F32)).astype(BF16)
        tok = jnp.where(scalar[4] == 0, values[2].astype(F32), values[3].astype(F32))
        return [tok + branch.astype(F32)]

    tiled = [(own, 1, 0), (other, 1, 0), (tok0, 1, start), (tok1, 1, 0)]
    return over_columns(compute, columns, tiled, [], at, [(own.shape, BF16, 0)], [])[0]


def place_chunk(piece, width, start, into):
    def kernel(*refs):
        src, dst, sem = refs[0], refs[-2], refs[-1]
        copy = pltpu.make_async_copy(src, dst.at[:, pl.ds(start, piece.shape[1])], sem)
        copy.start()
        copy.wait()

    hbm = pl.BlockSpec(memory_space=pl.ANY)
    operands = [piece] if into is None else [piece, in_hbm(into)]
    return pl.pallas_call(
        kernel,
        in_specs=[hbm] * len(operands),
        out_specs=hbm,
        out_shape=pltpu.HBM((piece.shape[0], width), piece.dtype),
        scratch_shapes=[pltpu.SemaphoreType.DMA],
        input_output_aliases={} if into is None else {1: 0},
        compiler_params=PARAMS,
        cost_estimate=LIGHT,
    )(*operands)


def body(pending, expert_ids, route_weight, gate_saved, up_saved, w_gate, w_up, w_down):
    own = pending[0]
    width = own.shape[1]
    rows, hid = gate_saved.shape[1:]
    cap = rows // (NX * NZ * NC)
    w_gate, w_up, w_down = w_gate[0], w_up[0], w_down[0]
    unit = width // 28
    a0, b0, a1, b1 = EARLY[0] * unit, EARLY[1] * unit, LATE[0] * unit, LATE[1] * unit
    early = a0 + b0
    at_a0, at_b0, at_a1, at_b1 = 0, a0, early, early + a1
    tie = lax.optimization_barrier

    def crossing(s):
        return s % NY == 0

    def swapped(s):
        return s % NY == NY - 1

    tok_a0 = section_move(own[:, :a0], crossing)
    info = jnp.concatenate([expert_ids[0].astype(F32), route_weight[0]], axis=1).T
    info_far = ep_move(info, dz=1)
    tok_b0 = section_move(own[:, a0:early], crossing)
    tok1 = section_move(release(own, tok_a0)[:, early:], crossing)
    section = lax.axis_index("section").astype(jnp.int32)
    position = lax.axis_index("ep").astype(jnp.int32)
    turned = (section % NY == NY - 1).astype(jnp.int32)
    last = jnp.maximum(turned, (section % NY == 0).astype(jnp.int32))
    z = (position >> 1) & 1
    at = jnp.stack([position >> 2, jnp.where(turned == 1, 1 - z, z), position & 1, turned, last])
    info0 = jnp.where(turned == 1, info_far, info)
    info1 = jnp.where(turned == 1, info, info_far)
    place, place_t, weight, place0, weight0, place1, weight1, keep_t, send_t = route(
        at, info0, info1, cap
    )
    f1, f2, hid_a, hid_b = saved(at, gate_saved[0], up_saved[0], cap)
    hid_at = hid_a.reshape(NC * NZ, -1, hid).transpose(0, 2, 1)
    hid_bt = hid_b.reshape(NC, -1, hid).transpose(0, 2, 1)
    hid_near = jnp.stack([hid_at[0], hid_at[2], hid_at[1], hid_at[3]])

    near_a0 = x_exchange(pack_a(place, weight, tok_a0, 0, a0))
    near_a0, far_tok0, f1, f2, hid_at, hid_bt, hid_near = tie(
        (near_a0, ep_move(tok_b0, dz=1), f1, f2, hid_at, hid_bt, hid_near)
    )
    far_a0 = ep_move(near_a0, dz=1)
    sent_b0 = pack_b(place0, weight0, place1, weight1, tok_b0, 0, far_tok0, cap)
    got_b0 = x_moves(sent_b0, 1)
    far_a0, got_b0, tok1 = tie((far_a0, got_b0, tok1))
    near_a1 = x_exchange(pack_a(place, weight, tok1, 0, a1))
    near_a1, far_tok1 = tie((near_a1, ep_move(tok1[:, a1:], dz=1)))
    far_a1 = ep_move(near_a1, dz=1)
    sent_b1 = pack_b(place0, weight0, place1, weight1, tok1, a1, far_tok1, cap)
    got_b1 = x_moves(sent_b1, 1)
    many = NX * cap
    mine0 = join([release(near_a0, sent_b1), far_a0, sent_b0[0]] + got_b0)
    theirs0 = ep_move(mine0, dc=1)
    rows_a0 = [(mine0, (0, many)), (theirs0, (0, many)), (mine0, (many, many)), (theirs0, (many, many))]
    rows_b0 = [(mine0, (2 * many, 2 * many)), (theirs0, (2 * many, 2 * many))]
    dh_a, grad = use_rows([[g] for g in rows_a0], w_down, hid_near, None, None, at_a0, True, True)
    dh_b, grad = use_rows([[g] for g in rows_b0], w_down, hid_bt, None, grad, at_b0, True, True)
    dh_near, dh_far0, dh_far1 = dh_a[: 2 * many], dh_a[2 * many : 3 * many], dh_a[3 * many :]
    dh_b0, dh_b1 = dh_b[: 2 * many], dh_b[2 * many :]

    def more_dh(groups, dh, start):
        return use_rows(groups, w_down, None, dh, None, start, True, False, at_once)

    far_a1, got_b1, dh_near, dh_far0, dh_far1, dh_b0, dh_b1, grad = tie(
        (far_a1, got_b1, dh_near, dh_far0, dh_far1, dh_b0, dh_b1, grad)
    )
    near_a1_other, far_a1_other = ep_move(near_a1, dc=1), ep_move(far_a1, dc=1)
    mine_b1 = [sent_b1[0]] + got_b1
    theirs_b1 = [ep_move(piece, dc=1) for piece in mine_b1]
    dh_b0 = more_dh([mine_b1], dh_b0, at_b1)
    dh_far0 = more_dh([[far_a1]], dh_far0, at_a1)
    dh_near = more_dh([[near_a1], [near_a1_other]], dh_near, at_a1)
    dh_b1 = more_dh([theirs_b1], dh_b1, at_b1)
    dh_far1 = more_dh([[far_a1_other]], dh_far1, at_a1)
    rows_a1 = [[near_a1], [far_a1], [near_a1_other], [far_a1_other]]
    rows_b1 = [mine_b1, theirs_b1]

    grads = activations(at, [dh_near, dh_far0, dh_far1, dh_b0, dh_b1], f1, f2, cap)

    def parts(kind, low, n, other, pieces, kernel, grads):
        dg, du = grads[:2] if kind == "A" else grads[2:]
        half = 1 if other is None else 0
        return parts_of(dg, du, w_gate, w_up, low, n, half, other, pieces, kernel)

    core_b1 = ep_move(parts("B", at_b1, b1, None, 1, at_once, grads)[0], dc=1)
    core_a1 = ep_move(parts("A", at_a1, a1, None, 1, at_once, grads)[0], dc=1)
    part_b1 = parts("B", at_b1, b1, core_b1, NX, at_once, grads)
    back_b1 = x_moves(part_b1, -1)
    keep_a1, send_a1 = parts("A", at_a1, a1, core_a1, NZ, at_once, grads)
    back_a1 = ep_move(send_a1, dz=1)
    grads = release(grads, part_b1, send_a1)
    core_b0 = ep_move(parts("B", at_b0, b0, None, 1, at_once, grads)[0], dc=1)
    core_a0 = ep_move(parts("A", at_a0, a0, None, 1, at_once, grads)[0], dc=1)
    part_b0 = parts("B", at_b0, b0, core_b0, NX, over_columns, grads)
    keep_a0, send_a0 = parts("A", at_a0, a0, core_a0, NZ, over_columns, grads)
    grad = use_rows(rows_a1, w_down, hid_at, None, release(grad, grads), at_a1, False, True)
    grad = use_rows(rows_b1, w_down, hid_bt, None, grad, at_b1, False, True)
    back_b1, back_a1, part_b0, keep_a0, send_a0, grad = tie(
        (back_b1, back_a1, part_b0, keep_a0, send_a0, grad)
    )
    keep_b1, send_b1 = combine_b(keep_t, send_t, [part_b1[0]] + back_b1)
    cross_b1 = ep_move(send_b1, dz=1)
    own_a1 = x_exchange(sum_z(keep_a1, back_a1))
    cross_b1, own_a1, part_b0, send_a0 = tie((cross_b1, own_a1, part_b0, send_a0))
    back_b0 = x_moves(part_b0, -1)
    back_a0 = ep_move(send_a0, dz=1)
    up_b1 = section_move(finish_b(at, keep_b1, cross_b1, tok1, a1, far_tok1), crossing)
    up_a1 = section_move(finish_a(place_t, tok1, 0, own_a1), swapped)
    back_b0, back_a0, up_b1 = tie((back_b0, back_a0, up_b1))
    keep_b0, send_b0 = combine_b(keep_t, send_t, [part_b0[0]] + back_b0)
    cross_b0 = ep_move(send_b0, dz=1)
    own_a0 = x_exchange(sum_z(keep_a0, back_a0))
    up_b0 = section_move(finish_b(at, keep_b0, cross_b0, tok_b0, 0, far_tok0), crossing)
    up_a0 = section_move(finish_a(place_t, tok_a0, 0, own_a0), swapped)
    out = place_chunk(up_b1, width, at_b1, None)
    out = place_chunk(up_a1, width, at_a1, out)
    out = place_chunk(up_b0, width, at_b0, out)
    out = place_chunk(up_a0, width, at_a0, out)
    return (out[None], grad[None])


def solution(mesh):
    placed = (
        P("section", "ep", None),
        P("section", "ep", None),
        P("section", "ep", None),
        P("section", None, "ep"),
        P("section", None, "ep"),
        P("section", None, "ep"),
        P("section", None, "ep"),
        P("section", "ep", None),
    )
    return jax.shard_map(
        body,
        mesh=mesh,
        in_specs=placed,
        out_specs=(P("section", "ep", None), P("section", "ep", None)),
        check_vma=False,
    )
```

```python
import functools

import jax
import jax.numpy as jnp
from jax import lax
from jax.experimental import pallas as pl
from jax.experimental.pallas import tpu as pltpu
from jax.sharding import PartitionSpec as P

NX, NZ, NC, NY = 4, 2, 2, 4
F32, BF16 = jnp.float32, jnp.bfloat16
PARAMS = pltpu.CompilerParams(vmem_limit_bytes=32 << 20)
LIGHT = pl.CostEstimate(flops=1, bytes_accessed=1, transcendentals=0)
EARLY, LATE = (5, 5), (9, 9)
CONTRACT_LAST = (((1,), (1,)), ((), ()))


def section_move(array, flip):
    sections, peers = lax.axis_size("section"), NX * NZ * NC
    pairs = []
    for s in range(sections):
        for q in range(peers):
            to = q ^ NC if flip(s) else q
            pairs.append((s * peers + q, (s - 1) % sections * peers + to))
    return lax.ppermute(array, ("section", "ep"), pairs)


def ep_move(array, dx=0, dz=0, dc=0):
    pairs = []
    for q in range(NX * NZ * NC):
        x, z, c = q // (NZ * NC), q // NC % NZ, q % NC
        pairs.append((q, (x + dx) % NX * NZ * NC + (z ^ dz) * NC + (c ^ dc)))
    return lax.ppermute(array, "ep", pairs)


def x_moves(blocks, sign):
    return [ep_move(blocks[d], dx=sign * d) for d in range(1, NX)]


def x_exchange(array):
    groups = [[x * NZ * NC + i for x in range(NX)] for i in range(NZ * NC)]
    blocks = array.reshape(NX, -1, array.shape[1])
    moved = lax.all_to_all(blocks, "ep", 0, 0, axis_index_groups=groups, tiled=True)
    return moved.reshape(array.shape)


def whole(shape):
    return pl.BlockSpec(shape, lambda *_: (0,) * len(shape))


def in_hbm(array):
    return pltpu.with_memory_space_constraint(array, pltpu.HBM)


def tile_of(columns):
    return max(t for t in range(128, 897, 128) if columns % t == 0)


def release(value, *after):
    return lax.optimization_barrier((value, after))[0]


def at_once(compute, columns, tiled, fixed, scalars, tiled_out, fixed_out):
    n_in, n_fix, n_out = len(tiled), len(fixed), len(tiled_out)

    def kernel(*refs):
        ins, fixes, outs = refs[:n_in], refs[n_in : n_in + n_fix], refs[n_in + n_fix :]
        results = compute(0, [r[...] for r in ins], fixes, None, outs[n_out:])
        for ref, value in zip(outs, results):
            ref[...] = value.astype(ref.dtype)

    operands, specs = [], []
    for array, axis, start in tiled:
        operands.append(array)
        if array.shape[axis] == columns:
            specs.append(whole(array.shape))
            continue
        shape = list(array.shape)
        shape[axis] = columns
        at = (0, start) if axis == 1 else (start, 0)
        specs.append(pl.BlockSpec(tuple(pl.Element(n) for n in shape), lambda *_, at=at: at))
    for array in fixed:
        operands.append(array)
        specs.append(whole(array.shape))
    shapes = [(shape, dtype) for shape, dtype, *_ in tiled_out] + list(fixed_out)
    return pl.pallas_call(
        kernel,
        in_specs=specs,
        out_specs=[whole(shape) for shape, _ in shapes],
        out_shape=[jax.ShapeDtypeStruct(shape, dtype) for shape, dtype in shapes],
        grid=(1,),
        compiler_params=PARAMS,
        cost_estimate=LIGHT,
    )(*operands)


def over_columns(
    compute, columns, tiled, fixed, scalars, tiled_out, fixed_out, into=None, pin=True,
    pin_out=True,
):
    row_windows = [entry[3] if len(entry) > 3 else None for entry in tiled]
    tiled = [entry[:3] for entry in tiled]
    tile = tile_of(columns)
    steps = columns // tile
    n_in, n_fix, n_out = len(tiled), len(fixed), len(tiled_out)

    def kernel(*refs):
        refs = list(refs)
        take = lambda n: [refs.pop(0) for _ in range(n)]
        ins, fixes = take(n_in), take(n_fix)
        scalar = take(1)[0] if scalars is not None else None
        if into is not None:
            take(1)
        outs, fix_outs = take(n_out), take(len(fixed_out))
        in_bufs, out_bufs, fix_bufs = take(n_in), take(n_out), take(n_fix)
        in_sems, out_sems, fix_sems = take(3)

        def window(ref, axis, start, t, rows=None):
            here = pl.ds(start + t * tile, tile)
            if rows is not None:
                return ref.at[pl.ds(*rows), here]
            return ref.at[:, here] if axis == 1 else ref.at[here, :]

        loads = [
            [
                pltpu.make_async_copy(
                    window(ins[i], axis, start, t, row_windows[i]),
                    window(in_bufs[i], axis, 0, t),
                    in_sems.at[i * steps + t],
                )
                for i, (_, axis, start) in enumerate(tiled)
            ]
            for t in range(steps)
        ]
        whole_loads = [
            pltpu.make_async_copy(fixes[i], fix_bufs[i], fix_sems.at[i]) for i in range(n_fix)
        ]
        for copy in whole_loads:
            copy.start()
        for t in range(steps):
            for copy in loads[t]:
                copy.start()
        for copy in whole_loads:
            copy.wait()
        stores = []
        for t in range(steps):
            for copy in loads[t]:
                copy.wait()
            values = [
                window(in_bufs[i], axis, 0, t)[...] for i, (_, axis, _) in enumerate(tiled)
            ]
            for i, value in enumerate(compute(t, values, fix_bufs, scalar, fix_outs)):
                buf = window(out_bufs[i], 1, 0, t)
                buf[...] = value.astype(out_bufs[i].dtype)
                copy = pltpu.make_async_copy(
                    buf, window(outs[i], 1, tiled_out[i][2], t), out_sems.at[i * steps + t]
                )
                copy.start()
                stores.append(copy)
        for copy in stores:
            copy.wait()

    hbm = pl.BlockSpec(memory_space=pl.ANY)
    operands = [in_hbm(a) if pin else a for a in [a for a, _, _ in tiled] + list(fixed)]
    specs = [hbm] * (n_in + n_fix)
    if scalars is not None:
        operands.append(scalars)
        specs.append(pl.BlockSpec(memory_space=pltpu.SMEM))
    aliases = {}
    if into is not None:
        aliases[len(operands)] = 0
        operands.append(in_hbm(into))
        specs.append(hbm)
    buffers = [
        pltpu.VMEM(
            (r[1] if r else a.shape[0], columns) if axis == 1 else (columns, a.shape[1]), a.dtype
        )
        for (a, axis, _), r in zip(tiled, row_windows)
    ] + [pltpu.VMEM((shape[0], columns), dtype) for shape, dtype, _ in tiled_out]
    buffers += [pltpu.VMEM(a.shape, a.dtype) for a in fixed]
    return pl.pallas_call(
        kernel,
        in_specs=specs,
        out_specs=[hbm] * n_out + [pl.BlockSpec(memory_space=pltpu.VMEM)] * len(fixed_out),
        out_shape=[
            (pltpu.HBM if pin_out else jax.ShapeDtypeStruct)(shape, dtype)
            for shape, dtype, _ in tiled_out
        ]
        + [jax.ShapeDtypeStruct(shape, dtype) for shape, dtype in fixed_out],
        scratch_shapes=buffers
        + [
            pltpu.SemaphoreType.DMA((max(1, n_in * steps),)),
            pltpu.SemaphoreType.DMA((max(1, n_out * steps),)),
            pltpu.SemaphoreType.DMA((max(1, n_fix),)),
        ],
        input_output_aliases=aliases,
        compiler_params=PARAMS,
        cost_estimate=LIGHT,
    )(*operands)


def tables_of(cap, info_ref, first_x):
    tokens = info_ref.shape[1]
    row = lax.broadcasted_iota(jnp.int32, (tokens, tokens), 0)
    col = lax.broadcasted_iota(jnp.int32, (tokens, tokens), 1)
    before = (row < col).astype(F32).astype(BF16)
    slot_of = lax.broadcasted_iota(jnp.int32, (cap, tokens), 0).astype(F32)
    places, weights = [], []
    for d in range(NX):
        expert = lax.rem(first_x + d, NX).astype(F32)
        first = info_ref[0:1, :] == expert
        second = info_ref[1:2, :] == expert
        named = jnp.where(first | second, 1.0, 0.0)
        prob = jnp.where(first, info_ref[2:3, :], jnp.where(second, info_ref[3:4, :], 0.0))
        rank = jnp.dot(
            jnp.broadcast_to(named, (8, tokens)).astype(BF16), before, preferred_element_type=F32
        )[0:1]
        placed = jnp.where((slot_of == rank) & (named > 0.0), 1.0, 0.0)
        places.append(placed)
        weights.append(
            jnp.broadcast_to(jnp.sum(placed * prob, axis=1, keepdims=True), (cap, 128))
        )
    return places, weights


def transposed(block):
    tokens = block.shape[1]
    row = lax.broadcasted_iota(jnp.int32, (tokens, tokens), 0)
    col = lax.broadcasted_iota(jnp.int32, (tokens, tokens), 1)
    eye = (row == col).astype(F32).astype(BF16)
    return lax.dot_general(eye, block.astype(BF16), CONTRACT_LAST, preferred_element_type=F32)


def route_kernel(
    cap, at_ref, info0_ref, info1_ref, pa_ref, pat_ref, wa_ref, p0_ref, w0_ref, p1_ref, w1_ref,
    keep_ref, send_ref,
):
    x, last = at_ref[0], at_ref[4].astype(F32)
    places, weights = tables_of(cap, info0_ref, jnp.int32(0))
    pa_ref[...] = jnp.concatenate(places, axis=0).astype(BF16)
    pat_ref[...] = transposed(jnp.concatenate(places, axis=0)).astype(BF16)
    wa_ref[...] = jnp.concatenate(weights, axis=0)
    places0, weights0 = tables_of(cap, info0_ref, x)
    places1, weights1 = tables_of(cap, info1_ref, x)
    p0_ref[...] = jnp.concatenate(places0, axis=0).astype(BF16)
    w0_ref[...] = jnp.concatenate(weights0, axis=0)
    p1_ref[...] = jnp.concatenate(places1, axis=0).astype(BF16)
    w1_ref[...] = jnp.concatenate(weights1, axis=0)
    for d in range(NX):
        keep = jnp.concatenate([places0[d] * (1.0 - last), places1[d] * last], axis=0)
        send = jnp.concatenate([places0[d] * last, places1[d] * (1.0 - last)], axis=0)
        keep_ref[d] = transposed(keep).astype(BF16)
        send_ref[d] = transposed(send).astype(BF16)


def route(at, info0, info1, cap):
    tokens = info0.shape[1]
    slots = NX * cap
    place, weight = (slots, tokens), (slots, 128)
    back = (NX, tokens, NZ * cap)
    shapes = [(place, BF16), ((tokens, slots), BF16), (weight, F32), (place, BF16), (weight, F32)]
    shapes += [(place, BF16), (weight, F32), (back, BF16), (back, BF16)]
    return pl.pallas_call(
        functools.partial(route_kernel, cap),
        in_specs=[pl.BlockSpec(memory_space=pltpu.SMEM), whole(info0.shape), whole(info1.shape)],
        out_specs=[whole(s) for s, _ in shapes],
        out_shape=[pltpu.HBM(s, t) for s, t in shapes],
        grid=(1,),
        compiler_params=PARAMS,
        cost_estimate=LIGHT,
    )(at, info0, info1)


def saved_kernel(cap, at_ref, gate_ref, up_ref, f1_ref, f2_ref, ha_ref, hb_ref, g3, u3, h3, k3):
    g3[...] = gate_ref[...].astype(F32).reshape(g3.shape)
    u3[...] = up_ref[...].astype(F32).reshape(u3.shape)
    z, c = at_ref[1], at_ref[2]
    for cr in range(NC):
        for zr in range(NZ):
            for xs in range(NX):
                j = (cr * NZ + zr) * NX + xs
                zs = z if zr == 0 else 1 - z
                cs = c if cr == 0 else 1 - c
                q = xs * (NZ * NC) + zs * NC + cs
                gate, upval = g3[q], u3[q]
                sig = jax.nn.sigmoid(gate)
                f1_ref[pl.ds(j * cap, cap), :] = upval * sig * (1.0 + gate * (1.0 - sig))
                f2_ref[pl.ds(j * cap, cap), :] = gate * sig
                h3[j] = gate * sig * upval
    ha_ref[...] = h3[...].reshape(ha_ref.shape).astype(BF16)
    a_to_b(at_ref[0], h3, k3)
    hb_ref[...] = k3[...].reshape(hb_ref.shape).astype(BF16)


def pairs_of_blocks(x):
    for cr in range(NC):
        for zr in range(NZ):
            for d in range(NX):
                yield (cr * NZ + zr) * NX + lax.rem(x + NX - d, NX), (cr * NX + d) * NZ + zr


def a_to_b(x, a3, b3):
    for ja, jb in pairs_of_blocks(x):
        b3[jb] = a3[ja]


def saved(at, gate, up, cap):
    rows, hid = gate.shape
    blocks = rows // cap
    return pl.pallas_call(
        functools.partial(saved_kernel, cap),
        in_specs=[pl.BlockSpec(memory_space=pltpu.SMEM), whole(gate.shape), whole(up.shape)],
        out_specs=[whole((rows, hid))] * 4,
        out_shape=[jax.ShapeDtypeStruct((rows, hid), t) for t in (F32, F32, BF16, BF16)],
        scratch_shapes=[pltpu.VMEM((blocks, cap, hid), F32)] * 4,
        grid=(1,),
        compiler_params=PARAMS,
        cost_estimate=LIGHT,
    )(at, gate, up)


def pack_a(place, weight, tok, start, columns):
    def compute(t, values, fixed, scalar, outs):
        rows = jnp.dot(fixed[0][...], values[0], preferred_element_type=F32)
        return [rows * fixed[1][:, 0:1]]

    out = ((place.shape[0], columns), BF16, 0)
    return over_columns(
        compute, columns, [(tok, 1, start)], [place, weight], None, [out], [], pin_out=False
    )[0]


def pack_b(place0, weight0, place1, weight1, tok0, start, tok1, cap):
    columns = tok1.shape[1]

    def compute(t, values, fixed, scalar, outs):
        rows0 = jnp.dot(fixed[0][...], values[0], preferred_element_type=F32) * fixed[1][:, 0:1]
        rows1 = jnp.dot(fixed[2][...], values[1], preferred_element_type=F32) * fixed[3][:, 0:1]
        cut = [slice(d * cap, (d + 1) * cap) for d in range(NX)]
        return [jnp.concatenate([rows0[i], rows1[i]], axis=0) for i in cut]

    out = ((NZ * cap, columns), BF16, 0)
    return over_columns(
        compute, columns, [(tok0, 1, start), (tok1, 1, 0)], [place0, weight0, place1, weight1],
        None, [out] * NX, [], pin_out=False,
    )


def use_rows(groups, w_down, hid_t, dh, grad, start, want_sum, want_grad, kernel=over_columns):
    hid, width = w_down.shape
    groups = [[e if isinstance(e, tuple) else (e, None) for e in g] for g in groups]
    columns = groups[0][0][0].shape[1]
    lengths = [sum(r[1] if r else a.shape[0] for a, r in g) for g in groups]
    rows = sum(lengths)
    tiled = [(a, 1, 0, r) if r else (a, 1, 0) for g in groups for a, r in g]
    fixed = []
    if want_sum:
        tiled.append((w_down, 1, start))
        if dh is not None:
            fixed.append(dh)
    if want_grad:
        fixed.append(hid_t)

    def compute(t, values, fixed_refs, scalar, outs):
        values, refs = list(values), list(fixed_refs)
        blocks = []
        for g in groups:
            parts = [values.pop(0) for _ in g]
            blocks.append(parts[0] if len(parts) == 1 else jnp.concatenate(parts, axis=0))
        if want_sum:
            before = refs.pop(0) if dh is not None else None
            low = 0
            for block, many in zip(blocks, lengths):
                here = pl.ds(low, many)
                more = lax.dot_general(block, values[0], CONTRACT_LAST, preferred_element_type=F32)
                if t > 0:
                    more += outs[0][here, :]
                elif before is not None:
                    more += before[here, :]
                outs[0][here, :] = more
                low += many
        if not want_grad:
            return []
        total = None
        for i, block in enumerate(blocks):
            more = jnp.dot(refs[0][i], block, preferred_element_type=F32)
            total = more if total is None else total + more
        return [total]

    sums = [((rows, hid), F32)] if want_sum else []
    if not want_grad:
        return kernel(compute, columns, tiled, fixed, None, [], sums)[0]
    done = over_columns(
        compute, columns, tiled, fixed, None, [((hid, width), F32, start)], sums, grad
    )
    return (done[1], done[0]) if want_sum else done[0]


def join(blocks):
    rows, columns = sum(b.shape[0] for b in blocks), blocks[0].shape[1]

    def compute(t, values, fixed, scalar, outs):
        return [jnp.concatenate(values, axis=0)]

    out = ((rows, columns), blocks[0].dtype, 0)
    return over_columns(compute, columns, [(b, 1, 0) for b in blocks], [], None, [out], [])[0]


def act_kernel(
    at_ref, near_ref, far0_ref, far1_ref, b0_ref, b1_ref, f1_ref, f2_ref,
    ga_ref, ua_ref, gb_ref, ub_ref, one, two,
):
    x = at_ref[0]
    half = two.shape[0] // NC
    two[pl.ds(0, half)] = b0_ref[...].reshape((half,) + two.shape[1:])
    two[pl.ds(half, half)] = b1_ref[...].reshape((half,) + two.shape[1:])
    for ja, jb in pairs_of_blocks(x):
        one[ja] = two[jb]
    many = far0_ref.shape[0]
    dh = jnp.concatenate(
        [near_ref[pl.ds(0, many), :], far0_ref[...], near_ref[pl.ds(many, many), :], far1_ref[...]],
        axis=0,
    ) + one[...].reshape(f1_ref.shape)
    dgate = dh * f1_ref[...]
    dup = dh * f2_ref[...]
    ga_ref[...] = dgate.astype(BF16)
    ua_ref[...] = dup.astype(BF16)
    for value, out_ref in ((dgate, gb_ref), (dup, ub_ref)):
        one[...] = value.reshape(one.shape)
        a_to_b(x, one, two)
        out_ref[...] = two[...].reshape(out_ref.shape).astype(BF16)


def activations(at, dhs, f1, f2, cap):
    rows, hid = f1.shape
    operands = list(dhs) + [f1, f2]
    return pl.pallas_call(
        act_kernel,
        in_specs=[pl.BlockSpec(memory_space=pltpu.SMEM)] + [whole(a.shape) for a in operands],
        out_specs=[whole((rows, hid))] * 4,
        out_shape=[jax.ShapeDtypeStruct((rows, hid), BF16)] * 4,
        scratch_shapes=[pltpu.VMEM((rows // cap, cap, hid), F32)] * 2,
        grid=(1,),
        compiler_params=PARAMS,
        cost_estimate=LIGHT,
    )(at, *operands)


def parts_of(dg, du, wg, wu, start, columns, half, other, pieces, kernel):
    many = dg.shape[0] // NC
    each = many // pieces
    tiled = [(wg, 0, start), (wu, 0, start)]
    if other is not None:
        tiled.append((other, 1, 0))

    def compute(t, values, fixed, scalar, outs):
        here = pl.ds(half * many, many)
        total = lax.dot_general(
            fixed[0][here, :], values[0], CONTRACT_LAST, preferred_element_type=F32
        )
        total += lax.dot_general(
            fixed[1][here, :], values[1], CONTRACT_LAST, preferred_element_type=F32
        )
        if other is not None:
            total += values[2].astype(F32)
        return [total[i * each : (i + 1) * each] for i in range(pieces)]

    out = ((each, columns), BF16, 0)
    return kernel(compute, columns, tiled, [dg, du], None, [out] * pieces, [])


def sum_z(a, b):
    def compute(t, values, fixed, scalar, outs):
        return [values[0].astype(F32) + values[1].astype(F32)]

    return over_columns(
        compute, a.shape[1], [(a, 1, 0), (b, 1, 0)], [], None, [(a.shape, BF16, 0)], []
    )[0]


def finish_a(place_t, tok, start, rows):
    def compute(t, values, fixed, scalar, outs):
        branch = jnp.dot(fixed[0][...], values[1], preferred_element_type=F32).astype(BF16)
        return [values[0].astype(F32) + branch.astype(F32)]

    out = ((tok.shape[0], rows.shape[1]), BF16, 0)
    return over_columns(
        compute, rows.shape[1], [(tok, 1, start), (rows, 1, 0)], [place_t], None, [out], []
    )[0]


def combine_b(keep, send, blocks):
    columns = blocks[0].shape[1]
    tokens = keep.shape[1]

    def compute(t, values, fixed, scalar, outs):
        totals = []
        for ref in fixed:
            total = None
            for d in range(NX):
                more = jnp.dot(ref[d], values[d], preferred_element_type=F32)
                total = more if total is None else total + more
            totals.append(total)
        return totals

    outs = [((tokens, columns), F32, 0), ((tokens, columns), BF16, 0)]
    return over_columns(compute, columns, [(b, 1, 0) for b in blocks], [keep, send], None, outs, [])


def finish_b(at, own, other, tok0, start, tok1):
    columns = own.shape[1]

    def compute(t, values, fixed, scalar, outs):
        branch = (values[0] + values[1].astype(F32)).astype(BF16)
        tok = jnp.where(scalar[4] == 0, values[2].astype(F32), values[3].astype(F32))
        return [tok + branch.astype(F32)]

    tiled = [(own, 1, 0), (other, 1, 0), (tok0, 1, start), (tok1, 1, 0)]
    return over_columns(compute, columns, tiled, [], at, [(own.shape, BF16, 0)], [])[0]


def place_chunk(piece, width, start, into):
    def compute(t, values, fixed, scalar, outs):
        return values

    columns = piece.shape[1]
    out = ((piece.shape[0], width), piece.dtype, start)
    return over_columns(compute, columns, [(piece, 1, 0)], [], None, [out], [], into, False)[0]


def body(pending, expert_ids, route_weight, gate_saved, up_saved, w_gate, w_up, w_down):
    own = pending[0]
    width = own.shape[1]
    rows, hid = gate_saved.shape[1:]
    cap = rows // (NX * NZ * NC)
    w_gate, w_up, w_down = w_gate[0], w_up[0], w_down[0]
    unit = width // 28
    a0, b0, a1, b1 = EARLY[0] * unit, EARLY[1] * unit, LATE[0] * unit, LATE[1] * unit
    early = a0 + b0
    at_a0, at_b0, at_a1, at_b1 = 0, a0, early, early + a1
    tie = lax.optimization_barrier

    def crossing(s):
        return s % NY == 0

    def swapped(s):
        return s % NY == NY - 1

    tok_a0 = section_move(own[:, :a0], crossing)
    info = jnp.concatenate([expert_ids[0].astype(F32), route_weight[0]], axis=1).T
    info_far = ep_move(info, dz=1)
    tok_b0 = section_move(own[:, a0:early], crossing)
    tok1 = section_move(release(own, tok_a0)[:, early:], crossing)
    section = lax.axis_index("section").astype(jnp.int32)
    position = lax.axis_index("ep").astype(jnp.int32)
    turned = (section % NY == NY - 1).astype(jnp.int32)
    last = jnp.maximum(turned, (section % NY == 0).astype(jnp.int32))
    z = (position >> 1) & 1
    at = jnp.stack([position >> 2, jnp.where(turned == 1, 1 - z, z), position & 1, turned, last])
    info0 = jnp.where(turned == 1, info_far, info)
    info1 = jnp.where(turned == 1, info, info_far)
    place, place_t, weight, place0, weight0, place1, weight1, keep_t, send_t = route(
        at, info0, info1, cap
    )

    near_a0 = x_exchange(pack_a(place, weight, tok_a0, 0, a0))
    near_a0, far_tok0, at_later = tie((near_a0, ep_move(tok_b0, dz=1), at))
    far_a0 = ep_move(near_a0, dz=1)
    sent_b0 = pack_b(place0, weight0, place1, weight1, tok_b0, 0, far_tok0, cap)
    got_b0 = x_moves(sent_b0, 1)
    f1, f2, hid_a, hid_b = saved(at_later, gate_saved[0], up_saved[0], cap)
    hid_at = hid_a.reshape(NC * NZ, -1, hid).transpose(0, 2, 1)
    hid_bt = hid_b.reshape(NC, -1, hid).transpose(0, 2, 1)
    hid_near = jnp.stack([hid_at[0], hid_at[2], hid_at[1], hid_at[3]])
    packed_a1, tok_b1 = pack_a(place, weight, tok1, 0, a1), tok1[:, a1:]
    far_a0, got_b0, packed_a1, tok_b1, f1, f2, hid_at, hid_bt, hid_near = tie(
        (far_a0, got_b0, packed_a1, tok_b1, f1, f2, hid_at, hid_bt, hid_near)
    )
    near_a1 = x_exchange(packed_a1)
    far_tok1 = ep_move(tok_b1, dz=1)
    mine0 = join([near_a0, far_a0, sent_b0[0]] + got_b0)
    theirs0 = ep_move(mine0, dc=1)
    near_a1, far_tok1, mine0, theirs0 = tie((near_a1, far_tok1, mine0, theirs0))
    far_a1 = ep_move(near_a1, dz=1)
    sent_b1 = pack_b(place0, weight0, place1, weight1, tok_b1, 0, far_tok1, cap)
    got_b1 = x_moves(sent_b1, 1)
    many = NX * cap
    rows_a0 = [(mine0, (0, many)), (theirs0, (0, many)), (mine0, (many, many)), (theirs0, (many, many))]
    rows_b0 = [(mine0, (2 * many, 2 * many)), (theirs0, (2 * many, 2 * many))]
    dh_a, grad = use_rows([[g] for g in rows_a0], w_down, hid_near, None, None, at_a0, True, True)
    dh_b, grad = use_rows([[g] for g in rows_b0], w_down, hid_bt, None, grad, at_b0, True, True)
    dh_near, dh_far0, dh_far1 = dh_a[: 2 * many], dh_a[2 * many : 3 * many], dh_a[3 * many :]
    dh_b0, dh_b1 = dh_b[: 2 * many], dh_b[2 * many :]

    def more_dh(groups, dh, start):
        return use_rows(groups, w_down, None, dh, None, start, True, False, at_once)

    far_a1, got_b1, dh_near, dh_far0, dh_far1, dh_b0, dh_b1, grad = tie(
        (far_a1, got_b1, dh_near, dh_far0, dh_far1, dh_b0, dh_b1, grad)
    )
    near_a1_other, far_a1_other = ep_move(near_a1, dc=1), ep_move(far_a1, dc=1)
    mine_b1 = [sent_b1[0]] + got_b1
    theirs_b1 = [ep_move(piece, dc=1) for piece in mine_b1]
    dh_b0 = more_dh([mine_b1], dh_b0, at_b1)
    dh_far0 = more_dh([[far_a1]], dh_far0, at_a1)
    dh_near = more_dh([[near_a1], [near_a1_other]], dh_near, at_a1)
    dh_b1 = more_dh([theirs_b1], dh_b1, at_b1)
    dh_far1 = more_dh([[far_a1_other]], dh_far1, at_a1)
    rows_a1 = [[near_a1], [far_a1], [near_a1_other], [far_a1_other]]
    rows_b1 = [mine_b1, theirs_b1]

    grads = activations(at, [dh_near, dh_far0, dh_far1, dh_b0, dh_b1], f1, f2, cap)

    def parts(kind, low, n, other, pieces, kernel, grads):
        dg, du = grads[:2] if kind == "A" else grads[2:]
        half = 1 if other is None else 0
        return parts_of(dg, du, w_gate, w_up, low, n, half, other, pieces, kernel)

    core_b1 = ep_move(parts("B", at_b1, b1, None, 1, at_once, grads)[0], dc=1)
    core_a1 = ep_move(parts("A", at_a1, a1, None, 1, at_once, grads)[0], dc=1)
    part_b1 = parts("B", at_b1, b1, core_b1, NX, at_once, grads)
    back_b1 = x_moves(part_b1, -1)
    keep_a1, send_a1 = parts("A", at_a1, a1, core_a1, NZ, at_once, grads)
    back_a1 = ep_move(send_a1, dz=1)
    grads = release(grads, part_b1, send_a1)
    core_b0 = ep_move(parts("B", at_b0, b0, None, 1, at_once, grads)[0], dc=1)
    core_a0 = ep_move(parts("A", at_a0, a0, None, 1, at_once, grads)[0], dc=1)
    part_b0 = parts("B", at_b0, b0, core_b0, NX, over_columns, grads)
    keep_a0, send_a0 = parts("A", at_a0, a0, core_a0, NZ, over_columns, grads)
    grad = use_rows(rows_a1, w_down, hid_at, None, release(grad, grads), at_a1, False, True)
    grad = use_rows(rows_b1, w_down, hid_bt, None, grad, at_b1, False, True)
    back_b1, back_a1, part_b0, keep_a0, send_a0, grad = tie(
        (back_b1, back_a1, part_b0, keep_a0, send_a0, grad)
    )
    keep_b1, send_b1 = combine_b(keep_t, send_t, [part_b1[0]] + back_b1)
    cross_b1 = ep_move(send_b1, dz=1)
    own_a1 = x_exchange(sum_z(keep_a1, release(back_a1, send_b1)))
    back_b0 = x_moves(part_b0, -1)
    back_a0 = ep_move(release(send_a0, cross_b1), dz=1)
    up_b1 = section_move(finish_b(at, keep_b1, cross_b1, tok_b1, 0, far_tok1), crossing)
    done_a1 = finish_a(place_t, tok1, 0, own_a1)
    back_b0, back_a0, done_a1, up_b1 = tie((back_b0, back_a0, done_a1, up_b1))
    up_a1 = section_move(done_a1, swapped)
    keep_b0, send_b0 = combine_b(keep_t, send_t, [part_b0[0]] + back_b0)
    cross_b0 = ep_move(send_b0, dz=1)
    own_a0 = x_exchange(sum_z(keep_a0, release(back_a0, send_b0)))
    up_b0 = section_move(finish_b(at, keep_b0, cross_b0, tok_b0, 0, far_tok0), crossing)
    up_a0 = section_move(finish_a(place_t, tok_a0, 0, own_a0), swapped)
    out = place_chunk(up_b1, width, at_b1, None)
    out = place_chunk(up_a1, width, at_a1, out)
    out = place_chunk(up_b0, width, at_b0, out)
    out = place_chunk(up_a0, width, at_a0, out)
    return (out[None], grad[None])


def solution(mesh):
    placed = (
        P("section", "ep", None),
        P("section", "ep", None),
        P("section", "ep", None),
        P("section", None, "ep"),
        P("section", None, "ep"),
        P("section", None, "ep"),
        P("section", None, "ep"),
        P("section", "ep", None),
    )
    return jax.shard_map(
        body,
        mesh=mesh,
        in_specs=placed,
        out_specs=(P("section", "ep", None), P("section", "ep", None)),
        check_vma=False,
    )
```

```python
import functools

import jax
import jax.numpy as jnp
from jax import lax
from jax.experimental import pallas as pl
from jax.experimental.pallas import tpu as pltpu
from jax.sharding import PartitionSpec as P

NX, NZ, NC, NY = 4, 2, 2, 4
F32, BF16 = jnp.float32, jnp.bfloat16
PARAMS = pltpu.CompilerParams(vmem_limit_bytes=32 << 20)
LIGHT = pl.CostEstimate(flops=1, bytes_accessed=1, transcendentals=0)
EARLY, LATE = (5, 5), (9, 9)
CONTRACT_LAST = (((1,), (1,)), ((), ()))


def section_move(array, flip):
    sections, peers = lax.axis_size("section"), NX * NZ * NC
    pairs = []
    for s in range(sections):
        for q in range(peers):
            to = q ^ NC if flip(s) else q
            pairs.append((s * peers + q, (s - 1) % sections * peers + to))
    return lax.ppermute(array, ("section", "ep"), pairs)


def ep_move(array, dx=0, dz=0, dc=0):
    pairs = []
    for q in range(NX * NZ * NC):
        x, z, c = q // (NZ * NC), q // NC % NZ, q % NC
        pairs.append((q, (x + dx) % NX * NZ * NC + (z ^ dz) * NC + (c ^ dc)))
    return lax.ppermute(array, "ep", pairs)


def x_moves(blocks, sign):
    return [ep_move(blocks[d], dx=sign * d) for d in range(1, NX)]


def x_exchange(array):
    groups = [[x * NZ * NC + i for x in range(NX)] for i in range(NZ * NC)]
    blocks = array.reshape(NX, -1, array.shape[1])
    moved = lax.all_to_all(blocks, "ep", 0, 0, axis_index_groups=groups, tiled=True)
    return moved.reshape(array.shape)


def whole(shape):
    return pl.BlockSpec(shape, lambda *_: (0,) * len(shape))


def in_hbm(array):
    return pltpu.with_memory_space_constraint(array, pltpu.HBM)


def tile_of(columns):
    return max(t for t in range(128, 897, 128) if columns % t == 0)


def release(value, *after):
    return lax.optimization_barrier((value, after))[0]


def at_once(compute, columns, tiled, fixed, scalars, tiled_out, fixed_out):
    n_in, n_fix, n_out = len(tiled), len(fixed), len(tiled_out)

    def kernel(*refs):
        ins, fixes, outs = refs[:n_in], refs[n_in : n_in + n_fix], refs[n_in + n_fix :]
        results = compute(0, [r[...] for r in ins], fixes, None, outs[n_out:])
        for ref, value in zip(outs, results):
            ref[...] = value.astype(ref.dtype)

    operands, specs = [], []
    for array, axis, start in tiled:
        operands.append(array)
        if array.shape[axis] == columns:
            specs.append(whole(array.shape))
            continue
        shape = list(array.shape)
        shape[axis] = columns
        at = (0, start) if axis == 1 else (start, 0)
        specs.append(pl.BlockSpec(tuple(pl.Element(n) for n in shape), lambda *_, at=at: at))
    for array in fixed:
        operands.append(array)
        specs.append(whole(array.shape))
    shapes = [(shape, dtype) for shape, dtype, *_ in tiled_out] + list(fixed_out)
    return pl.pallas_call(
        kernel,
        in_specs=specs,
        out_specs=[whole(shape) for shape, _ in shapes],
        out_shape=[jax.ShapeDtypeStruct(shape, dtype) for shape, dtype in shapes],
        grid=(1,),
        compiler_params=PARAMS,
        cost_estimate=LIGHT,
    )(*operands)


def over_columns(
    compute, columns, tiled, fixed, scalars, tiled_out, fixed_out, into=None, pin=True,
    pin_out=True,
):
    row_windows = [entry[3] if len(entry) > 3 else None for entry in tiled]
    tiled = [entry[:3] for entry in tiled]
    tile = tile_of(columns)
    steps = columns // tile
    n_in, n_fix, n_out = len(tiled), len(fixed), len(tiled_out)

    def kernel(*refs):
        refs = list(refs)
        take = lambda n: [refs.pop(0) for _ in range(n)]
        ins, fixes = take(n_in), take(n_fix)
        scalar = take(1)[0] if scalars is not None else None
        if into is not None:
            take(1)
        outs, fix_outs = take(n_out), take(len(fixed_out))
        in_bufs, out_bufs, fix_bufs = take(n_in), take(n_out), take(n_fix)
        in_sems, out_sems, fix_sems = take(3)

        def window(ref, axis, start, t, rows=None):
            here = pl.ds(start + t * tile, tile)
            if rows is not None:
                return ref.at[pl.ds(*rows), here]
            return ref.at[:, here] if axis == 1 else ref.at[here, :]

        loads = [
            [
                pltpu.make_async_copy(
                    window(ins[i], axis, start, t, row_windows[i]),
                    window(in_bufs[i], axis, 0, t),
                    in_sems.at[i * steps + t],
                )
                for i, (_, axis, start) in enumerate(tiled)
            ]
            for t in range(steps)
        ]
        whole_loads = [
            pltpu.make_async_copy(fixes[i], fix_bufs[i], fix_sems.at[i]) for i in range(n_fix)
        ]
        for copy in whole_loads:
            copy.start()
        for t in range(steps):
            for copy in loads[t]:
                copy.start()
        for copy in whole_loads:
            copy.wait()
        stores = []
        for t in range(steps):
            for copy in loads[t]:
                copy.wait()
            values = [
                window(in_bufs[i], axis, 0, t)[...] for i, (_, axis, _) in enumerate(tiled)
            ]
            for i, value in enumerate(compute(t, values, fix_bufs, scalar, fix_outs)):
                buf = window(out_bufs[i], 1, 0, t)
                buf[...] = value.astype(out_bufs[i].dtype)
                copy = pltpu.make_async_copy(
                    buf, window(outs[i], 1, tiled_out[i][2], t), out_sems.at[i * steps + t]
                )
                copy.start()
                stores.append(copy)
        for copy in stores:
            copy.wait()

    hbm = pl.BlockSpec(memory_space=pl.ANY)
    operands = [in_hbm(a) if pin else a for a in [a for a, _, _ in tiled] + list(fixed)]
    specs = [hbm] * (n_in + n_fix)
    if scalars is not None:
        operands.append(scalars)
        specs.append(pl.BlockSpec(memory_space=pltpu.SMEM))
    aliases = {}
    if into is not None:
        aliases[len(operands)] = 0
        operands.append(in_hbm(into))
        specs.append(hbm)
    buffers = [
        pltpu.VMEM(
            (r[1] if r else a.shape[0], columns) if axis == 1 else (columns, a.shape[1]), a.dtype
        )
        for (a, axis, _), r in zip(tiled, row_windows)
    ] + [pltpu.VMEM((shape[0], columns), dtype) for shape, dtype, _ in tiled_out]
    buffers += [pltpu.VMEM(a.shape, a.dtype) for a in fixed]
    return pl.pallas_call(
        kernel,
        in_specs=specs,
        out_specs=[hbm] * n_out + [pl.BlockSpec(memory_space=pltpu.VMEM)] * len(fixed_out),
        out_shape=[
            (pltpu.HBM if pin_out else jax.ShapeDtypeStruct)(shape, dtype)
            for shape, dtype, _ in tiled_out
        ]
        + [jax.ShapeDtypeStruct(shape, dtype) for shape, dtype in fixed_out],
        scratch_shapes=buffers
        + [
            pltpu.SemaphoreType.DMA((max(1, n_in * steps),)),
            pltpu.SemaphoreType.DMA((max(1, n_out * steps),)),
            pltpu.SemaphoreType.DMA((max(1, n_fix),)),
        ],
        input_output_aliases=aliases,
        compiler_params=PARAMS,
        cost_estimate=LIGHT,
    )(*operands)


def tables_of(cap, info_ref, first_x):
    tokens = info_ref.shape[1]
    row = lax.broadcasted_iota(jnp.int32, (tokens, tokens), 0)
    col = lax.broadcasted_iota(jnp.int32, (tokens, tokens), 1)
    before = (row < col).astype(F32).astype(BF16)
    slot_of = lax.broadcasted_iota(jnp.int32, (cap, tokens), 0).astype(F32)
    places, weights = [], []
    for d in range(NX):
        expert = lax.rem(first_x + d, NX).astype(F32)
        first = info_ref[0:1, :] == expert
        second = info_ref[1:2, :] == expert
        named = jnp.where(first | second, 1.0, 0.0)
        prob = jnp.where(first, info_ref[2:3, :], jnp.where(second, info_ref[3:4, :], 0.0))
        rank = jnp.dot(
            jnp.broadcast_to(named, (8, tokens)).astype(BF16), before, preferred_element_type=F32
        )[0:1]
        placed = jnp.where((slot_of == rank) & (named > 0.0), 1.0, 0.0)
        places.append(placed)
        weights.append(
            jnp.broadcast_to(jnp.sum(placed * prob, axis=1, keepdims=True), (cap, 128))
        )
    return places, weights


def transposed(block):
    tokens = block.shape[1]
    row = lax.broadcasted_iota(jnp.int32, (tokens, tokens), 0)
    col = lax.broadcasted_iota(jnp.int32, (tokens, tokens), 1)
    eye = (row == col).astype(F32).astype(BF16)
    return lax.dot_general(eye, block.astype(BF16), CONTRACT_LAST, preferred_element_type=F32)


def route_kernel(
    cap, at_ref, info0_ref, info1_ref, pa_ref, pat_ref, wa_ref, p0_ref, w0_ref, p1_ref, w1_ref,
    keep_ref, send_ref,
):
    x, last = at_ref[0], at_ref[4].astype(F32)
    places, weights = tables_of(cap, info0_ref, jnp.int32(0))
    pa_ref[...] = jnp.concatenate(places, axis=0).astype(BF16)
    pat_ref[...] = transposed(jnp.concatenate(places, axis=0)).astype(BF16)
    wa_ref[...] = jnp.concatenate(weights, axis=0)
    places0, weights0 = tables_of(cap, info0_ref, x)
    places1, weights1 = tables_of(cap, info1_ref, x)
    p0_ref[...] = jnp.concatenate(places0, axis=0).astype(BF16)
    w0_ref[...] = jnp.concatenate(weights0, axis=0)
    p1_ref[...] = jnp.concatenate(places1, axis=0).astype(BF16)
    w1_ref[...] = jnp.concatenate(weights1, axis=0)
    for d in range(NX):
        keep = jnp.concatenate([places0[d] * (1.0 - last), places1[d] * last], axis=0)
        send = jnp.concatenate([places0[d] * last, places1[d] * (1.0 - last)], axis=0)
        keep_ref[d] = transposed(keep).astype(BF16)
        send_ref[d] = transposed(send).astype(BF16)


def route(at, info0, info1, cap):
    tokens = info0.shape[1]
    slots = NX * cap
    place, weight = (slots, tokens), (slots, 128)
    back = (NX, tokens, NZ * cap)
    shapes = [(place, BF16), ((tokens, slots), BF16), (weight, F32), (place, BF16), (weight, F32)]
    shapes += [(place, BF16), (weight, F32), (back, BF16), (back, BF16)]
    return pl.pallas_call(
        functools.partial(route_kernel, cap),
        in_specs=[pl.BlockSpec(memory_space=pltpu.SMEM), whole(info0.shape), whole(info1.shape)],
        out_specs=[whole(s) for s, _ in shapes],
        out_shape=[pltpu.HBM(s, t) for s, t in shapes],
        grid=(1,),
        compiler_params=PARAMS,
        cost_estimate=LIGHT,
    )(at, info0, info1)


def saved_kernel(cap, at_ref, gate_ref, up_ref, f1_ref, f2_ref, ha_ref, hb_ref, g3, u3, h3, k3):
    g3[...] = gate_ref[...].astype(F32).reshape(g3.shape)
    u3[...] = up_ref[...].astype(F32).reshape(u3.shape)
    z, c = at_ref[1], at_ref[2]
    for cr in range(NC):
        for zr in range(NZ):
            for xs in range(NX):
                j = (cr * NZ + zr) * NX + xs
                zs = z if zr == 0 else 1 - z
                cs = c if cr == 0 else 1 - c
                q = xs * (NZ * NC) + zs * NC + cs
                gate, upval = g3[q], u3[q]
                sig = jax.nn.sigmoid(gate)
                f1_ref[pl.ds(j * cap, cap), :] = upval * sig * (1.0 + gate * (1.0 - sig))
                f2_ref[pl.ds(j * cap, cap), :] = gate * sig
                h3[j] = gate * sig * upval
    ha_ref[...] = h3[...].reshape(ha_ref.shape).astype(BF16)
    a_to_b(at_ref[0], h3, k3)
    hb_ref[...] = k3[...].reshape(hb_ref.shape).astype(BF16)


def pairs_of_blocks(x):
    for cr in range(NC):
        for zr in range(NZ):
            for d in range(NX):
                yield (cr * NZ + zr) * NX + lax.rem(x + NX - d, NX), (cr * NX + d) * NZ + zr


def a_to_b(x, a3, b3):
    for ja, jb in pairs_of_blocks(x):
        b3[jb] = a3[ja]


def saved(at, gate, up, cap):
    rows, hid = gate.shape
    blocks = rows // cap
    return pl.pallas_call(
        functools.partial(saved_kernel, cap),
        in_specs=[pl.BlockSpec(memory_space=pltpu.SMEM), whole(gate.shape), whole(up.shape)],
        out_specs=[whole((rows, hid))] * 4,
        out_shape=[jax.ShapeDtypeStruct((rows, hid), t) for t in (F32, F32, BF16, BF16)],
        scratch_shapes=[pltpu.VMEM((blocks, cap, hid), F32)] * 4,
        grid=(1,),
        compiler_params=PARAMS,
        cost_estimate=LIGHT,
    )(at, gate, up)


def pack_a(place, weight, tok, start, columns):
    def compute(t, values, fixed, scalar, outs):
        rows = jnp.dot(fixed[0][...], values[0], preferred_element_type=F32)
        return [rows * fixed[1][:, 0:1]]

    out = ((place.shape[0], columns), BF16, 0)
    return over_columns(
        compute, columns, [(tok, 1, start)], [place, weight], None, [out], [], pin_out=False
    )[0]


def pack_b(place0, weight0, place1, weight1, tok0, start, tok1, cap):
    columns = tok1.shape[1]

    def compute(t, values, fixed, scalar, outs):
        rows0 = jnp.dot(fixed[0][...], values[0], preferred_element_type=F32) * fixed[1][:, 0:1]
        rows1 = jnp.dot(fixed[2][...], values[1], preferred_element_type=F32) * fixed[3][:, 0:1]
        cut = [slice(d * cap, (d + 1) * cap) for d in range(NX)]
        return [jnp.concatenate([rows0[i], rows1[i]], axis=0) for i in cut]

    out = ((NZ * cap, columns), BF16, 0)
    return over_columns(
        compute, columns, [(tok0, 1, start), (tok1, 1, 0)], [place0, weight0, place1, weight1],
        None, [out] * NX, [], pin_out=False,
    )


def use_rows(groups, w_down, hid_t, dh, grad, start, want_sum, want_grad, kernel=over_columns):
    hid, width = w_down.shape
    groups = [[e if isinstance(e, tuple) else (e, None) for e in g] for g in groups]
    columns = groups[0][0][0].shape[1]
    lengths = [sum(r[1] if r else a.shape[0] for a, r in g) for g in groups]
    rows = sum(lengths)
    tiled = [(a, 1, 0, r) if r else (a, 1, 0) for g in groups for a, r in g]
    fixed = []
    if want_sum:
        tiled.append((w_down, 1, start))
        if dh is not None:
            fixed.append(dh)
    if want_grad:
        fixed.append(hid_t)

    def compute(t, values, fixed_refs, scalar, outs):
        values, refs = list(values), list(fixed_refs)
        blocks = []
        for g in groups:
            parts = [values.pop(0) for _ in g]
            blocks.append(parts[0] if len(parts) == 1 else jnp.concatenate(parts, axis=0))
        if want_sum:
            before = refs.pop(0) if dh is not None else None
            low = 0
            for block, many in zip(blocks, lengths):
                here = pl.ds(low, many)
                more = lax.dot_general(block, values[0], CONTRACT_LAST, preferred_element_type=F32)
                if t > 0:
                    more += outs[0][here, :]
                elif before is not None:
                    more += before[here, :]
                outs[0][here, :] = more
                low += many
        if not want_grad:
            return []
        total = None
        for i, block in enumerate(blocks):
            more = jnp.dot(refs[0][i], block, preferred_element_type=F32)
            total = more if total is None else total + more
        return [total]

    sums = [((rows, hid), F32)] if want_sum else []
    if not want_grad:
        return kernel(compute, columns, tiled, fixed, None, [], sums)[0]
    done = over_columns(
        compute, columns, tiled, fixed, None, [((hid, width), F32, start)], sums, grad
    )
    return (done[1], done[0]) if want_sum else done[0]


def join(blocks):
    rows, columns = sum(b.shape[0] for b in blocks), blocks[0].shape[1]

    def compute(t, values, fixed, scalar, outs):
        return [jnp.concatenate(values, axis=0)]

    out = ((rows, columns), blocks[0].dtype, 0)
    return over_columns(compute, columns, [(b, 1, 0) for b in blocks], [], None, [out], [])[0]


def act_kernel(
    at_ref, near_ref, far0_ref, far1_ref, b0_ref, b1_ref, f1_ref, f2_ref,
    ga_ref, ua_ref, gb_ref, ub_ref, one, two,
):
    x = at_ref[0]
    half = two.shape[0] // NC
    two[pl.ds(0, half)] = b0_ref[...].reshape((half,) + two.shape[1:])
    two[pl.ds(half, half)] = b1_ref[...].reshape((half,) + two.shape[1:])
    for ja, jb in pairs_of_blocks(x):
        one[ja] = two[jb]
    many = far0_ref.shape[0]
    dh = jnp.concatenate(
        [near_ref[pl.ds(0, many), :], far0_ref[...], near_ref[pl.ds(many, many), :], far1_ref[...]],
        axis=0,
    ) + one[...].reshape(f1_ref.shape)
    dgate = dh * f1_ref[...]
    dup = dh * f2_ref[...]
    ga_ref[...] = dgate.astype(BF16)
    ua_ref[...] = dup.astype(BF16)
    for value, out_ref in ((dgate, gb_ref), (dup, ub_ref)):
        one[...] = value.reshape(one.shape)
        a_to_b(x, one, two)
        out_ref[...] = two[...].reshape(out_ref.shape).astype(BF16)


def activations(at, dhs, f1, f2, cap):
    rows, hid = f1.shape
    operands = list(dhs) + [f1, f2]
    return pl.pallas_call(
        act_kernel,
        in_specs=[pl.BlockSpec(memory_space=pltpu.SMEM)] + [whole(a.shape) for a in operands],
        out_specs=[whole((rows, hid))] * 4,
        out_shape=[jax.ShapeDtypeStruct((rows, hid), BF16)] * 4,
        scratch_shapes=[pltpu.VMEM((rows // cap, cap, hid), F32)] * 2,
        grid=(1,),
        compiler_params=PARAMS,
        cost_estimate=LIGHT,
    )(at, *operands)


def unpinned(*args):
    return over_columns(*args, pin_out=False)


def parts_of(dg, du, wg, wu, start, columns, half, other, pieces, kernel):
    many = dg.shape[0] // NC
    each = many // pieces
    tiled = [(wg, 0, start), (wu, 0, start)]
    if other is not None:
        tiled.append((other, 1, 0))

    def compute(t, values, fixed, scalar, outs):
        here = pl.ds(half * many, many)
        total = lax.dot_general(
            fixed[0][here, :], values[0], CONTRACT_LAST, preferred_element_type=F32
        )
        total += lax.dot_general(
            fixed[1][here, :], values[1], CONTRACT_LAST, preferred_element_type=F32
        )
        if other is not None:
            total += values[2].astype(F32)
        return [total[i * each : (i + 1) * each] for i in range(pieces)]

    out = ((each, columns), BF16, 0)
    return kernel(compute, columns, tiled, [dg, du], None, [out] * pieces, [])


def sum_z(a, b):
    def compute(t, values, fixed, scalar, outs):
        return [values[0].astype(F32) + values[1].astype(F32)]

    return over_columns(
        compute, a.shape[1], [(a, 1, 0), (b, 1, 0)], [], None, [(a.shape, BF16, 0)], []
    )[0]


def finish_a(place_t, tok, start, rows):
    def compute(t, values, fixed, scalar, outs):
        branch = jnp.dot(fixed[0][...], values[1], preferred_element_type=F32).astype(BF16)
        return [values[0].astype(F32) + branch.astype(F32)]

    out = ((tok.shape[0], rows.shape[1]), BF16, 0)
    return over_columns(
        compute, rows.shape[1], [(tok, 1, start), (rows, 1, 0)], [place_t], None, [out], []
    )[0]


def combine_b(keep, send, blocks):
    columns = blocks[0].shape[1]
    tokens = keep.shape[1]

    def compute(t, values, fixed, scalar, outs):
        totals = []
        for ref in fixed:
            total = None
            for d in range(NX):
                more = jnp.dot(ref[d], values[d], preferred_element_type=F32)
                total = more if total is None else total + more
            totals.append(total)
        return totals

    outs = [((tokens, columns), F32, 0), ((tokens, columns), BF16, 0)]
    return over_columns(compute, columns, [(b, 1, 0) for b in blocks], [keep, send], None, outs, [])


def finish_b(at, own, other, tok0, start, tok1):
    columns = own.shape[1]

    def compute(t, values, fixed, scalar, outs):
        branch = (values[0] + values[1].astype(F32)).astype(BF16)
        tok = jnp.where(scalar[4] == 0, values[2].astype(F32), values[3].astype(F32))
        return [tok + branch.astype(F32)]

    tiled = [(own, 1, 0), (other, 1, 0), (tok0, 1, start), (tok1, 1, 0)]
    return over_columns(compute, columns, tiled, [], at, [(own.shape, BF16, 0)], [])[0]


def place_chunk(piece, width, start, into):
    def compute(t, values, fixed, scalar, outs):
        return values

    columns = piece.shape[1]
    out = ((piece.shape[0], width), piece.dtype, start)
    return over_columns(compute, columns, [(piece, 1, 0)], [], None, [out], [], into, False)[0]


def body(pending, expert_ids, route_weight, gate_saved, up_saved, w_gate, w_up, w_down):
    own = pending[0]
    width = own.shape[1]
    rows, hid = gate_saved.shape[1:]
    cap = rows // (NX * NZ * NC)
    w_gate, w_up, w_down = w_gate[0], w_up[0], w_down[0]
    unit = width // 28
    a0, b0, a1, b1 = EARLY[0] * unit, EARLY[1] * unit, LATE[0] * unit, LATE[1] * unit
    early = a0 + b0
    at_a0, at_b0, at_a1, at_b1 = 0, a0, early, early + a1
    tie = lax.optimization_barrier

    def crossing(s):
        return s % NY == 0

    def swapped(s):
        return s % NY == NY - 1

    tok_a0 = section_move(own[:, :a0], crossing)
    info = jnp.concatenate([expert_ids[0].astype(F32), route_weight[0]], axis=1).T
    info_far = ep_move(info, dz=1)
    tok_b0 = section_move(own[:, a0:early], crossing)
    tok1 = section_move(release(own, tok_b0)[:, early:], crossing)
    section = lax.axis_index("section").astype(jnp.int32)
    position = lax.axis_index("ep").astype(jnp.int32)
    turned = (section % NY == NY - 1).astype(jnp.int32)
    last = jnp.maximum(turned, (section % NY == 0).astype(jnp.int32))
    z = (position >> 1) & 1
    at = jnp.stack([position >> 2, jnp.where(turned == 1, 1 - z, z), position & 1, turned, last])
    info0 = jnp.where(turned == 1, info_far, info)
    info1 = jnp.where(turned == 1, info, info_far)
    place, place_t, weight, place0, weight0, place1, weight1, keep_t, send_t = route(
        at, info0, info1, cap
    )

    near_a0 = x_exchange(pack_a(place, weight, tok_a0, 0, a0))
    near_a0, far_tok0, at_later = tie((near_a0, ep_move(tok_b0, dz=1), at))
    far_a0 = ep_move(near_a0, dz=1)
    sent_b0 = pack_b(place0, weight0, place1, weight1, tok_b0, 0, far_tok0, cap)
    got_b0 = x_moves(sent_b0, 1)
    f1, f2, hid_a, hid_b = saved(at_later, gate_saved[0], up_saved[0], cap)
    hid_at = hid_a.reshape(NC * NZ, -1, hid).transpose(0, 2, 1)
    hid_bt = hid_b.reshape(NC, -1, hid).transpose(0, 2, 1)
    hid_near = jnp.stack([hid_at[0], hid_at[2], hid_at[1], hid_at[3]])
    packed_a1, tok_b1 = pack_a(place, weight, tok1, 0, a1), tok1[:, a1:]
    far_a0, got_b0, packed_a1, tok_b1, f1, f2, hid_at, hid_bt, hid_near = tie(
        (far_a0, got_b0, packed_a1, tok_b1, f1, f2, hid_at, hid_bt, hid_near)
    )
    near_a1 = x_exchange(packed_a1)
    far_tok1 = ep_move(tok_b1, dz=1)
    mine0 = join([near_a0, far_a0, sent_b0[0]] + got_b0)
    near_a1, far_tok1, mine0 = tie((near_a1, far_tok1, mine0))
    far_a1 = ep_move(near_a1, dz=1)
    sent_b1 = pack_b(place0, weight0, place1, weight1, tok_b1, 0, far_tok1, cap)
    got_b1 = x_moves(sent_b1, 1)
    many = NX * cap
    theirs0 = ep_move(mine0, dc=1)
    rows_a0 = [(mine0, (0, many)), (theirs0, (0, many)), (mine0, (many, many)), (theirs0, (many, many))]
    rows_b0 = [(mine0, (2 * many, 2 * many)), (theirs0, (2 * many, 2 * many))]
    dh_a, grad = use_rows([[g] for g in rows_a0], w_down, hid_near, None, None, at_a0, True, True)
    dh_b, grad = use_rows([[g] for g in rows_b0], w_down, hid_bt, None, grad, at_b0, True, True)
    dh_near, dh_far0, dh_far1 = dh_a[: 2 * many], dh_a[2 * many : 3 * many], dh_a[3 * many :]
    dh_b0, dh_b1 = dh_b[: 2 * many], dh_b[2 * many :]

    def more_dh(groups, dh, start):
        return use_rows(groups, w_down, None, dh, None, start, True, False, at_once)

    far_a1, got_b1, dh_near, dh_far0, dh_far1, dh_b0, dh_b1, grad = tie(
        (far_a1, got_b1, dh_near, dh_far0, dh_far1, dh_b0, dh_b1, grad)
    )
    near_a1_other, far_a1_other = ep_move(near_a1, dc=1), ep_move(far_a1, dc=1)
    mine_b1 = [sent_b1[0]] + got_b1
    theirs_b1 = [ep_move(piece, dc=1) for piece in mine_b1]
    dh_b0 = more_dh([mine_b1], dh_b0, at_b1)
    dh_far0 = more_dh([[far_a1]], dh_far0, at_a1)
    dh_near = more_dh([[near_a1], [near_a1_other]], dh_near, at_a1)
    dh_b1 = more_dh([theirs_b1], dh_b1, at_b1)
    dh_far1 = more_dh([[far_a1_other]], dh_far1, at_a1)
    rows_a1 = [[near_a1], [far_a1], [near_a1_other], [far_a1_other]]
    rows_b1 = [mine_b1, theirs_b1]

    grads = activations(at, [dh_near, dh_far0, dh_far1, dh_b0, dh_b1], f1, f2, cap)

    def parts(kind, low, n, other, pieces, kernel, grads):
        dg, du = grads[:2] if kind == "A" else grads[2:]
        half = 1 if other is None else 0
        return parts_of(dg, du, w_gate, w_up, low, n, half, other, pieces, kernel)

    core_b1 = ep_move(parts("B", at_b1, b1, None, 1, at_once, grads)[0], dc=1)
    core_a1 = ep_move(parts("A", at_a1, a1, None, 1, at_once, grads)[0], dc=1)
    part_b1 = parts("B", at_b1, b1, core_b1, NX, at_once, grads)
    back_b1 = x_moves(part_b1, -1)
    keep_a1, send_a1 = parts("A", at_a1, a1, core_a1, NZ, at_once, grads)
    back_a1 = ep_move(send_a1, dz=1)
    grads = release(grads, part_b1, send_a1)
    core_b0 = ep_move(parts("B", at_b0, b0, None, 1, at_once, grads)[0], dc=1)
    core_a0 = ep_move(parts("A", at_a0, a0, None, 1, at_once, grads)[0], dc=1)
    part_b0 = parts("B", at_b0, b0, core_b0, NX, unpinned, grads)
    keep_a0, send_a0 = parts("A", at_a0, a0, core_a0, NZ, over_columns, grads)
    grad = use_rows(rows_a1, w_down, hid_at, None, release(grad, grads), at_a1, False, True)
    grad = use_rows(rows_b1, w_down, hid_bt, None, grad, at_b1, False, True)
    back_b1, back_a1, part_b0, keep_a0, send_a0, grad = tie(
        (back_b1, back_a1, part_b0, keep_a0, send_a0, grad)
    )
    keep_b1, send_b1 = combine_b(keep_t, send_t, [part_b1[0]] + back_b1)
    cross_b1 = ep_move(send_b1, dz=1)
    back_b0 = x_moves(part_b0, -1)
    back_a0 = ep_move(release(send_a0, cross_b1), dz=1)
    cross_b1, back_b0, back_a1 = tie((cross_b1, back_b0, back_a1))
    up_b1 = section_move(finish_b(at, keep_b1, cross_b1, tok_b1, 0, far_tok1), crossing)
    own_a1 = x_exchange(sum_z(keep_a1, back_a1))
    keep_b0, send_b0 = combine_b(keep_t, send_t, [part_b0[0]] + back_b0)
    cross_b0 = ep_move(send_b0, dz=1)
    own_a1, cross_b0, back_a0, up_b1 = tie((own_a1, cross_b0, back_a0, up_b1))
    own_a0 = x_exchange(sum_z(keep_a0, back_a0))
    up_a1 = section_move(finish_a(place_t, tok1, 0, own_a1), swapped)
    up_b0 = section_move(finish_b(at, keep_b0, cross_b0, tok_b0, 0, far_tok0), crossing)
    up_a0 = section_move(finish_a(place_t, tok_a0, 0, own_a0), swapped)
    out = place_chunk(up_b1, width, at_b1, None)
    out = place_chunk(up_a1, width, at_a1, out)
    out = place_chunk(up_b0, width, at_b0, out)
    out = place_chunk(up_a0, width, at_a0, out)
    return (out[None], grad[None])


def solution(mesh):
    placed = (
        P("section", "ep", None),
        P("section", "ep", None),
        P("section", "ep", None),
        P("section", None, "ep"),
        P("section", None, "ep"),
        P("section", None, "ep"),
        P("section", None, "ep"),
        P("section", "ep", None),
    )
    return jax.shard_map(
        body,
        mesh=mesh,
        in_specs=placed,
        out_specs=(P("section", "ep", None), P("section", "ep", None)),
        check_vma=False,
    )
```

```python
import functools

import jax
import jax.numpy as jnp
from jax import lax
from jax.experimental import pallas as pl
from jax.experimental.pallas import tpu as pltpu
from jax.sharding import PartitionSpec as P

NX, NZ, NC, NY = 4, 2, 2, 4
F32, BF16 = jnp.float32, jnp.bfloat16
PARAMS = pltpu.CompilerParams(vmem_limit_bytes=32 << 20)
LIGHT = pl.CostEstimate(flops=1, bytes_accessed=1, transcendentals=0)
EARLY, LATE = (5, 5), (9, 9)
CONTRACT_LAST = (((1,), (1,)), ((), ()))


def section_move(array, flip):
    sections, peers = lax.axis_size("section"), NX * NZ * NC
    pairs = []
    for s in range(sections):
        for q in range(peers):
            to = q ^ NC if flip(s) else q
            pairs.append((s * peers + q, (s - 1) % sections * peers + to))
    return lax.ppermute(array, ("section", "ep"), pairs)


def ep_move(array, dx=0, dz=0, dc=0):
    pairs = []
    for q in range(NX * NZ * NC):
        x, z, c = q // (NZ * NC), q // NC % NZ, q % NC
        pairs.append((q, (x + dx) % NX * NZ * NC + (z ^ dz) * NC + (c ^ dc)))
    return lax.ppermute(array, "ep", pairs)


def x_moves(blocks, sign):
    return [ep_move(blocks[d], dx=sign * d) for d in range(1, NX)]


def x_exchange(array):
    groups = [[x * NZ * NC + i for x in range(NX)] for i in range(NZ * NC)]
    blocks = array.reshape(NX, -1, array.shape[1])
    moved = lax.all_to_all(blocks, "ep", 0, 0, axis_index_groups=groups, tiled=True)
    return moved.reshape(array.shape)


def whole(shape):
    return pl.BlockSpec(shape, lambda *_: (0,) * len(shape))


def in_hbm(array):
    return pltpu.with_memory_space_constraint(array, pltpu.HBM)


def tile_of(columns):
    return max(t for t in range(128, 897, 128) if columns % t == 0)


def release(value, *after):
    return lax.optimization_barrier((value, after))[0]


def at_once(compute, columns, tiled, fixed, scalars, tiled_out, fixed_out):
    n_in, n_fix, n_out = len(tiled), len(fixed), len(tiled_out)

    def kernel(*refs):
        ins, fixes, outs = refs[:n_in], refs[n_in : n_in + n_fix], refs[n_in + n_fix :]
        results = compute(0, [r[...] for r in ins], fixes, None, outs[n_out:])
        for ref, value in zip(outs, results):
            ref[...] = value.astype(ref.dtype)

    operands, specs = [], []
    for array, axis, start in tiled:
        operands.append(array)
        if array.shape[axis] == columns:
            specs.append(whole(array.shape))
            continue
        shape = list(array.shape)
        shape[axis] = columns
        at = (0, start) if axis == 1 else (start, 0)
        specs.append(pl.BlockSpec(tuple(pl.Element(n) for n in shape), lambda *_, at=at: at))
    for array in fixed:
        operands.append(array)
        specs.append(whole(array.shape))
    shapes = [(shape, dtype) for shape, dtype, *_ in tiled_out] + list(fixed_out)
    return pl.pallas_call(
        kernel,
        in_specs=specs,
        out_specs=[whole(shape) for shape, _ in shapes],
        out_shape=[jax.ShapeDtypeStruct(shape, dtype) for shape, dtype in shapes],
        grid=(1,),
        compiler_params=PARAMS,
        cost_estimate=LIGHT,
    )(*operands)


def over_columns(
    compute, columns, tiled, fixed, scalars, tiled_out, fixed_out, into=None, pin=True,
    pin_out=True,
):
    row_windows = [entry[3] if len(entry) > 3 else None for entry in tiled]
    tiled = [entry[:3] for entry in tiled]
    tile = tile_of(columns)
    steps = columns // tile
    n_in, n_fix, n_out = len(tiled), len(fixed), len(tiled_out)

    def kernel(*refs):
        refs = list(refs)
        take = lambda n: [refs.pop(0) for _ in range(n)]
        ins, fixes = take(n_in), take(n_fix)
        scalar = take(1)[0] if scalars is not None else None
        if into is not None:
            take(1)
        outs, fix_outs = take(n_out), take(len(fixed_out))
        in_bufs, out_bufs, fix_bufs = take(n_in), take(n_out), take(n_fix)
        in_sems, out_sems, fix_sems = take(3)

        def window(ref, axis, start, t, rows=None):
            here = pl.ds(pl.multiple_of(start + t * tile, 128), tile)
            if rows is not None:
                return ref.at[pl.ds(*rows), here]
            return ref.at[:, here] if axis == 1 else ref.at[here, :]

        def loads(t):
            return [
                pltpu.make_async_copy(
                    window(ins[i], axis, start, t, row_windows[i]),
                    window(in_bufs[i], axis, 0, t),
                    in_sems.at[i * steps + t],
                )
                for i, (_, axis, start) in enumerate(tiled)
            ]

        def stores(t):
            return [
                pltpu.make_async_copy(
                    window(out_bufs[i], 1, 0, t),
                    window(outs[i], 1, tiled_out[i][2], t),
                    out_sems.at[i * steps + t],
                )
                for i in range(n_out)
            ]

        whole_loads = [
            pltpu.make_async_copy(fixes[i], fix_bufs[i], fix_sems.at[i]) for i in range(n_fix)
        ]
        for copy in whole_loads:
            copy.start()
        for t in range(steps):
            for copy in loads(t):
                copy.start()
        for copy in whole_loads:
            copy.wait()

        def step(t):
            for copy in loads(t):
                copy.wait()
            values = [
                window(in_bufs[i], axis, 0, t)[...] for i, (_, axis, _) in enumerate(tiled)
            ]
            results = compute(t, values, fix_bufs, scalar, fix_outs)
            for i, value in enumerate(results):
                window(out_bufs[i], 1, 0, t)[...] = value.astype(out_bufs[i].dtype)
            for copy in stores(t):
                copy.start()

        if fixed_out:
            for t in range(steps):
                step(t)
        else:
            pl.loop(0, steps)(step)
        for t in range(steps):
            for copy in stores(t):
                copy.wait()

    hbm = pl.BlockSpec(memory_space=pl.ANY)
    operands = [in_hbm(a) if pin else a for a in [a for a, _, _ in tiled] + list(fixed)]
    specs = [hbm] * (n_in + n_fix)
    if scalars is not None:
        operands.append(scalars)
        specs.append(pl.BlockSpec(memory_space=pltpu.SMEM))
    aliases = {}
    if into is not None:
        aliases[len(operands)] = 0
        operands.append(in_hbm(into))
        specs.append(hbm)
    buffers = [
        pltpu.VMEM(
            (r[1] if r else a.shape[0], columns) if axis == 1 else (columns, a.shape[1]), a.dtype
        )
        for (a, axis, _), r in zip(tiled, row_windows)
    ] + [pltpu.VMEM((shape[0], columns), dtype) for shape, dtype, _ in tiled_out]
    buffers += [pltpu.VMEM(a.shape, a.dtype) for a in fixed]
    return pl.pallas_call(
        kernel,
        in_specs=specs,
        out_specs=[hbm] * n_out + [pl.BlockSpec(memory_space=pltpu.VMEM)] * len(fixed_out),
        out_shape=[
            (pltpu.HBM if pin_out else jax.ShapeDtypeStruct)(shape, dtype)
            for shape, dtype, _ in tiled_out
        ]
        + [jax.ShapeDtypeStruct(shape, dtype) for shape, dtype in fixed_out],
        scratch_shapes=buffers
        + [
            pltpu.SemaphoreType.DMA((max(1, n_in * steps),)),
            pltpu.SemaphoreType.DMA((max(1, n_out * steps),)),
            pltpu.SemaphoreType.DMA((max(1, n_fix),)),
        ],
        input_output_aliases=aliases,
        compiler_params=PARAMS,
        cost_estimate=LIGHT,
    )(*operands)


def tables_of(cap, info_ref, first_x):
    tokens = info_ref.shape[1]
    row = lax.broadcasted_iota(jnp.int32, (tokens, tokens), 0)
    col = lax.broadcasted_iota(jnp.int32, (tokens, tokens), 1)
    before = (row < col).astype(F32).astype(BF16)
    slot_of = lax.broadcasted_iota(jnp.int32, (cap, tokens), 0).astype(F32)
    places, weights = [], []
    for d in range(NX):
        expert = lax.rem(first_x + d, NX).astype(F32)
        first = info_ref[0:1, :] == expert
        second = info_ref[1:2, :] == expert
        named = jnp.where(first | second, 1.0, 0.0)
        prob = jnp.where(first, info_ref[2:3, :], jnp.where(second, info_ref[3:4, :], 0.0))
        rank = jnp.dot(
            jnp.broadcast_to(named, (8, tokens)).astype(BF16), before, preferred_element_type=F32
        )[0:1]
        placed = jnp.where((slot_of == rank) & (named > 0.0), 1.0, 0.0)
        places.append(placed)
        weights.append(
            jnp.broadcast_to(jnp.sum(placed * prob, axis=1, keepdims=True), (cap, 128))
        )
    return places, weights


def transposed(block):
    tokens = block.shape[1]
    row = lax.broadcasted_iota(jnp.int32, (tokens, tokens), 0)
    col = lax.broadcasted_iota(jnp.int32, (tokens, tokens), 1)
    eye = (row == col).astype(F32).astype(BF16)
    return lax.dot_general(eye, block.astype(BF16), CONTRACT_LAST, preferred_element_type=F32)


def route_kernel(
    cap, at_ref, info0_ref, info1_ref, pa_ref, pat_ref, wa_ref, p0_ref, w0_ref, p1_ref, w1_ref,
    keep_ref, send_ref,
):
    x, last = at_ref[0], at_ref[4].astype(F32)
    places, weights = tables_of(cap, info0_ref, jnp.int32(0))
    pa_ref[...] = jnp.concatenate(places, axis=0).astype(BF16)
    pat_ref[...] = transposed(jnp.concatenate(places, axis=0)).astype(BF16)
    wa_ref[...] = jnp.concatenate(weights, axis=0)
    places0, weights0 = tables_of(cap, info0_ref, x)
    places1, weights1 = tables_of(cap, info1_ref, x)
    p0_ref[...] = jnp.concatenate(places0, axis=0).astype(BF16)
    w0_ref[...] = jnp.concatenate(weights0, axis=0)
    p1_ref[...] = jnp.concatenate(places1, axis=0).astype(BF16)
    w1_ref[...] = jnp.concatenate(weights1, axis=0)
    for d in range(NX):
        keep = jnp.concatenate([places0[d] * (1.0 - last), places1[d] * last], axis=0)
        send = jnp.concatenate([places0[d] * last, places1[d] * (1.0 - last)], axis=0)
        keep_ref[d] = transposed(keep).astype(BF16)
        send_ref[d] = transposed(send).astype(BF16)


def route(at, info0, info1, cap):
    tokens = info0.shape[1]
    slots = NX * cap
    place, weight = (slots, tokens), (slots, 128)
    back = (NX, tokens, NZ * cap)
    shapes = [(place, BF16), ((tokens, slots), BF16), (weight, F32), (place, BF16), (weight, F32)]
    shapes += [(place, BF16), (weight, F32), (back, BF16), (back, BF16)]
    return pl.pallas_call(
        functools.partial(route_kernel, cap),
        in_specs=[pl.BlockSpec(memory_space=pltpu.SMEM), whole(info0.shape), whole(info1.shape)],
        out_specs=[whole(s) for s, _ in shapes],
        out_shape=[pltpu.HBM(s, t) for s, t in shapes],
        grid=(1,),
        compiler_params=PARAMS,
        cost_estimate=LIGHT,
    )(at, info0, info1)


def saved_kernel(cap, at_ref, gate_ref, up_ref, f1_ref, f2_ref, ha_ref, hb_ref, g3, u3, h3, k3):
    g3[...] = gate_ref[...].astype(F32).reshape(g3.shape)
    u3[...] = up_ref[...].astype(F32).reshape(u3.shape)
    z, c = at_ref[1], at_ref[2]
    for cr in range(NC):
        for zr in range(NZ):
            for xs in range(NX):
                j = (cr * NZ + zr) * NX + xs
                zs = z if zr == 0 else 1 - z
                cs = c if cr == 0 else 1 - c
                q = xs * (NZ * NC) + zs * NC + cs
                gate, upval = g3[q], u3[q]
                sig = jax.nn.sigmoid(gate)
                f1_ref[pl.ds(j * cap, cap), :] = upval * sig * (1.0 + gate * (1.0 - sig))
                f2_ref[pl.ds(j * cap, cap), :] = gate * sig
                h3[j] = gate * sig * upval
    ha_ref[...] = h3[...].reshape(ha_ref.shape).astype(BF16)
    a_to_b(at_ref[0], h3, k3)
    hb_ref[...] = k3[...].reshape(hb_ref.shape).astype(BF16)


def pairs_of_blocks(x):
    for cr in range(NC):
        for zr in range(NZ):
            for d in range(NX):
                yield (cr * NZ + zr) * NX + lax.rem(x + NX - d, NX), (cr * NX + d) * NZ + zr


def a_to_b(x, a3, b3):
    for ja, jb in pairs_of_blocks(x):
        b3[jb] = a3[ja]


def saved(at, gate, up, cap):
    rows, hid = gate.shape
    blocks = rows // cap
    return pl.pallas_call(
        functools.partial(saved_kernel, cap),
        in_specs=[pl.BlockSpec(memory_space=pltpu.SMEM), whole(gate.shape), whole(up.shape)],
        out_specs=[whole((rows, hid))] * 4,
        out_shape=[jax.ShapeDtypeStruct((rows, hid), t) for t in (F32, F32, BF16, BF16)],
        scratch_shapes=[pltpu.VMEM((blocks, cap, hid), F32)] * 4,
        grid=(1,),
        compiler_params=PARAMS,
        cost_estimate=LIGHT,
    )(at, gate, up)


def pack_a(place, weight, tok, start, columns):
    def compute(t, values, fixed, scalar, outs):
        rows = jnp.dot(fixed[0][...], values[0], preferred_element_type=F32)
        return [rows * fixed[1][:, 0:1]]

    out = ((place.shape[0], columns), BF16, 0)
    return over_columns(
        compute, columns, [(tok, 1, start)], [place, weight], None, [out], [], pin_out=False
    )[0]


def pack_b(place0, weight0, place1, weight1, tok0, start, tok1, cap):
    columns = tok1.shape[1]

    def compute(t, values, fixed, scalar, outs):
        rows0 = jnp.dot(fixed[0][...], values[0], preferred_element_type=F32) * fixed[1][:, 0:1]
        rows1 = jnp.dot(fixed[2][...], values[1], preferred_element_type=F32) * fixed[3][:, 0:1]
        cut = [slice(d * cap, (d + 1) * cap) for d in range(NX)]
        return [jnp.concatenate([rows0[i], rows1[i]], axis=0) for i in cut]

    out = ((NZ * cap, columns), BF16, 0)
    return over_columns(
        compute, columns, [(tok0, 1, start), (tok1, 1, 0)], [place0, weight0, place1, weight1],
        None, [out] * NX, [], pin_out=False,
    )


def use_rows(groups, w_down, hid_t, dh, grad, start, want_sum, want_grad, kernel=over_columns):
    hid, width = w_down.shape
    groups = [[e if isinstance(e, tuple) else (e, None) for e in g] for g in groups]
    columns = groups[0][0][0].shape[1]
    lengths = [sum(r[1] if r else a.shape[0] for a, r in g) for g in groups]
    rows = sum(lengths)
    tiled = [(a, 1, 0, r) if r else (a, 1, 0) for g in groups for a, r in g]
    fixed = []
    if want_sum:
        tiled.append((w_down, 1, start))
        if dh is not None:
            fixed.append(dh)
    if want_grad:
        fixed.append(hid_t)

    def compute(t, values, fixed_refs, scalar, outs):
        values, refs = list(values), list(fixed_refs)
        blocks = []
        for g in groups:
            parts = [values.pop(0) for _ in g]
            blocks.append(parts[0] if len(parts) == 1 else jnp.concatenate(parts, axis=0))
        if want_sum:
            before = refs.pop(0) if dh is not None else None
            low = 0
            for block, many in zip(blocks, lengths):
                here = pl.ds(low, many)
                more = lax.dot_general(block, values[0], CONTRACT_LAST, preferred_element_type=F32)
                if t > 0:
                    more += outs[0][here, :]
                elif before is not None:
                    more += before[here, :]
                outs[0][here, :] = more
                low += many
        if not want_grad:
            return []
        total = None
        for i, block in enumerate(blocks):
            more = jnp.dot(refs[0][i], block, preferred_element_type=F32)
            total = more if total is None else total + more
        return [total]

    sums = [((rows, hid), F32)] if want_sum else []
    if not want_grad:
        return kernel(compute, columns, tiled, fixed, None, [], sums)[0]
    done = over_columns(
        compute, columns, tiled, fixed, None, [((hid, width), F32, start)], sums, grad
    )
    return (done[1], done[0]) if want_sum else done[0]


def join(blocks):
    rows, columns = sum(b.shape[0] for b in blocks), blocks[0].shape[1]

    def compute(t, values, fixed, scalar, outs):
        return [jnp.concatenate(values, axis=0)]

    out = ((rows, columns), blocks[0].dtype, 0)
    return over_columns(compute, columns, [(b, 1, 0) for b in blocks], [], None, [out], [])[0]


def act_kernel(
    at_ref, near_ref, far0_ref, far1_ref, b0_ref, b1_ref, f1_ref, f2_ref,
    ga_ref, ua_ref, gb_ref, ub_ref, one, two,
):
    x = at_ref[0]
    half = two.shape[0] // NC
    two[pl.ds(0, half)] = b0_ref[...].reshape((half,) + two.shape[1:])
    two[pl.ds(half, half)] = b1_ref[...].reshape((half,) + two.shape[1:])
    for ja, jb in pairs_of_blocks(x):
        one[ja] = two[jb]
    many = far0_ref.shape[0]
    dh = jnp.concatenate(
        [near_ref[pl.ds(0, many), :], far0_ref[...], near_ref[pl.ds(many, many), :], far1_ref[...]],
        axis=0,
    ) + one[...].reshape(f1_ref.shape)
    dgate = dh * f1_ref[...]
    dup = dh * f2_ref[...]
    ga_ref[...] = dgate.astype(BF16)
    ua_ref[...] = dup.astype(BF16)
    for value, out_ref in ((dgate, gb_ref), (dup, ub_ref)):
        one[...] = value.reshape(one.shape)
        a_to_b(x, one, two)
        out_ref[...] = two[...].reshape(out_ref.shape).astype(BF16)


def activations(at, dhs, f1, f2, cap):
    rows, hid = f1.shape
    operands = list(dhs) + [f1, f2]
    return pl.pallas_call(
        act_kernel,
        in_specs=[pl.BlockSpec(memory_space=pltpu.SMEM)] + [whole(a.shape) for a in operands],
        out_specs=[whole((rows, hid))] * 4,
        out_shape=[jax.ShapeDtypeStruct((rows, hid), BF16)] * 4,
        scratch_shapes=[pltpu.VMEM((rows // cap, cap, hid), F32)] * 2,
        grid=(1,),
        compiler_params=PARAMS,
        cost_estimate=LIGHT,
    )(at, *operands)


def unpinned(*args):
    return over_columns(*args, pin_out=False)


def parts_of(dg, du, wg, wu, start, columns, half, other, pieces, kernel):
    many = dg.shape[0] // NC
    each = many // pieces
    tiled = [(wg, 0, start), (wu, 0, start)]
    if other is not None:
        tiled.append((other, 1, 0))

    def compute(t, values, fixed, scalar, outs):
        here = pl.ds(half * many, many)
        total = lax.dot_general(
            fixed[0][here, :], values[0], CONTRACT_LAST, preferred_element_type=F32
        )
        total += lax.dot_general(
            fixed[1][here, :], values[1], CONTRACT_LAST, preferred_element_type=F32
        )
        if other is not None:
            total += values[2].astype(F32)
        return [total[i * each : (i + 1) * each] for i in range(pieces)]

    out = ((each, columns), BF16, 0)
    return kernel(compute, columns, tiled, [dg, du], None, [out] * pieces, [])


def sum_z(a, b):
    def compute(t, values, fixed, scalar, outs):
        return [values[0].astype(F32) + values[1].astype(F32)]

    return over_columns(
        compute, a.shape[1], [(a, 1, 0), (b, 1, 0)], [], None, [(a.shape, BF16, 0)], []
    )[0]


def finish_a(place_t, tok, start, rows):
    def compute(t, values, fixed, scalar, outs):
        branch = jnp.dot(fixed[0][...], values[1], preferred_element_type=F32).astype(BF16)
        return [values[0].astype(F32) + branch.astype(F32)]

    out = ((tok.shape[0], rows.shape[1]), BF16, 0)
    return over_columns(
        compute, rows.shape[1], [(tok, 1, start), (rows, 1, 0)], [place_t], None, [out], []
    )[0]


def combine_b(keep, send, blocks):
    columns = blocks[0].shape[1]
    tokens = keep.shape[1]

    def compute(t, values, fixed, scalar, outs):
        totals = []
        for ref in fixed:
            total = None
            for d in range(NX):
                more = jnp.dot(ref[d], values[d], preferred_element_type=F32)
                total = more if total is None else total + more
            totals.append(total)
        return totals

    outs = [((tokens, columns), F32, 0), ((tokens, columns), BF16, 0)]
    return over_columns(compute, columns, [(b, 1, 0) for b in blocks], [keep, send], None, outs, [])


def finish_b(at, own, other, tok0, start, tok1):
    columns = own.shape[1]

    def compute(t, values, fixed, scalar, outs):
        branch = (values[0] + values[1].astype(F32)).astype(BF16)
        tok = jnp.where(scalar[4] == 0, values[2].astype(F32), values[3].astype(F32))
        return [tok + branch.astype(F32)]

    tiled = [(own, 1, 0), (other, 1, 0), (tok0, 1, start), (tok1, 1, 0)]
    return over_columns(compute, columns, tiled, [], at, [(own.shape, BF16, 0)], [])[0]


def place_chunk(piece, width, start, into):
    def compute(t, values, fixed, scalar, outs):
        return values

    columns = piece.shape[1]
    out = ((piece.shape[0], width), piece.dtype, start)
    return over_columns(compute, columns, [(piece, 1, 0)], [], None, [out], [], into, False)[0]


def body(pending, expert_ids, route_weight, gate_saved, up_saved, w_gate, w_up, w_down):
    own = pending[0]
    width = own.shape[1]
    rows, hid = gate_saved.shape[1:]
    cap = rows // (NX * NZ * NC)
    w_gate, w_up, w_down = w_gate[0], w_up[0], w_down[0]
    unit = width // 28
    a0, b0, a1, b1 = EARLY[0] * unit, EARLY[1] * unit, LATE[0] * unit, LATE[1] * unit
    early = a0 + b0
    at_a0, at_b0, at_a1, at_b1 = 0, a0, early, early + a1
    tie = lax.optimization_barrier

    def crossing(s):
        return s % NY == 0

    def swapped(s):
        return s % NY == NY - 1

    tok_a0 = section_move(own[:, :a0], crossing)
    own_b0 = own[:, a0:early]
    next_b0 = ep_move(own_b0, dz=1)
    info = jnp.concatenate([expert_ids[0].astype(F32), route_weight[0]], axis=1).T
    info_far = ep_move(info, dz=1)
    tok_b0 = section_move(release(own_b0, tok_a0), crossing)
    far_tok0 = section_move(next_b0, crossing)
    own_late = release(own, tok_b0)
    tok_a1 = section_move(own_late[:, early : early + a1], crossing)
    tok_b1 = section_move(release(own_late, tok_a1)[:, early + a1 :], crossing)
    section = lax.axis_index("section").astype(jnp.int32)
    position = lax.axis_index("ep").astype(jnp.int32)
    turned = (section % NY == NY - 1).astype(jnp.int32)
    last = jnp.maximum(turned, (section % NY == 0).astype(jnp.int32))
    z = (position >> 1) & 1
    at = jnp.stack([position >> 2, jnp.where(turned == 1, 1 - z, z), position & 1, turned, last])
    info0 = jnp.where(turned == 1, info_far, info)
    info1 = jnp.where(turned == 1, info, info_far)
    place, place_t, weight, place0, weight0, place1, weight1, keep_t, send_t = route(
        at, info0, info1, cap
    )

    near_a0 = x_exchange(pack_a(place, weight, tok_a0, 0, a0))
    near_a0, tok_b0, far_tok0, at_later = tie((near_a0, tok_b0, far_tok0, at))
    far_a0 = ep_move(near_a0, dz=1)
    sent_b0 = pack_b(place0, weight0, place1, weight1, tok_b0, 0, far_tok0, cap)
    got_b0 = x_moves(sent_b0, 1)
    f1, f2, hid_a, hid_b = saved(release(at_later, sent_b0), gate_saved[0], up_saved[0], cap)
    hid_at = hid_a.reshape(NC * NZ, -1, hid).transpose(0, 2, 1)
    hid_bt = hid_b.reshape(NC, -1, hid).transpose(0, 2, 1)
    hid_near = jnp.stack([hid_at[0], hid_at[2], hid_at[1], hid_at[3]])
    packed_a1 = pack_a(place, weight, tok_a1, 0, a1)
    far_a0, got_b0, packed_a1, f1, f2, hid_at, hid_bt, hid_near = tie(
        (far_a0, got_b0, packed_a1, f1, f2, hid_at, hid_bt, hid_near)
    )
    near_a1 = x_exchange(packed_a1)
    far_tok1 = ep_move(tok_b1, dz=1)
    mine0 = join([near_a0, far_a0, sent_b0[0]] + got_b0)
    near_a1, far_tok1, mine0 = tie((near_a1, far_tok1, mine0))
    far_a1 = ep_move(near_a1, dz=1)
    sent_b1 = pack_b(place0, weight0, place1, weight1, tok_b1, 0, far_tok1, cap)
    got_b1 = x_moves(sent_b1, 1)
    many = NX * cap
    theirs0 = ep_move(mine0, dc=1)
    rows_a0 = [(mine0, (0, many)), (theirs0, (0, many)), (mine0, (many, many)), (theirs0, (many, many))]
    rows_b0 = [(mine0, (2 * many, 2 * many)), (theirs0, (2 * many, 2 * many))]
    dh_a, grad = use_rows([[g] for g in rows_a0], w_down, hid_near, None, None, at_a0, True, True)
    dh_b, grad = use_rows([[g] for g in rows_b0], w_down, hid_bt, None, grad, at_b0, True, True)
    dh_near, dh_far0, dh_far1 = dh_a[: 2 * many], dh_a[2 * many : 3 * many], dh_a[3 * many :]
    dh_b0, dh_b1 = dh_b[: 2 * many], dh_b[2 * many :]

    def more_dh(groups, dh, start):
        return use_rows(groups, w_down, None, dh, None, start, True, False, at_once)

    far_a1, got_b1, dh_near, dh_far0, dh_far1, dh_b0, dh_b1, grad = tie(
        (far_a1, got_b1, dh_near, dh_far0, dh_far1, dh_b0, dh_b1, grad)
    )
    near_a1_other, far_a1_other = ep_move(near_a1, dc=1), ep_move(far_a1, dc=1)
    mine_b1 = [sent_b1[0]] + got_b1
    theirs_b1 = [ep_move(piece, dc=1) for piece in mine_b1]
    dh_b0 = more_dh([mine_b1], dh_b0, at_b1)
    dh_far0 = more_dh([[far_a1]], dh_far0, at_a1)
    dh_near = more_dh([[near_a1], [near_a1_other]], dh_near, at_a1)
    dh_b1 = more_dh([theirs_b1], dh_b1, at_b1)
    dh_far1 = more_dh([[far_a1_other]], dh_far1, at_a1)
    rows_a1 = [[near_a1], [far_a1], [near_a1_other], [far_a1_other]]
    rows_b1 = [mine_b1, theirs_b1]

    grads = activations(at, [dh_near, dh_far0, dh_far1, dh_b0, dh_b1], f1, f2, cap)

    def parts(kind, low, n, other, pieces, kernel, grads):
        dg, du = grads[:2] if kind == "A" else grads[2:]
        half = 1 if other is None else 0
        return parts_of(dg, du, w_gate, w_up, low, n, half, other, pieces, kernel)

    core_b1 = ep_move(parts("B", at_b1, b1, None, 1, at_once, grads)[0], dc=1)
    core_a1 = ep_move(parts("A", at_a1, a1, None, 1, at_once, grads)[0], dc=1)
    part_b1 = parts("B", at_b1, b1, core_b1, NX, at_once, grads)
    back_b1 = x_moves(part_b1, -1)
    keep_a1, send_a1 = parts("A", at_a1, a1, core_a1, NZ, at_once, grads)
    back_a1 = ep_move(send_a1, dz=1)
    core_b0 = ep_move(parts("B", at_b0, b0, None, 1, at_once, grads)[0], dc=1)
    core_a0 = ep_move(parts("A", at_a0, a0, None, 1, at_once, grads)[0], dc=1)
    grads = release(grads, part_b1, send_a1)
    part_b0 = parts("B", at_b0, b0, core_b0, NX, unpinned, grads)
    keep_a0, send_a0 = parts("A", at_a0, a0, core_a0, NZ, over_columns, grads)
    grad = use_rows(rows_a1, w_down, hid_at, None, release(grad, grads), at_a1, False, True)
    grad = use_rows(rows_b1, w_down, hid_bt, None, grad, at_b1, False, True)
    back_b1, back_a1, part_b0, keep_a0, send_a0, grad = tie(
        (back_b1, back_a1, part_b0, keep_a0, send_a0, grad)
    )
    back_b0 = x_moves(part_b0, -1)
    back_a0 = ep_move(send_a0, dz=1)
    keep_b1, send_b1 = combine_b(keep_t, send_t, [part_b1[0]] + back_b1)
    cross_b1 = ep_move(send_b1, dz=1)
    cross_b1, back_b0, back_a0, back_a1 = tie((cross_b1, back_b0, back_a0, back_a1))
    own_a1 = x_exchange(sum_z(keep_a1, back_a1))
    up_b1 = section_move(finish_b(at, keep_b1, cross_b1, tok_b1, 0, far_tok1), crossing)
    keep_b0, send_b0 = combine_b(keep_t, send_t, [part_b0[0]] + back_b0)
    cross_b0 = ep_move(send_b0, dz=1)
    sum_a0 = sum_z(keep_a0, back_a0)
    own_a1, cross_b0, sum_a0, up_b1 = tie((own_a1, cross_b0, sum_a0, up_b1))
    own_a0 = x_exchange(sum_a0)
    up_a1 = section_move(finish_a(place_t, tok_a1, 0, own_a1), swapped)
    up_b0 = section_move(finish_b(at, keep_b0, cross_b0, tok_b0, 0, far_tok0), crossing)
    up_a0 = section_move(finish_a(place_t, tok_a0, 0, own_a0), swapped)
    out = place_chunk(up_b1, width, at_b1, None)
    out = place_chunk(up_a1, width, at_a1, out)
    out = place_chunk(up_b0, width, at_b0, out)
    out = place_chunk(up_a0, width, at_a0, out)
    return (out[None], grad[None])


def solution(mesh):
    placed = (
        P("section", "ep", None),
        P("section", "ep", None),
        P("section", "ep", None),
        P("section", None, "ep"),
        P("section", None, "ep"),
        P("section", None, "ep"),
        P("section", None, "ep"),
        P("section", "ep", None),
    )
    return jax.shard_map(
        body,
        mesh=mesh,
        in_specs=placed,
        out_specs=(P("section", "ep", None), P("section", "ep", None)),
        check_vma=False,
    )
```

```python
import functools

import jax
import jax.numpy as jnp
from jax import lax
from jax.experimental import pallas as pl
from jax.experimental.pallas import tpu as pltpu
from jax.sharding import PartitionSpec as P

NX, NZ, NC, NY = 4, 2, 2, 4
F32, BF16 = jnp.float32, jnp.bfloat16
PARAMS = pltpu.CompilerParams(vmem_limit_bytes=32 << 20)
LIGHT = pl.CostEstimate(flops=1, bytes_accessed=1, transcendentals=0)
EARLY, LATE = (5, 5), (10, 8)
CONTRACT_LAST = (((1,), (1,)), ((), ()))


def section_move(array, flip):
    sections, peers = lax.axis_size("section"), NX * NZ * NC
    pairs = []
    for s in range(sections):
        for q in range(peers):
            to = q ^ NC if flip(s) else q
            pairs.append((s * peers + q, (s - 1) % sections * peers + to))
    return lax.ppermute(array, ("section", "ep"), pairs)


def ep_move(array, dx=0, dz=0, dc=0):
    pairs = []
    for q in range(NX * NZ * NC):
        x, z, c = q // (NZ * NC), q // NC % NZ, q % NC
        pairs.append((q, (x + dx) % NX * NZ * NC + (z ^ dz) * NC + (c ^ dc)))
    return lax.ppermute(array, "ep", pairs)


def x_moves(blocks, sign):
    return [ep_move(blocks[d], dx=sign * d) for d in range(1, NX)]


def x_exchange(array):
    groups = [[x * NZ * NC + i for x in range(NX)] for i in range(NZ * NC)]
    blocks = array.reshape(NX, -1, array.shape[1])
    moved = lax.all_to_all(blocks, "ep", 0, 0, axis_index_groups=groups, tiled=True)
    return moved.reshape(array.shape)


def whole(shape):
    return pl.BlockSpec(shape, lambda *_: (0,) * len(shape))


def in_hbm(array):
    return pltpu.with_memory_space_constraint(array, pltpu.HBM)


def tile_of(columns):
    return max(t for t in range(128, 897, 128) if columns % t == 0)


def release(value, *after):
    return lax.optimization_barrier((value, after))[0]


def at_once(compute, columns, tiled, fixed, scalars, tiled_out, fixed_out):
    n_in, n_fix, n_out = len(tiled), len(fixed), len(tiled_out)

    def kernel(*refs):
        ins, fixes, outs = refs[:n_in], refs[n_in : n_in + n_fix], refs[n_in + n_fix :]
        results = compute(0, [r[...] for r in ins], fixes, None, outs[n_out:])
        for ref, value in zip(outs, results):
            ref[...] = value.astype(ref.dtype)

    operands, specs = [], []
    for array, axis, start in tiled:
        operands.append(array)
        if array.shape[axis] == columns:
            specs.append(whole(array.shape))
            continue
        shape = list(array.shape)
        shape[axis] = columns
        at = (0, start) if axis == 1 else (start, 0)
        specs.append(pl.BlockSpec(tuple(pl.Element(n) for n in shape), lambda *_, at=at: at))
    for array in fixed:
        operands.append(array)
        specs.append(whole(array.shape))
    shapes = [(shape, dtype) for shape, dtype, *_ in tiled_out] + list(fixed_out)
    return pl.pallas_call(
        kernel,
        in_specs=specs,
        out_specs=[whole(shape) for shape, _ in shapes],
        out_shape=[jax.ShapeDtypeStruct(shape, dtype) for shape, dtype in shapes],
        grid=(1,),
        compiler_params=PARAMS,
        cost_estimate=LIGHT,
    )(*operands)


def over_columns(
    compute, columns, tiled, fixed, scalars, tiled_out, fixed_out, into=None, pin=True,
    pin_out=True,
):
    row_windows = [entry[3] if len(entry) > 3 else None for entry in tiled]
    tiled = [entry[:3] for entry in tiled]
    tile = tile_of(columns)
    steps = columns // tile
    n_in, n_fix, n_out = len(tiled), len(fixed), len(tiled_out)

    def kernel(*refs):
        refs = list(refs)
        take = lambda n: [refs.pop(0) for _ in range(n)]
        ins, fixes = take(n_in), take(n_fix)
        scalar = take(1)[0] if scalars is not None else None
        if into is not None:
            take(1)
        outs, fix_outs = take(n_out), take(len(fixed_out))
        in_bufs, out_bufs, fix_bufs = take(n_in), take(n_out), take(n_fix)
        in_sems, out_sems, fix_sems = take(3)

        def window(ref, axis, start, t, rows=None):
            here = pl.ds(pl.multiple_of(start + t * tile, 128), tile)
            if rows is not None:
                return ref.at[pl.ds(*rows), here]
            return ref.at[:, here] if axis == 1 else ref.at[here, :]

        def loads(t):
            return [
                pltpu.make_async_copy(
                    window(ins[i], axis, start, t, row_windows[i]),
                    window(in_bufs[i], axis, 0, t),
                    in_sems.at[i * steps + t],
                )
                for i, (_, axis, start) in enumerate(tiled)
            ]

        def stores(t):
            return [
                pltpu.make_async_copy(
                    window(out_bufs[i], 1, 0, t),
                    window(outs[i], 1, tiled_out[i][2], t),
                    out_sems.at[i * steps + t],
                )
                for i in range(n_out)
            ]

        whole_loads = [
            pltpu.make_async_copy(fixes[i], fix_bufs[i], fix_sems.at[i]) for i in range(n_fix)
        ]
        for copy in whole_loads:
            copy.start()
        for t in range(steps):
            for copy in loads(t):
                copy.start()
        for copy in whole_loads:
            copy.wait()

        def step(t):
            for copy in loads(t):
                copy.wait()
            values = [
                window(in_bufs[i], axis, 0, t)[...] for i, (_, axis, _) in enumerate(tiled)
            ]
            results = compute(t, values, fix_bufs, scalar, fix_outs)
            for i, value in enumerate(results):
                window(out_bufs[i], 1, 0, t)[...] = value.astype(out_bufs[i].dtype)
            for copy in stores(t):
                copy.start()

        if fixed_out:
            for t in range(steps):
                step(t)
        else:
            pl.loop(0, steps)(step)
        for t in range(steps):
            for copy in stores(t):
                copy.wait()

    hbm = pl.BlockSpec(memory_space=pl.ANY)
    operands = [in_hbm(a) if pin else a for a in [a for a, _, _ in tiled] + list(fixed)]
    specs = [hbm] * (n_in + n_fix)
    if scalars is not None:
        operands.append(scalars)
        specs.append(pl.BlockSpec(memory_space=pltpu.SMEM))
    aliases = {}
    if into is not None:
        aliases[len(operands)] = 0
        operands.append(in_hbm(into))
        specs.append(hbm)
    buffers = [
        pltpu.VMEM(
            (r[1] if r else a.shape[0], columns) if axis == 1 else (columns, a.shape[1]), a.dtype
        )
        for (a, axis, _), r in zip(tiled, row_windows)
    ] + [pltpu.VMEM((shape[0], columns), dtype) for shape, dtype, _ in tiled_out]
    buffers += [pltpu.VMEM(a.shape, a.dtype) for a in fixed]
    return pl.pallas_call(
        kernel,
        in_specs=specs,
        out_specs=[hbm] * n_out + [pl.BlockSpec(memory_space=pltpu.VMEM)] * len(fixed_out),
        out_shape=[
            (pltpu.HBM if pin_out else jax.ShapeDtypeStruct)(shape, dtype)
            for shape, dtype, _ in tiled_out
        ]
        + [jax.ShapeDtypeStruct(shape, dtype) for shape, dtype in fixed_out],
        scratch_shapes=buffers
        + [
            pltpu.SemaphoreType.DMA((max(1, n_in * steps),)),
            pltpu.SemaphoreType.DMA((max(1, n_out * steps),)),
            pltpu.SemaphoreType.DMA((max(1, n_fix),)),
        ],
        input_output_aliases=aliases,
        compiler_params=PARAMS,
        cost_estimate=LIGHT,
    )(*operands)


def tables_of(cap, info_ref, first_x):
    tokens = info_ref.shape[1]
    row = lax.broadcasted_iota(jnp.int32, (tokens, tokens), 0)
    col = lax.broadcasted_iota(jnp.int32, (tokens, tokens), 1)
    before = (row < col).astype(F32).astype(BF16)
    slot_of = lax.broadcasted_iota(jnp.int32, (cap, tokens), 0).astype(F32)
    places, weights = [], []
    for d in range(NX):
        expert = lax.rem(first_x + d, NX).astype(F32)
        first = info_ref[0:1, :] == expert
        second = info_ref[1:2, :] == expert
        named = jnp.where(first | second, 1.0, 0.0)
        prob = jnp.where(first, info_ref[2:3, :], jnp.where(second, info_ref[3:4, :], 0.0))
        rank = jnp.dot(
            jnp.broadcast_to(named, (8, tokens)).astype(BF16), before, preferred_element_type=F32
        )[0:1]
        placed = jnp.where((slot_of == rank) & (named > 0.0), 1.0, 0.0)
        places.append(placed)
        weights.append(
            jnp.broadcast_to(jnp.sum(placed * prob, axis=1, keepdims=True), (cap, 128))
        )
    return places, weights


def transposed(block):
    tokens = block.shape[1]
    row = lax.broadcasted_iota(jnp.int32, (tokens, tokens), 0)
    col = lax.broadcasted_iota(jnp.int32, (tokens, tokens), 1)
    eye = (row == col).astype(F32).astype(BF16)
    return lax.dot_general(eye, block.astype(BF16), CONTRACT_LAST, preferred_element_type=F32)


def route_kernel(
    cap, at_ref, info0_ref, info1_ref, pa_ref, pat_ref, wa_ref, p0_ref, w0_ref, p1_ref, w1_ref,
    keep_ref, send_ref,
):
    x, last = at_ref[0], at_ref[4].astype(F32)
    places, weights = tables_of(cap, info0_ref, jnp.int32(0))
    pa_ref[...] = jnp.concatenate(places, axis=0).astype(BF16)
    pat_ref[...] = transposed(jnp.concatenate(places, axis=0)).astype(BF16)
    wa_ref[...] = jnp.concatenate(weights, axis=0)
    places0, weights0 = tables_of(cap, info0_ref, x)
    places1, weights1 = tables_of(cap, info1_ref, x)
    p0_ref[...] = jnp.concatenate(places0, axis=0).astype(BF16)
    w0_ref[...] = jnp.concatenate(weights0, axis=0)
    p1_ref[...] = jnp.concatenate(places1, axis=0).astype(BF16)
    w1_ref[...] = jnp.concatenate(weights1, axis=0)
    for d in range(NX):
        keep = jnp.concatenate([places0[d] * (1.0 - last), places1[d] * last], axis=0)
        send = jnp.concatenate([places0[d] * last, places1[d] * (1.0 - last)], axis=0)
        keep_ref[d] = transposed(keep).astype(BF16)
        send_ref[d] = transposed(send).astype(BF16)


def route(at, info0, info1, cap):
    tokens = info0.shape[1]
    slots = NX * cap
    place, weight = (slots, tokens), (slots, 128)
    back = (NX, tokens, NZ * cap)
    shapes = [(place, BF16), ((tokens, slots), BF16), (weight, F32), (place, BF16), (weight, F32)]
    shapes += [(place, BF16), (weight, F32), (back, BF16), (back, BF16)]
    return pl.pallas_call(
        functools.partial(route_kernel, cap),
        in_specs=[pl.BlockSpec(memory_space=pltpu.SMEM), whole(info0.shape), whole(info1.shape)],
        out_specs=[whole(s) for s, _ in shapes],
        out_shape=[pltpu.HBM(s, t) for s, t in shapes],
        grid=(1,),
        compiler_params=PARAMS,
        cost_estimate=LIGHT,
    )(at, info0, info1)


def saved_kernel(cap, at_ref, gate_ref, up_ref, f1_ref, f2_ref, ha_ref, hb_ref, g3, u3, h3, k3):
    g3[...] = gate_ref[...].astype(F32).reshape(g3.shape)
    u3[...] = up_ref[...].astype(F32).reshape(u3.shape)
    z, c = at_ref[1], at_ref[2]
    for cr in range(NC):
        for zr in range(NZ):
            for xs in range(NX):
                j = (cr * NZ + zr) * NX + xs
                zs = z if zr == 0 else 1 - z
                cs = c if cr == 0 else 1 - c
                q = xs * (NZ * NC) + zs * NC + cs
                gate, upval = g3[q], u3[q]
                sig = jax.nn.sigmoid(gate)
                f1_ref[pl.ds(j * cap, cap), :] = upval * sig * (1.0 + gate * (1.0 - sig))
                f2_ref[pl.ds(j * cap, cap), :] = gate * sig
                h3[j] = gate * sig * upval
    ha_ref[...] = h3[...].reshape(ha_ref.shape).astype(BF16)
    a_to_b(at_ref[0], h3, k3)
    hb_ref[...] = k3[...].reshape(hb_ref.shape).astype(BF16)


def pairs_of_blocks(x):
    for cr in range(NC):
        for zr in range(NZ):
            for d in range(NX):
                yield (cr * NZ + zr) * NX + lax.rem(x + NX - d, NX), (cr * NX + d) * NZ + zr


def a_to_b(x, a3, b3):
    for ja, jb in pairs_of_blocks(x):
        b3[jb] = a3[ja]


def saved(at, gate, up, cap):
    rows, hid = gate.shape
    blocks = rows // cap
    return pl.pallas_call(
        functools.partial(saved_kernel, cap),
        in_specs=[pl.BlockSpec(memory_space=pltpu.SMEM), whole(gate.shape), whole(up.shape)],
        out_specs=[whole((rows, hid))] * 4,
        out_shape=[jax.ShapeDtypeStruct((rows, hid), t) for t in (F32, F32, BF16, BF16)],
        scratch_shapes=[pltpu.VMEM((blocks, cap, hid), F32)] * 4,
        grid=(1,),
        compiler_params=PARAMS,
        cost_estimate=LIGHT,
    )(at, gate, up)


def pack_a(place, weight, tok, start, columns):
    def compute(t, values, fixed, scalar, outs):
        rows = jnp.dot(fixed[0][...], values[0], preferred_element_type=F32)
        return [rows * fixed[1][:, 0:1]]

    out = ((place.shape[0], columns), BF16, 0)
    return over_columns(
        compute, columns, [(tok, 1, start)], [place, weight], None, [out], [], pin_out=False
    )[0]


def pack_b(place0, weight0, place1, weight1, tok0, start, tok1, cap):
    columns = tok1.shape[1]

    def compute(t, values, fixed, scalar, outs):
        rows0 = jnp.dot(fixed[0][...], values[0], preferred_element_type=F32) * fixed[1][:, 0:1]
        rows1 = jnp.dot(fixed[2][...], values[1], preferred_element_type=F32) * fixed[3][:, 0:1]
        cut = [slice(d * cap, (d + 1) * cap) for d in range(NX)]
        return [jnp.concatenate([rows0[i], rows1[i]], axis=0) for i in cut]

    out = ((NZ * cap, columns), BF16, 0)
    return over_columns(
        compute, columns, [(tok0, 1, start), (tok1, 1, 0)], [place0, weight0, place1, weight1],
        None, [out] * NX, [], pin_out=False,
    )


def use_rows(groups, w_down, hid_t, dh, grad, start, want_sum, want_grad, kernel=over_columns):
    hid, width = w_down.shape
    groups = [[e if isinstance(e, tuple) else (e, None) for e in g] for g in groups]
    columns = groups[0][0][0].shape[1]
    lengths = [sum(r[1] if r else a.shape[0] for a, r in g) for g in groups]
    rows = sum(lengths)
    tiled = [(a, 1, 0, r) if r else (a, 1, 0) for g in groups for a, r in g]
    fixed = []
    if want_sum:
        tiled.append((w_down, 1, start))
        if dh is not None:
            fixed.append(dh)
    if want_grad:
        fixed.append(hid_t)

    def compute(t, values, fixed_refs, scalar, outs):
        values, refs = list(values), list(fixed_refs)
        blocks = []
        for g in groups:
            parts = [values.pop(0) for _ in g]
            blocks.append(parts[0] if len(parts) == 1 else jnp.concatenate(parts, axis=0))
        if want_sum:
            before = refs.pop(0) if dh is not None else None
            low = 0
            for block, many in zip(blocks, lengths):
                here = pl.ds(low, many)
                more = lax.dot_general(block, values[0], CONTRACT_LAST, preferred_element_type=F32)
                if t > 0:
                    more += outs[0][here, :]
                elif before is not None:
                    more += before[here, :]
                outs[0][here, :] = more
                low += many
        if not want_grad:
            return []
        total = None
        for i, block in enumerate(blocks):
            more = jnp.dot(refs[0][i], block, preferred_element_type=F32)
            total = more if total is None else total + more
        return [total]

    sums = [((rows, hid), F32)] if want_sum else []
    if not want_grad:
        return kernel(compute, columns, tiled, fixed, None, [], sums)[0]
    done = over_columns(
        compute, columns, tiled, fixed, None, [((hid, width), F32, start)], sums, grad
    )
    return (done[1], done[0]) if want_sum else done[0]


def join(blocks):
    rows, columns = sum(b.shape[0] for b in blocks), blocks[0].shape[1]

    def compute(t, values, fixed, scalar, outs):
        return [jnp.concatenate(values, axis=0)]

    out = ((rows, columns), blocks[0].dtype, 0)
    return over_columns(compute, columns, [(b, 1, 0) for b in blocks], [], None, [out], [])[0]


def act_kernel(
    at_ref, near_ref, far0_ref, far1_ref, b0_ref, b1_ref, f1_ref, f2_ref,
    ga_ref, ua_ref, gb_ref, ub_ref, one, two,
):
    x = at_ref[0]
    half = two.shape[0] // NC
    two[pl.ds(0, half)] = b0_ref[...].reshape((half,) + two.shape[1:])
    two[pl.ds(half, half)] = b1_ref[...].reshape((half,) + two.shape[1:])
    for ja, jb in pairs_of_blocks(x):
        one[ja] = two[jb]
    many = far0_ref.shape[0]
    dh = jnp.concatenate(
        [near_ref[pl.ds(0, many), :], far0_ref[...], near_ref[pl.ds(many, many), :], far1_ref[...]],
        axis=0,
    ) + one[...].reshape(f1_ref.shape)
    dgate = dh * f1_ref[...]
    dup = dh * f2_ref[...]
    ga_ref[...] = dgate.astype(BF16)
    ua_ref[...] = dup.astype(BF16)
    for value, out_ref in ((dgate, gb_ref), (dup, ub_ref)):
        one[...] = value.reshape(one.shape)
        a_to_b(x, one, two)
        out_ref[...] = two[...].reshape(out_ref.shape).astype(BF16)


def activations(at, dhs, f1, f2, cap):
    rows, hid = f1.shape
    operands = list(dhs) + [f1, f2]
    return pl.pallas_call(
        act_kernel,
        in_specs=[pl.BlockSpec(memory_space=pltpu.SMEM)] + [whole(a.shape) for a in operands],
        out_specs=[whole((rows, hid))] * 4,
        out_shape=[jax.ShapeDtypeStruct((rows, hid), BF16)] * 4,
        scratch_shapes=[pltpu.VMEM((rows // cap, cap, hid), F32)] * 2,
        grid=(1,),
        compiler_params=PARAMS,
        cost_estimate=LIGHT,
    )(at, *operands)


def unpinned(*args):
    return over_columns(*args, pin_out=False)


def parts_of(dg, du, wg, wu, start, columns, half, other, pieces, kernel):
    many = dg.shape[0] // NC
    each = many // pieces
    tiled = [(wg, 0, start), (wu, 0, start)]
    if other is not None:
        tiled.append((other, 1, 0))

    def compute(t, values, fixed, scalar, outs):
        here = pl.ds(half * many, many)
        total = lax.dot_general(
            fixed[0][here, :], values[0], CONTRACT_LAST, preferred_element_type=F32
        )
        total += lax.dot_general(
            fixed[1][here, :], values[1], CONTRACT_LAST, preferred_element_type=F32
        )
        if other is not None:
            total += values[2].astype(F32)
        return [total[i * each : (i + 1) * each] for i in range(pieces)]

    out = ((each, columns), BF16, 0)
    return kernel(compute, columns, tiled, [dg, du], None, [out] * pieces, [])


def sum_z(a, b):
    def compute(t, values, fixed, scalar, outs):
        return [values[0].astype(F32) + values[1].astype(F32)]

    return over_columns(
        compute, a.shape[1], [(a, 1, 0), (b, 1, 0)], [], None, [(a.shape, BF16, 0)], []
    )[0]


def finish_a(place_t, tok, start, rows):
    def compute(t, values, fixed, scalar, outs):
        branch = jnp.dot(fixed[0][...], values[1], preferred_element_type=F32).astype(BF16)
        return [values[0].astype(F32) + branch.astype(F32)]

    out = ((tok.shape[0], rows.shape[1]), BF16, 0)
    return over_columns(
        compute, rows.shape[1], [(tok, 1, start), (rows, 1, 0)], [place_t], None, [out], []
    )[0]


def combine_b(keep, send, blocks):
    columns = blocks[0].shape[1]
    tokens = keep.shape[1]

    def compute(t, values, fixed, scalar, outs):
        totals = []
        for ref in fixed:
            total = None
            for d in range(NX):
                more = jnp.dot(ref[d], values[d], preferred_element_type=F32)
                total = more if total is None else total + more
            totals.append(total)
        return totals

    outs = [((tokens, columns), F32, 0), ((tokens, columns), BF16, 0)]
    return over_columns(compute, columns, [(b, 1, 0) for b in blocks], [keep, send], None, outs, [])


def finish_b(at, own, other, tok0, start, tok1):
    columns = own.shape[1]

    def compute(t, values, fixed, scalar, outs):
        branch = (values[0] + values[1].astype(F32)).astype(BF16)
        tok = jnp.where(scalar[4] == 0, values[2].astype(F32), values[3].astype(F32))
        return [tok + branch.astype(F32)]

    tiled = [(own, 1, 0), (other, 1, 0), (tok0, 1, start), (tok1, 1, 0)]
    return over_columns(compute, columns, tiled, [], at, [(own.shape, BF16, 0)], [])[0]


def place_chunk(piece, width, start, into):
    def compute(t, values, fixed, scalar, outs):
        return values

    columns = piece.shape[1]
    out = ((piece.shape[0], width), piece.dtype, start)
    return over_columns(compute, columns, [(piece, 1, 0)], [], None, [out], [], into, False)[0]


def body(pending, expert_ids, route_weight, gate_saved, up_saved, w_gate, w_up, w_down):
    own = pending[0]
    width = own.shape[1]
    rows, hid = gate_saved.shape[1:]
    cap = rows // (NX * NZ * NC)
    w_gate, w_up, w_down = w_gate[0], w_up[0], w_down[0]
    unit = width // 28
    a0, b0, a1, b1 = EARLY[0] * unit, EARLY[1] * unit, LATE[0] * unit, LATE[1] * unit
    early = a0 + b0
    at_a0, at_b0, at_a1, at_b1 = 0, a0, early, early + a1
    tie = lax.optimization_barrier

    def crossing(s):
        return s % NY == 0

    def swapped(s):
        return s % NY == NY - 1

    tok_a0 = section_move(own[:, :a0], crossing)
    own_b0 = own[:, a0:early]
    next_b0 = ep_move(own_b0, dz=1)
    info = jnp.concatenate([expert_ids[0].astype(F32), route_weight[0]], axis=1).T
    info_far = ep_move(info, dz=1)
    tok_b0 = section_move(release(own_b0, info_far), crossing)
    far_tok0 = section_move(next_b0, crossing)
    own_late = release(own, tok_b0)
    tok_a1 = section_move(own_late[:, early : early + a1], crossing)
    tok_b1 = section_move(release(own_late, tok_a1)[:, early + a1 :], crossing)
    section = lax.axis_index("section").astype(jnp.int32)
    position = lax.axis_index("ep").astype(jnp.int32)
    turned = (section % NY == NY - 1).astype(jnp.int32)
    last = jnp.maximum(turned, (section % NY == 0).astype(jnp.int32))
    z = (position >> 1) & 1
    at = jnp.stack([position >> 2, jnp.where(turned == 1, 1 - z, z), position & 1, turned, last])
    info0 = jnp.where(turned == 1, info_far, info)
    info1 = jnp.where(turned == 1, info, info_far)
    place, place_t, weight, place0, weight0, place1, weight1, keep_t, send_t = route(
        at, info0, info1, cap
    )

    near_a0 = x_exchange(release(pack_a(place, weight, tok_a0, 0, a0), tok_b0))
    near_a0, tok_b0, far_tok0, at_later = tie((near_a0, tok_b0, far_tok0, at))
    far_a0 = ep_move(near_a0, dz=1)
    sent_b0 = pack_b(place0, weight0, place1, weight1, tok_b0, 0, far_tok0, cap)
    got_b0 = x_moves(sent_b0, 1)
    packed_a1 = pack_a(place, weight, tok_a1, 0, a1)
    far_a0, got_b0, packed_a1 = tie((far_a0, got_b0, packed_a1))
    near_a1 = x_exchange(packed_a1)
    far_tok1 = ep_move(tok_b1, dz=1)
    mine0 = join([near_a0, far_a0, sent_b0[0]] + got_b0)
    near_a1, far_tok1, mine0 = tie((near_a1, far_tok1, mine0))
    far_a1 = ep_move(near_a1, dz=1)
    sent_b1 = pack_b(place0, weight0, place1, weight1, tok_b1, 0, far_tok1, cap)
    got_b1 = x_moves(sent_b1, 1)
    many = NX * cap
    theirs0 = ep_move(mine0, dc=1)
    f1, f2, hid_a, hid_b = saved(release(at_later, sent_b1), gate_saved[0], up_saved[0], cap)
    hid_at = hid_a.reshape(NC * NZ, -1, hid).transpose(0, 2, 1)
    hid_bt = hid_b.reshape(NC, -1, hid).transpose(0, 2, 1)
    hid_near = jnp.stack([hid_at[0], hid_at[2], hid_at[1], hid_at[3]])
    rows_a0 = [(mine0, (0, many)), (theirs0, (0, many)), (mine0, (many, many)), (theirs0, (many, many))]
    rows_b0 = [(mine0, (2 * many, 2 * many)), (theirs0, (2 * many, 2 * many))]
    dh_a, grad = use_rows([[g] for g in rows_a0], w_down, hid_near, None, None, at_a0, True, True)
    dh_b, grad = use_rows([[g] for g in rows_b0], w_down, hid_bt, None, grad, at_b0, True, True)
    dh_near, dh_far0, dh_far1 = dh_a[: 2 * many], dh_a[2 * many : 3 * many], dh_a[3 * many :]
    dh_b0, dh_b1 = dh_b[: 2 * many], dh_b[2 * many :]

    def more_dh(groups, dh, start):
        return use_rows(groups, w_down, None, dh, None, start, True, False, at_once)

    far_a1, got_b1, dh_near, dh_far0, dh_far1, dh_b0, dh_b1, grad = tie(
        (far_a1, got_b1, dh_near, dh_far0, dh_far1, dh_b0, dh_b1, grad)
    )
    near_a1_other, far_a1_other = ep_move(near_a1, dc=1), ep_move(far_a1, dc=1)
    mine_b1 = [sent_b1[0]] + got_b1
    theirs_b1 = [ep_move(piece, dc=1) for piece in mine_b1]
    dh_b0 = more_dh([mine_b1], dh_b0, at_b1)
    dh_far0 = more_dh([[far_a1]], dh_far0, at_a1)
    dh_near = more_dh([[near_a1], [near_a1_other]], dh_near, at_a1)
    dh_b1 = more_dh([theirs_b1], dh_b1, at_b1)
    dh_far1 = more_dh([[far_a1_other]], dh_far1, at_a1)
    rows_a1 = [[near_a1], [far_a1], [near_a1_other], [far_a1_other]]
    rows_b1 = [mine_b1, theirs_b1]

    grads = activations(at, [dh_near, dh_far0, dh_far1, dh_b0, dh_b1], f1, f2, cap)

    def parts(kind, low, n, other, pieces, kernel, grads):
        dg, du = grads[:2] if kind == "A" else grads[2:]
        half = 1 if other is None else 0
        return parts_of(dg, du, w_gate, w_up, low, n, half, other, pieces, kernel)

    core_b1 = ep_move(parts("B", at_b1, b1, None, 1, at_once, grads)[0], dc=1)
    core_a1 = ep_move(parts("A", at_a1, a1, None, 1, at_once, grads)[0], dc=1)
    part_b1 = parts("B", at_b1, b1, core_b1, NX, at_once, grads)
    back_b1 = x_moves(part_b1, -1)
    keep_a1, send_a1 = parts("A", at_a1, a1, core_a1, NZ, at_once, grads)
    back_a1 = ep_move(send_a1, dz=1)
    core_b0 = ep_move(parts("B", at_b0, b0, None, 1, at_once, grads)[0], dc=1)
    core_a0 = ep_move(parts("A", at_a0, a0, None, 1, at_once, grads)[0], dc=1)
    grads = release(grads, part_b1, send_a1)
    part_b0 = parts("B", at_b0, b0, core_b0, NX, unpinned, grads)
    keep_a0, send_a0 = parts("A", at_a0, a0, core_a0, NZ, over_columns, grads)
    grad = use_rows(rows_a1, w_down, hid_at, None, release(grad, grads), at_a1, False, True)
    grad = use_rows(rows_b1, w_down, hid_bt, None, grad, at_b1, False, True)
    back_b1, back_a1, part_b0, keep_a0, send_a0, grad = tie(
        (back_b1, back_a1, part_b0, keep_a0, send_a0, grad)
    )
    back_b0 = x_moves(part_b0, -1)
    keep_b1, send_b1 = combine_b(keep_t, send_t, [part_b1[0]] + back_b1)
    cross_b1 = ep_move(send_b1, dz=1)
    back_a0 = ep_move(release(send_a0, cross_b1), dz=1)
    own_a1 = x_exchange(release(sum_z(keep_a1, back_a1), back_b0, cross_b1))
    up_b1 = section_move(finish_b(at, keep_b1, cross_b1, tok_b1, 0, far_tok1), crossing)
    keep_b0, send_b0 = combine_b(keep_t, send_t, [part_b0[0]] + back_b0)
    cross_b0 = ep_move(send_b0, dz=1)
    sum_a0 = sum_z(keep_a0, back_a0)
    done_a1 = finish_a(place_t, tok_a1, 0, own_a1)
    done_b0 = finish_b(at, keep_b0, cross_b0, tok_b0, 0, far_tok0)
    done_a1, sum_a0, up_b1 = tie((done_a1, sum_a0, up_b1))
    up_a1 = section_move(done_a1, swapped)
    own_a0 = x_exchange(sum_a0)
    up_b0 = section_move(done_b0, crossing)
    up_a0 = section_move(finish_a(place_t, tok_a0, 0, own_a0), swapped)
    out = place_chunk(up_b1, width, at_b1, None)
    out = place_chunk(up_a1, width, at_a1, out)
    out = place_chunk(up_b0, width, at_b0, out)
    out = place_chunk(up_a0, width, at_a0, out)
    return (out[None], grad[None])


def solution(mesh):
    placed = (
        P("section", "ep", None),
        P("section", "ep", None),
        P("section", "ep", None),
        P("section", None, "ep"),
        P("section", None, "ep"),
        P("section", None, "ep"),
        P("section", None, "ep"),
        P("section", "ep", None),
    )
    return jax.shard_map(
        body,
        mesh=mesh,
        in_specs=placed,
        out_specs=(P("section", "ep", None), P("section", "ep", None)),
        check_vma=False,
    )
```

```python
import functools

import jax
import jax.numpy as jnp
from jax import lax
from jax.experimental import pallas as pl
from jax.experimental.pallas import tpu as pltpu
from jax.sharding import PartitionSpec as P

NX, NZ, NC, NY = 4, 2, 2, 4
F32, BF16 = jnp.float32, jnp.bfloat16
PARAMS = pltpu.CompilerParams(vmem_limit_bytes=32 << 20)
LIGHT = pl.CostEstimate(flops=1, bytes_accessed=1, transcendentals=0)
EARLY, LATE = (5, 5), (9, 9)
ONCE_TILE = 768
CONTRACT_LAST = (((1,), (1,)), ((), ()))


def section_move(array, flip):
    sections, peers = lax.axis_size("section"), NX * NZ * NC
    pairs = []
    for s in range(sections):
        for q in range(peers):
            to = q ^ NC if flip(s) else q
            pairs.append((s * peers + q, (s - 1) % sections * peers + to))
    return lax.ppermute(array, ("section", "ep"), pairs)


def ep_move(array, dx=0, dz=0, dc=0):
    pairs = []
    for q in range(NX * NZ * NC):
        x, z, c = q // (NZ * NC), q // NC % NZ, q % NC
        pairs.append((q, (x + dx) % NX * NZ * NC + (z ^ dz) * NC + (c ^ dc)))
    return lax.ppermute(array, "ep", pairs)


def x_moves(blocks, sign):
    return [ep_move(blocks[d], dx=sign * d) for d in range(1, NX)]


def x_exchange(array):
    groups = [[x * NZ * NC + i for x in range(NX)] for i in range(NZ * NC)]
    blocks = array.reshape(NX, -1, array.shape[1])
    moved = lax.all_to_all(blocks, "ep", 0, 0, axis_index_groups=groups, tiled=True)
    return moved.reshape(array.shape)


def whole(shape):
    return pl.BlockSpec(shape, lambda *_: (0,) * len(shape))


def in_hbm(array):
    return pltpu.with_memory_space_constraint(array, pltpu.HBM)


def tile_of(columns):
    return max(t for t in range(128, 897, 128) if columns % t == 0)


def release(value, *after):
    return lax.optimization_barrier((value, after))[0]


def at_once(compute, columns, tiled, fixed, scalars, tiled_out, fixed_out, begin=None):
    n_in, n_fix, n_out = len(tiled), len(fixed), len(tiled_out)
    tile = ONCE_TILE if columns % ONCE_TILE == 0 else tile_of(columns)

    def kernel(*refs):
        ins, fixes, outs = refs[:n_in], refs[n_in : n_in + n_fix], refs[n_in + n_fix :]
        if begin is not None:
            begin(fixes, outs[n_out:])

        def step(t):
            here = pl.ds(pl.multiple_of(t * tile, 128), tile)
            values = [
                r[:, here] if axis == 1 else r[here, :] for r, (_, axis, _) in zip(ins, tiled)
            ]
            for ref, value in zip(outs, compute(t, values, fixes, None, outs[n_out:])):
                ref[:, here] = value.astype(ref.dtype)

        pl.loop(0, columns // tile)(step)

    operands, specs = [], []
    for array, axis, start in tiled:
        operands.append(array)
        if array.shape[axis] == columns:
            specs.append(whole(array.shape))
            continue
        shape = list(array.shape)
        shape[axis] = columns
        at = (0, start) if axis == 1 else (start, 0)
        specs.append(pl.BlockSpec(tuple(pl.Element(n) for n in shape), lambda *_, at=at: at))
    for array in fixed:
        operands.append(array)
        specs.append(whole(array.shape))
    shapes = [(shape, dtype) for shape, dtype, *_ in tiled_out] + list(fixed_out)
    return pl.pallas_call(
        kernel,
        in_specs=specs,
        out_specs=[whole(shape) for shape, _ in shapes],
        out_shape=[jax.ShapeDtypeStruct(shape, dtype) for shape, dtype in shapes],
        grid=(1,),
        compiler_params=PARAMS,
        cost_estimate=LIGHT,
    )(*operands)


def over_columns(
    compute, columns, tiled, fixed, scalars, tiled_out, fixed_out, into=None, pin=True,
    pin_out=True, begin=None,
):
    row_windows = [entry[3] if len(entry) > 3 else None for entry in tiled]
    tiled = [entry[:3] for entry in tiled]
    tile = tile_of(columns)
    steps = columns // tile
    n_in, n_fix, n_out = len(tiled), len(fixed), len(tiled_out)

    def kernel(*refs):
        refs = list(refs)
        take = lambda n: [refs.pop(0) for _ in range(n)]
        ins, fixes = take(n_in), take(n_fix)
        scalar = take(1)[0] if scalars is not None else None
        if into is not None:
            take(1)
        outs, fix_outs = take(n_out), take(len(fixed_out))
        in_bufs, out_bufs, fix_bufs = take(n_in), take(n_out), take(n_fix)
        in_sems, out_sems, fix_sems = take(3)

        def window(ref, axis, start, t, rows=None):
            here = pl.ds(pl.multiple_of(start + t * tile, 128), tile)
            if rows is not None:
                return ref.at[pl.ds(*rows), here]
            return ref.at[:, here] if axis == 1 else ref.at[here, :]

        def loads(t):
            return [
                pltpu.make_async_copy(
                    window(ins[i], axis, start, t, row_windows[i]),
                    window(in_bufs[i], axis, 0, t),
                    in_sems.at[i * steps + t],
                )
                for i, (_, axis, start) in enumerate(tiled)
            ]

        def stores(t):
            return [
                pltpu.make_async_copy(
                    window(out_bufs[i], 1, 0, t),
                    window(outs[i], 1, tiled_out[i][2], t),
                    out_sems.at[i * steps + t],
                )
                for i in range(n_out)
            ]

        whole_loads = [
            pltpu.make_async_copy(fixes[i], fix_bufs[i], fix_sems.at[i]) for i in range(n_fix)
        ]
        for copy in whole_loads:
            copy.start()
        for t in range(steps):
            for copy in loads(t):
                copy.start()
        for copy in whole_loads:
            copy.wait()

        def step(t):
            for copy in loads(t):
                copy.wait()
            values = [
                window(in_bufs[i], axis, 0, t)[...] for i, (_, axis, _) in enumerate(tiled)
            ]
            results = compute(t, values, fix_bufs, scalar, fix_outs)
            for i, value in enumerate(results):
                window(out_bufs[i], 1, 0, t)[...] = value.astype(out_bufs[i].dtype)
            for copy in stores(t):
                copy.start()

        if begin is not None:
            begin(fix_bufs, fix_outs)
        pl.loop(0, steps)(step)
        for t in range(steps):
            for copy in stores(t):
                copy.wait()

    hbm = pl.BlockSpec(memory_space=pl.ANY)
    operands = [in_hbm(a) if pin else a for a in [a for a, _, _ in tiled] + list(fixed)]
    specs = [hbm] * (n_in + n_fix)
    if scalars is not None:
        operands.append(scalars)
        specs.append(pl.BlockSpec(memory_space=pltpu.SMEM))
    aliases = {}
    if into is not None:
        aliases[len(operands)] = 0
        operands.append(in_hbm(into))
        specs.append(hbm)
    buffers = [
        pltpu.VMEM(
            (r[1] if r else a.shape[0], columns) if axis == 1 else (columns, a.shape[1]), a.dtype
        )
        for (a, axis, _), r in zip(tiled, row_windows)
    ] + [pltpu.VMEM((shape[0], columns), dtype) for shape, dtype, _ in tiled_out]
    buffers += [pltpu.VMEM(a.shape, a.dtype) for a in fixed]
    return pl.pallas_call(
        kernel,
        in_specs=specs,
        out_specs=[hbm] * n_out + [pl.BlockSpec(memory_space=pltpu.VMEM)] * len(fixed_out),
        out_shape=[
            (pltpu.HBM if pin_out else jax.ShapeDtypeStruct)(shape, dtype)
            for shape, dtype, _ in tiled_out
        ]
        + [jax.ShapeDtypeStruct(shape, dtype) for shape, dtype in fixed_out],
        scratch_shapes=buffers
        + [
            pltpu.SemaphoreType.DMA((max(1, n_in * steps),)),
            pltpu.SemaphoreType.DMA((max(1, n_out * steps),)),
            pltpu.SemaphoreType.DMA((max(1, n_fix),)),
        ],
        input_output_aliases=aliases,
        compiler_params=PARAMS,
        cost_estimate=LIGHT,
    )(*operands)


def tables_of(cap, info_ref, first_x):
    tokens = info_ref.shape[1]
    row = lax.broadcasted_iota(jnp.int32, (tokens, tokens), 0)
    col = lax.broadcasted_iota(jnp.int32, (tokens, tokens), 1)
    before = (row < col).astype(F32).astype(BF16)
    slot_of = lax.broadcasted_iota(jnp.int32, (cap, tokens), 0).astype(F32)
    places, weights = [], []
    for d in range(NX):
        expert = lax.rem(first_x + d, NX).astype(F32)
        first = info_ref[0:1, :] == expert
        second = info_ref[1:2, :] == expert
        named = jnp.where(first | second, 1.0, 0.0)
        prob = jnp.where(first, info_ref[2:3, :], jnp.where(second, info_ref[3:4, :], 0.0))
        rank = jnp.dot(
            jnp.broadcast_to(named, (8, tokens)).astype(BF16), before, preferred_element_type=F32
        )[0:1]
        placed = jnp.where((slot_of == rank) & (named > 0.0), 1.0, 0.0)
        places.append(placed)
        weights.append(
            jnp.broadcast_to(jnp.sum(placed * prob, axis=1, keepdims=True), (cap, 128))
        )
    return places, weights


def transposed(block):
    tokens = block.shape[1]
    row = lax.broadcasted_iota(jnp.int32, (tokens, tokens), 0)
    col = lax.broadcasted_iota(jnp.int32, (tokens, tokens), 1)
    eye = (row == col).astype(F32).astype(BF16)
    return lax.dot_general(eye, block.astype(BF16), CONTRACT_LAST, preferred_element_type=F32)


def route_kernel(
    cap, at_ref, info0_ref, info1_ref, pa_ref, pat_ref, wa_ref, p0_ref, w0_ref, p1_ref, w1_ref,
    keep_ref, send_ref,
):
    x, last = at_ref[0], at_ref[4].astype(F32)
    places, weights = tables_of(cap, info0_ref, jnp.int32(0))
    pa_ref[...] = jnp.concatenate(places, axis=0).astype(BF16)
    pat_ref[...] = transposed(jnp.concatenate(places, axis=0)).astype(BF16)
    wa_ref[...] = jnp.concatenate(weights, axis=0)
    places0, weights0 = tables_of(cap, info0_ref, x)
    places1, weights1 = tables_of(cap, info1_ref, x)
    p0_ref[...] = jnp.concatenate(places0, axis=0).astype(BF16)
    w0_ref[...] = jnp.concatenate(weights0, axis=0)
    p1_ref[...] = jnp.concatenate(places1, axis=0).astype(BF16)
    w1_ref[...] = jnp.concatenate(weights1, axis=0)
    for d in range(NX):
        keep = jnp.concatenate([places0[d] * (1.0 - last), places1[d] * last], axis=0)
        send = jnp.concatenate([places0[d] * last, places1[d] * (1.0 - last)], axis=0)
        keep_ref[d] = transposed(keep).astype(BF16)
        send_ref[d] = transposed(send).astype(BF16)


def route(at, info0, info1, cap):
    tokens = info0.shape[1]
    slots = NX * cap
    place, weight = (slots, tokens), (slots, 128)
    back = (NX, tokens, NZ * cap)
    shapes = [(place, BF16), ((tokens, slots), BF16), (weight, F32), (place, BF16), (weight, F32)]
    shapes += [(place, BF16), (weight, F32), (back, BF16), (back, BF16)]
    return pl.pallas_call(
        functools.partial(route_kernel, cap),
        in_specs=[pl.BlockSpec(memory_space=pltpu.SMEM), whole(info0.shape), whole(info1.shape)],
        out_specs=[whole(s) for s, _ in shapes],
        out_shape=[pltpu.HBM(s, t) for s, t in shapes],
        grid=(1,),
        compiler_params=PARAMS,
        cost_estimate=LIGHT,
    )(at, info0, info1)


def saved_kernel(cap, at_ref, gate_ref, up_ref, f1_ref, f2_ref, ha_ref, hb_ref, g3, u3, h3, k3):
    g3[...] = gate_ref[...].astype(F32).reshape(g3.shape)
    u3[...] = up_ref[...].astype(F32).reshape(u3.shape)
    z, c = at_ref[1], at_ref[2]
    for cr in range(NC):
        for zr in range(NZ):
            for xs in range(NX):
                j = (cr * NZ + zr) * NX + xs
                zs = z if zr == 0 else 1 - z
                cs = c if cr == 0 else 1 - c
                q = xs * (NZ * NC) + zs * NC + cs
                gate, upval = g3[q], u3[q]
                sig = jax.nn.sigmoid(gate)
                f1_ref[pl.ds(j * cap, cap), :] = upval * sig * (1.0 + gate * (1.0 - sig))
                f2_ref[pl.ds(j * cap, cap), :] = gate * sig
                h3[j] = gate * sig * upval
    ha_ref[...] = h3[...].reshape(ha_ref.shape).astype(BF16)
    a_to_b(at_ref[0], h3, k3)
    hb_ref[...] = k3[...].reshape(hb_ref.shape).astype(BF16)


def pairs_of_blocks(x):
    for cr in range(NC):
        for zr in range(NZ):
            for d in range(NX):
                yield (cr * NZ + zr) * NX + lax.rem(x + NX - d, NX), (cr * NX + d) * NZ + zr


def a_to_b(x, a3, b3):
    for ja, jb in pairs_of_blocks(x):
        b3[jb] = a3[ja]


def saved(at, gate, up, cap):
    rows, hid = gate.shape
    blocks = rows // cap
    return pl.pallas_call(
        functools.partial(saved_kernel, cap),
        in_specs=[pl.BlockSpec(memory_space=pltpu.SMEM), whole(gate.shape), whole(up.shape)],
        out_specs=[whole((rows, hid))] * 4,
        out_shape=[jax.ShapeDtypeStruct((rows, hid), t) for t in (F32, F32, BF16, BF16)],
        scratch_shapes=[pltpu.VMEM((blocks, cap, hid), F32)] * 4,
        grid=(1,),
        compiler_params=PARAMS,
        cost_estimate=LIGHT,
    )(at, gate, up)


def pack_a(place, weight, tok, start, columns):
    def compute(t, values, fixed, scalar, outs):
        rows = jnp.dot(fixed[0][...], values[0], preferred_element_type=F32)
        return [rows * fixed[1][:, 0:1]]

    out = ((place.shape[0], columns), BF16, 0)
    return over_columns(
        compute, columns, [(tok, 1, start)], [place, weight], None, [out], [], pin_out=False
    )[0]


def pack_b(place0, weight0, place1, weight1, tok0, start, tok1, cap):
    columns = tok1.shape[1]

    def compute(t, values, fixed, scalar, outs):
        rows0 = jnp.dot(fixed[0][...], values[0], preferred_element_type=F32) * fixed[1][:, 0:1]
        rows1 = jnp.dot(fixed[2][...], values[1], preferred_element_type=F32) * fixed[3][:, 0:1]
        cut = [slice(d * cap, (d + 1) * cap) for d in range(NX)]
        return [jnp.concatenate([rows0[i], rows1[i]], axis=0) for i in cut]

    out = ((NZ * cap, columns), BF16, 0)
    return over_columns(
        compute, columns, [(tok0, 1, start), (tok1, 1, 0)], [place0, weight0, place1, weight1],
        None, [out] * NX, [], pin_out=False,
    )


def use_rows(groups, w_down, hid_t, dh, grad, start, want_sum, want_grad, kernel=over_columns):
    hid, width = w_down.shape
    groups = [[e if isinstance(e, tuple) else (e, None) for e in g] for g in groups]
    columns = groups[0][0][0].shape[1]
    lengths = [sum(r[1] if r else a.shape[0] for a, r in g) for g in groups]
    rows = sum(lengths)
    tiled = [(a, 1, 0, r) if r else (a, 1, 0) for g in groups for a, r in g]
    fixed = []
    if want_sum:
        tiled.append((w_down, 1, start))
        if dh is not None:
            fixed.append(dh)
    if want_grad:
        fixed.append(hid_t)

    def compute(t, values, fixed_refs, scalar, outs):
        values, refs = list(values), list(fixed_refs)
        blocks = []
        for g in groups:
            parts = [values.pop(0) for _ in g]
            blocks.append(parts[0] if len(parts) == 1 else jnp.concatenate(parts, axis=0))
        if want_sum:
            if dh is not None:
                refs.pop(0)
            low = 0
            for block, many in zip(blocks, lengths):
                here = pl.ds(low, many)
                more = lax.dot_general(block, values[0], CONTRACT_LAST, preferred_element_type=F32)
                outs[0][here, :] += more
                low += many
        if not want_grad:
            return []
        total = None
        for i, block in enumerate(blocks):
            more = jnp.dot(refs[0][i], block, preferred_element_type=F32)
            total = more if total is None else total + more
        return [total]

    def begin(fixed_refs, outs):
        outs[0][...] = fixed_refs[0][...] if dh is not None else jnp.zeros((rows, hid), F32)

    begin = begin if want_sum else None
    sums = [((rows, hid), F32)] if want_sum else []
    if not want_grad:
        return kernel(compute, columns, tiled, fixed, None, [], sums, begin=begin)[0]
    done = over_columns(
        compute, columns, tiled, fixed, None, [((hid, width), F32, start)], sums, grad, begin=begin
    )
    return (done[1], done[0]) if want_sum else done[0]


def join(blocks):
    rows, columns = sum(b.shape[0] for b in blocks), blocks[0].shape[1]

    def compute(t, values, fixed, scalar, outs):
        return [jnp.concatenate(values, axis=0)]

    out = ((rows, columns), blocks[0].dtype, 0)
    return over_columns(compute, columns, [(b, 1, 0) for b in blocks], [], None, [out], [])[0]


def act_kernel(
    at_ref, near_ref, far0_ref, far1_ref, b0_ref, b1_ref, f1_ref, f2_ref,
    ga_ref, ua_ref, gb_ref, ub_ref, one, two,
):
    x = at_ref[0]
    half = two.shape[0] // NC
    two[pl.ds(0, half)] = b0_ref[...].reshape((half,) + two.shape[1:])
    two[pl.ds(half, half)] = b1_ref[...].reshape((half,) + two.shape[1:])
    for ja, jb in pairs_of_blocks(x):
        one[ja] = two[jb]
    many = far0_ref.shape[0]
    dh = jnp.concatenate(
        [near_ref[pl.ds(0, many), :], far0_ref[...], near_ref[pl.ds(many, many), :], far1_ref[...]],
        axis=0,
    ) + one[...].reshape(f1_ref.shape)
    dgate = dh * f1_ref[...]
    dup = dh * f2_ref[...]
    ga_ref[...] = dgate.astype(BF16)
    ua_ref[...] = dup.astype(BF16)
    for value, out_ref in ((dgate, gb_ref), (dup, ub_ref)):
        one[...] = value.reshape(one.shape)
        a_to_b(x, one, two)
        out_ref[...] = two[...].reshape(out_ref.shape).astype(BF16)


def activations(at, dhs, f1, f2, cap):
    rows, hid = f1.shape
    operands = list(dhs) + [f1, f2]
    return pl.pallas_call(
        act_kernel,
        in_specs=[pl.BlockSpec(memory_space=pltpu.SMEM)] + [whole(a.shape) for a in operands],
        out_specs=[whole((rows, hid))] * 4,
        out_shape=[jax.ShapeDtypeStruct((rows, hid), BF16)] * 4,
        scratch_shapes=[pltpu.VMEM((rows // cap, cap, hid), F32)] * 2,
        grid=(1,),
        compiler_params=PARAMS,
        cost_estimate=LIGHT,
    )(at, *operands)


def unpinned(*args):
    return over_columns(*args, pin_out=False)


def parts_of(dg, du, wg, wu, start, columns, half, other, pieces, kernel):
    many = dg.shape[0] // NC
    each = many // pieces
    tiled = [(wg, 0, start), (wu, 0, start)]
    if other is not None:
        tiled.append((other, 1, 0))

    def compute(t, values, fixed, scalar, outs):
        here = pl.ds(half * many, many)
        total = lax.dot_general(
            fixed[0][here, :], values[0], CONTRACT_LAST, preferred_element_type=F32
        )
        total += lax.dot_general(
            fixed[1][here, :], values[1], CONTRACT_LAST, preferred_element_type=F32
        )
        if other is not None:
            total += values[2].astype(F32)
        return [total[i * each : (i + 1) * each] for i in range(pieces)]

    out = ((each, columns), BF16, 0)
    return kernel(compute, columns, tiled, [dg, du], None, [out] * pieces, [])


def sum_z(a, b):
    def compute(t, values, fixed, scalar, outs):
        return [values[0].astype(F32) + values[1].astype(F32)]

    return over_columns(
        compute, a.shape[1], [(a, 1, 0), (b, 1, 0)], [], None, [(a.shape, BF16, 0)], []
    )[0]


def finish_a(place_t, tok, start, rows):
    def compute(t, values, fixed, scalar, outs):
        branch = jnp.dot(fixed[0][...], values[1], preferred_element_type=F32).astype(BF16)
        return [values[0].astype(F32) + branch.astype(F32)]

    out = ((tok.shape[0], rows.shape[1]), BF16, 0)
    return over_columns(
        compute, rows.shape[1], [(tok, 1, start), (rows, 1, 0)], [place_t], None, [out], []
    )[0]


def combine_b(keep, send, blocks):
    columns = blocks[0].shape[1]
    tokens = keep.shape[1]

    def compute(t, values, fixed, scalar, outs):
        totals = []
        for ref in fixed:
            total = None
            for d in range(NX):
                more = jnp.dot(ref[d], values[d], preferred_element_type=F32)
                total = more if total is None else total + more
            totals.append(total)
        return totals

    outs = [((tokens, columns), F32, 0), ((tokens, columns), BF16, 0)]
    return over_columns(compute, columns, [(b, 1, 0) for b in blocks], [keep, send], None, outs, [])


def finish_b(at, own, other, tok0, start, tok1):
    columns = own.shape[1]

    def compute(t, values, fixed, scalar, outs):
        branch = (values[0] + values[1].astype(F32)).astype(BF16)
        tok = jnp.where(scalar[4] == 0, values[2].astype(F32), values[3].astype(F32))
        return [tok + branch.astype(F32)]

    tiled = [(own, 1, 0), (other, 1, 0), (tok0, 1, start), (tok1, 1, 0)]
    return over_columns(compute, columns, tiled, [], at, [(own.shape, BF16, 0)], [])[0]


def place_chunk(piece, width, start, into):
    def compute(t, values, fixed, scalar, outs):
        return values

    columns = piece.shape[1]
    out = ((piece.shape[0], width), piece.dtype, start)
    return over_columns(compute, columns, [(piece, 1, 0)], [], None, [out], [], into, False)[0]


def body(pending, expert_ids, route_weight, gate_saved, up_saved, w_gate, w_up, w_down):
    own = pending[0]
    width = own.shape[1]
    rows, hid = gate_saved.shape[1:]
    cap = rows // (NX * NZ * NC)
    w_gate, w_up, w_down = w_gate[0], w_up[0], w_down[0]
    unit = width // 28
    a0, b0, a1, b1 = EARLY[0] * unit, EARLY[1] * unit, LATE[0] * unit, LATE[1] * unit
    early = a0 + b0
    at_a0, at_b0, at_a1, at_b1 = 0, a0, early, early + a1
    tie = lax.optimization_barrier

    def crossing(s):
        return s % NY == 0

    def swapped(s):
        return s % NY == NY - 1

    tok_a0 = section_move(own[:, :a0], crossing)
    own_b0 = own[:, a0:early]
    next_b0 = ep_move(own_b0, dz=1)
    info = jnp.concatenate([expert_ids[0].astype(F32), route_weight[0]], axis=1).T
    info_far = ep_move(info, dz=1)
    tok_b0 = section_move(release(own_b0, tok_a0), crossing)
    far_tok0 = section_move(next_b0, crossing)
    own_late = release(own, tok_b0)
    tok_a1 = section_move(own_late[:, early : early + a1], crossing)
    tok_b1 = section_move(release(own_late, tok_a1)[:, early + a1 :], crossing)
    section = lax.axis_index("section").astype(jnp.int32)
    position = lax.axis_index("ep").astype(jnp.int32)
    turned = (section % NY == NY - 1).astype(jnp.int32)
    last = jnp.maximum(turned, (section % NY == 0).astype(jnp.int32))
    z = (position >> 1) & 1
    at = jnp.stack([position >> 2, jnp.where(turned == 1, 1 - z, z), position & 1, turned, last])
    info0 = jnp.where(turned == 1, info_far, info)
    info1 = jnp.where(turned == 1, info, info_far)
    place, place_t, weight, place0, weight0, place1, weight1, keep_t, send_t = route(
        at, info0, info1, cap
    )

    near_a0 = x_exchange(pack_a(place, weight, tok_a0, 0, a0))
    near_a0, tok_b0, far_tok0, at_later = tie((near_a0, tok_b0, far_tok0, at))
    far_a0 = ep_move(near_a0, dz=1)
    sent_b0 = pack_b(place0, weight0, place1, weight1, tok_b0, 0, far_tok0, cap)
    got_b0 = x_moves(sent_b0, 1)
    f1, f2, hid_a, hid_b = saved(release(at_later, sent_b0), gate_saved[0], up_saved[0], cap)
    hid_at = hid_a.reshape(NC * NZ, -1, hid).transpose(0, 2, 1)
    hid_bt = hid_b.reshape(NC, -1, hid).transpose(0, 2, 1)
    hid_near = jnp.stack([hid_at[0], hid_at[2], hid_at[1], hid_at[3]])
    packed_a1 = pack_a(place, weight, tok_a1, 0, a1)
    far_a0, got_b0, packed_a1, f1, f2, hid_at, hid_bt, hid_near = tie(
        (far_a0, got_b0, packed_a1, f1, f2, hid_at, hid_bt, hid_near)
    )
    near_a1 = x_exchange(packed_a1)
    far_tok1 = ep_move(tok_b1, dz=1)
    mine0 = join([near_a0, far_a0, sent_b0[0]] + got_b0)
    near_a1, far_tok1, mine0 = tie((near_a1, far_tok1, mine0))
    far_a1 = ep_move(near_a1, dz=1)
    sent_b1 = pack_b(place0, weight0, place1, weight1, tok_b1, 0, far_tok1, cap)
    got_b1 = x_moves(sent_b1, 1)
    many = NX * cap
    theirs0 = ep_move(mine0, dc=1)
    rows_a0 = [(mine0, (0, many)), (theirs0, (0, many)), (mine0, (many, many)), (theirs0, (many, many))]
    rows_b0 = [(mine0, (2 * many, 2 * many)), (theirs0, (2 * many, 2 * many))]
    dh_a, grad = use_rows([[g] for g in rows_a0], w_down, hid_near, None, None, at_a0, True, True)
    dh_b, grad = use_rows([[g] for g in rows_b0], w_down, hid_bt, None, grad, at_b0, True, True)
    dh_near, dh_far0, dh_far1 = dh_a[: 2 * many], dh_a[2 * many : 3 * many], dh_a[3 * many :]
    dh_b0, dh_b1 = dh_b[: 2 * many], dh_b[2 * many :]

    def more_dh(groups, dh, start):
        return use_rows(groups, w_down, None, dh, None, start, True, False, at_once)

    far_a1, got_b1, dh_near, dh_far0, dh_far1, dh_b0, dh_b1, grad = tie(
        (far_a1, got_b1, dh_near, dh_far0, dh_far1, dh_b0, dh_b1, grad)
    )
    near_a1_other, far_a1_other = ep_move(near_a1, dc=1), ep_move(far_a1, dc=1)
    mine_b1 = [sent_b1[0]] + got_b1
    theirs_b1 = [ep_move(piece, dc=1) for piece in mine_b1]
    dh_b0 = more_dh([mine_b1], dh_b0, at_b1)
    dh_far0 = more_dh([[far_a1]], dh_far0, at_a1)
    dh_near = more_dh([[near_a1], [near_a1_other]], dh_near, at_a1)
    dh_b1 = more_dh([theirs_b1], dh_b1, at_b1)
    dh_far1 = more_dh([[far_a1_other]], dh_far1, at_a1)
    rows_a1 = [[near_a1], [far_a1], [near_a1_other], [far_a1_other]]
    rows_b1 = [mine_b1, theirs_b1]

    grads = activations(at, [dh_near, dh_far0, dh_far1, dh_b0, dh_b1], f1, f2, cap)

    def parts(kind, low, n, other, pieces, kernel, grads):
        dg, du = grads[:2] if kind == "A" else grads[2:]
        half = 1 if other is None else 0
        return parts_of(dg, du, w_gate, w_up, low, n, half, other, pieces, kernel)

    core_b1 = ep_move(parts("B", at_b1, b1, None, 1, at_once, grads)[0], dc=1)
    core_a1 = ep_move(parts("A", at_a1, a1, None, 1, at_once, grads)[0], dc=1)
    part_b1 = parts("B", at_b1, b1, core_b1, NX, at_once, grads)
    back_b1 = x_moves(part_b1, -1)
    keep_a1, send_a1 = parts("A", at_a1, a1, core_a1, NZ, at_once, grads)
    back_a1 = ep_move(send_a1, dz=1)
    core_b0 = ep_move(parts("B", at_b0, b0, None, 1, at_once, grads)[0], dc=1)
    core_a0 = ep_move(parts("A", at_a0, a0, None, 1, at_once, grads)[0], dc=1)
    grads = release(grads, part_b1, send_a1)
    part_b0 = parts("B", at_b0, b0, core_b0, NX, unpinned, grads)
    keep_a0, send_a0 = parts("A", at_a0, a0, core_a0, NZ, over_columns, grads)
    grad = use_rows(rows_a1, w_down, hid_at, None, release(grad, grads), at_a1, False, True)
    grad = use_rows(rows_b1, w_down, hid_bt, None, grad, at_b1, False, True)
    back_b1, back_a1, part_b0, keep_a0, send_a0, grad = tie(
        (back_b1, back_a1, part_b0, keep_a0, send_a0, grad)
    )
    back_b0 = x_moves(part_b0, -1)
    back_a0 = ep_move(send_a0, dz=1)
    keep_b1, send_b1 = combine_b(keep_t, send_t, [part_b1[0]] + back_b1)
    cross_b1 = ep_move(send_b1, dz=1)
    keep_b0, send_b0 = combine_b(keep_t, send_t, [part_b0[0]] + back_b0)
    sum_a1 = sum_z(keep_a1, back_a1)
    cross_b1, send_b0, back_a0, sum_a1 = tie((cross_b1, send_b0, back_a0, sum_a1))
    own_a1 = x_exchange(sum_a1)
    up_b1 = section_move(finish_b(at, keep_b1, cross_b1, tok_b1, 0, far_tok1), crossing)
    cross_b0 = ep_move(send_b0, dz=1)
    sum_a0 = sum_z(keep_a0, back_a0)
    done_a1 = finish_a(place_t, tok_a1, 0, own_a1)
    done_a1, cross_b0, sum_a0, up_b1 = tie((done_a1, cross_b0, sum_a0, up_b1))
    up_a1 = section_move(done_a1, swapped)
    own_a0 = x_exchange(sum_a0)
    up_b0 = section_move(finish_b(at, keep_b0, cross_b0, tok_b0, 0, far_tok0), crossing)
    up_a0 = section_move(finish_a(place_t, tok_a0, 0, own_a0), swapped)
    out = place_chunk(up_b1, width, at_b1, None)
    out = place_chunk(up_a1, width, at_a1, out)
    out = place_chunk(up_b0, width, at_b0, out)
    out = place_chunk(up_a0, width, at_a0, out)
    return (out[None], grad[None])


def solution(mesh):
    placed = (
        P("section", "ep", None),
        P("section", "ep", None),
        P("section", "ep", None),
        P("section", None, "ep"),
        P("section", None, "ep"),
        P("section", None, "ep"),
        P("section", None, "ep"),
        P("section", "ep", None),
    )
    return jax.shard_map(
        body,
        mesh=mesh,
        in_specs=placed,
        out_specs=(P("section", "ep", None), P("section", "ep", None)),
        check_vma=False,
    )
```

```python
import functools

import jax
import jax.numpy as jnp
from jax import lax
from jax.experimental import pallas as pl
from jax.experimental.pallas import tpu as pltpu
from jax.sharding import PartitionSpec as P

NX, NZ, NC, NY = 4, 2, 2, 4
F32, BF16 = jnp.float32, jnp.bfloat16
PARAMS = pltpu.CompilerParams(vmem_limit_bytes=32 << 20)
LIGHT = pl.CostEstimate(flops=1, bytes_accessed=1, transcendentals=0)
EARLY, LATE = (5, 5), (9, 9)
ONCE_TILE = 768
CONTRACT_LAST = (((1,), (1,)), ((), ()))


def section_move(array, flip):
    sections, peers = lax.axis_size("section"), NX * NZ * NC
    pairs = []
    for s in range(sections):
        for q in range(peers):
            to = q ^ NC if flip(s) else q
            pairs.append((s * peers + q, (s - 1) % sections * peers + to))
    return lax.ppermute(array, ("section", "ep"), pairs)


def ep_move(array, dx=0, dz=0, dc=0):
    pairs = []
    for q in range(NX * NZ * NC):
        x, z, c = q // (NZ * NC), q // NC % NZ, q % NC
        pairs.append((q, (x + dx) % NX * NZ * NC + (z ^ dz) * NC + (c ^ dc)))
    return lax.ppermute(array, "ep", pairs)


def x_moves(blocks, sign):
    return [ep_move(blocks[d], dx=sign * d) for d in range(1, NX)]


def x_exchange(array):
    groups = [[x * NZ * NC + i for x in range(NX)] for i in range(NZ * NC)]
    blocks = array.reshape(NX, -1, array.shape[1])
    moved = lax.all_to_all(blocks, "ep", 0, 0, axis_index_groups=groups, tiled=True)
    return moved.reshape(array.shape)


def whole(shape):
    return pl.BlockSpec(shape, lambda *_: (0,) * len(shape))


def in_hbm(array):
    return pltpu.with_memory_space_constraint(array, pltpu.HBM)


def tile_of(columns):
    return max(t for t in range(128, 897, 128) if columns % t == 0)


def release(value, *after):
    return lax.optimization_barrier((value, after))[0]


def at_once(compute, columns, tiled, fixed, scalars, tiled_out, fixed_out, begin=None):
    n_in, n_fix, n_out = len(tiled), len(fixed), len(tiled_out)
    tile = ONCE_TILE if columns % ONCE_TILE == 0 else tile_of(columns)

    def kernel(*refs):
        ins, fixes, outs = refs[:n_in], refs[n_in : n_in + n_fix], refs[n_in + n_fix :]
        if begin is not None:
            begin(fixes, outs[n_out:])

        def step(t):
            here = pl.ds(pl.multiple_of(t * tile, 128), tile)
            values = [
                r[:, here] if axis == 1 else r[here, :] for r, (_, axis, _) in zip(ins, tiled)
            ]
            for ref, value in zip(outs, compute(t, values, fixes, None, outs[n_out:])):
                ref[:, here] = value.astype(ref.dtype)

        pl.loop(0, columns // tile)(step)

    operands, specs = [], []
    for array, axis, start in tiled:
        operands.append(array)
        if array.shape[axis] == columns:
            specs.append(whole(array.shape))
            continue
        shape = list(array.shape)
        shape[axis] = columns
        at = (0, start) if axis == 1 else (start, 0)
        specs.append(pl.BlockSpec(tuple(pl.Element(n) for n in shape), lambda *_, at=at: at))
    for array in fixed:
        operands.append(array)
        specs.append(whole(array.shape))
    shapes = [(shape, dtype) for shape, dtype, *_ in tiled_out] + list(fixed_out)
    return pl.pallas_call(
        kernel,
        in_specs=specs,
        out_specs=[whole(shape) for shape, _ in shapes],
        out_shape=[jax.ShapeDtypeStruct(shape, dtype) for shape, dtype in shapes],
        grid=(1,),
        compiler_params=PARAMS,
        cost_estimate=LIGHT,
    )(*operands)


def over_columns(
    compute, columns, tiled, fixed, scalars, tiled_out, fixed_out, into=None, pin=True,
    pin_out=True, begin=None,
):
    row_windows = [entry[3] if len(entry) > 3 else None for entry in tiled]
    tiled = [entry[:3] for entry in tiled]
    tile = tile_of(columns)
    steps = columns // tile
    n_in, n_fix, n_out = len(tiled), len(fixed), len(tiled_out)

    def kernel(*refs):
        refs = list(refs)
        take = lambda n: [refs.pop(0) for _ in range(n)]
        ins, fixes = take(n_in), take(n_fix)
        scalar = take(1)[0] if scalars is not None else None
        if into is not None:
            take(1)
        outs, fix_outs = take(n_out), take(len(fixed_out))
        in_bufs, out_bufs, fix_bufs = take(n_in), take(n_out), take(n_fix)
        in_sems, out_sems, fix_sems = take(3)

        def window(ref, axis, start, t, rows=None):
            here = pl.ds(pl.multiple_of(start + t * tile, 128), tile)
            if rows is not None:
                return ref.at[pl.ds(*rows), here]
            return ref.at[:, here] if axis == 1 else ref.at[here, :]

        def loads(t):
            return [
                pltpu.make_async_copy(
                    window(ins[i], axis, start, t, row_windows[i]),
                    window(in_bufs[i], axis, 0, t),
                    in_sems.at[i * steps + t],
                )
                for i, (_, axis, start) in enumerate(tiled)
            ]

        def stores(t):
            return [
                pltpu.make_async_copy(
                    window(out_bufs[i], 1, 0, t),
                    window(outs[i], 1, tiled_out[i][2], t),
                    out_sems.at[i * steps + t],
                )
                for i in range(n_out)
            ]

        whole_loads = [
            pltpu.make_async_copy(fixes[i], fix_bufs[i], fix_sems.at[i]) for i in range(n_fix)
        ]
        for copy in whole_loads:
            copy.start()
        for t in range(steps):
            for copy in loads(t):
                copy.start()
        for copy in whole_loads:
            copy.wait()

        def step(t):
            for copy in loads(t):
                copy.wait()
            values = [
                window(in_bufs[i], axis, 0, t)[...] for i, (_, axis, _) in enumerate(tiled)
            ]
            results = compute(t, values, fix_bufs, scalar, fix_outs)
            for i, value in enumerate(results):
                window(out_bufs[i], 1, 0, t)[...] = value.astype(out_bufs[i].dtype)
            for copy in stores(t):
                copy.start()

        if begin is not None:
            begin(fix_bufs, fix_outs)
        pl.loop(0, steps)(step)
        for t in range(steps):
            for copy in stores(t):
                copy.wait()

    hbm = pl.BlockSpec(memory_space=pl.ANY)
    operands = [in_hbm(a) if pin else a for a in [a for a, _, _ in tiled] + list(fixed)]
    specs = [hbm] * (n_in + n_fix)
    if scalars is not None:
        operands.append(scalars)
        specs.append(pl.BlockSpec(memory_space=pltpu.SMEM))
    aliases = {}
    if into is not None:
        aliases[len(operands)] = 0
        operands.append(in_hbm(into))
        specs.append(hbm)
    buffers = [
        pltpu.VMEM(
            (r[1] if r else a.shape[0], columns) if axis == 1 else (columns, a.shape[1]), a.dtype
        )
        for (a, axis, _), r in zip(tiled, row_windows)
    ] + [pltpu.VMEM((shape[0], columns), dtype) for shape, dtype, _ in tiled_out]
    buffers += [pltpu.VMEM(a.shape, a.dtype) for a in fixed]
    return pl.pallas_call(
        kernel,
        in_specs=specs,
        out_specs=[hbm] * n_out + [pl.BlockSpec(memory_space=pltpu.VMEM)] * len(fixed_out),
        out_shape=[
            (pltpu.HBM if pin_out else jax.ShapeDtypeStruct)(shape, dtype)
            for shape, dtype, _ in tiled_out
        ]
        + [jax.ShapeDtypeStruct(shape, dtype) for shape, dtype in fixed_out],
        scratch_shapes=buffers
        + [
            pltpu.SemaphoreType.DMA((max(1, n_in * steps),)),
            pltpu.SemaphoreType.DMA((max(1, n_out * steps),)),
            pltpu.SemaphoreType.DMA((max(1, n_fix),)),
        ],
        input_output_aliases=aliases,
        compiler_params=PARAMS,
        cost_estimate=LIGHT,
    )(*operands)


def tables_of(cap, info_ref, first_x):
    tokens = info_ref.shape[1]
    row = lax.broadcasted_iota(jnp.int32, (tokens, tokens), 0)
    col = lax.broadcasted_iota(jnp.int32, (tokens, tokens), 1)
    before = (row < col).astype(F32).astype(BF16)
    slot_of = lax.broadcasted_iota(jnp.int32, (cap, tokens), 0).astype(F32)
    places, weights = [], []
    for d in range(NX):
        expert = lax.rem(first_x + d, NX).astype(F32)
        first = info_ref[0:1, :] == expert
        second = info_ref[1:2, :] == expert
        named = jnp.where(first | second, 1.0, 0.0)
        prob = jnp.where(first, info_ref[2:3, :], jnp.where(second, info_ref[3:4, :], 0.0))
        rank = jnp.dot(
            jnp.broadcast_to(named, (8, tokens)).astype(BF16), before, preferred_element_type=F32
        )[0:1]
        placed = jnp.where((slot_of == rank) & (named > 0.0), 1.0, 0.0)
        places.append(placed)
        weights.append(
            jnp.broadcast_to(jnp.sum(placed * prob, axis=1, keepdims=True), (cap, 128))
        )
    return places, weights


def transposed(block):
    tokens = block.shape[1]
    row = lax.broadcasted_iota(jnp.int32, (tokens, tokens), 0)
    col = lax.broadcasted_iota(jnp.int32, (tokens, tokens), 1)
    eye = (row == col).astype(F32).astype(BF16)
    return lax.dot_general(eye, block.astype(BF16), CONTRACT_LAST, preferred_element_type=F32)


def route_kernel(
    cap, at_ref, info0_ref, info1_ref, pa_ref, pat_ref, wa_ref, p0_ref, w0_ref, p1_ref, w1_ref,
    keep_ref, send_ref,
):
    x, last = at_ref[0], at_ref[4].astype(F32)
    places, weights = tables_of(cap, info0_ref, jnp.int32(0))
    pa_ref[...] = jnp.concatenate(places, axis=0).astype(BF16)
    pat_ref[...] = transposed(jnp.concatenate(places, axis=0)).astype(BF16)
    wa_ref[...] = jnp.concatenate(weights, axis=0)
    places0, weights0 = tables_of(cap, info0_ref, x)
    places1, weights1 = tables_of(cap, info1_ref, x)
    p0_ref[...] = jnp.concatenate(places0, axis=0).astype(BF16)
    w0_ref[...] = jnp.concatenate(weights0, axis=0)
    p1_ref[...] = jnp.concatenate(places1, axis=0).astype(BF16)
    w1_ref[...] = jnp.concatenate(weights1, axis=0)
    for d in range(NX):
        keep = jnp.concatenate([places0[d] * (1.0 - last), places1[d] * last], axis=0)
        send = jnp.concatenate([places0[d] * last, places1[d] * (1.0 - last)], axis=0)
        keep_ref[d] = transposed(keep).astype(BF16)
        send_ref[d] = transposed(send).astype(BF16)


def route(at, info0, info1, cap):
    tokens = info0.shape[1]
    slots = NX * cap
    place, weight = (slots, tokens), (slots, 128)
    back = (NX, tokens, NZ * cap)
    shapes = [(place, BF16), ((tokens, slots), BF16), (weight, F32), (place, BF16), (weight, F32)]
    shapes += [(place, BF16), (weight, F32), (back, BF16), (back, BF16)]
    return pl.pallas_call(
        functools.partial(route_kernel, cap),
        in_specs=[pl.BlockSpec(memory_space=pltpu.SMEM), whole(info0.shape), whole(info1.shape)],
        out_specs=[whole(s) for s, _ in shapes],
        out_shape=[pltpu.HBM(s, t) for s, t in shapes],
        grid=(1,),
        compiler_params=PARAMS,
        cost_estimate=LIGHT,
    )(at, info0, info1)


def saved_kernel(cap, at_ref, gate_ref, up_ref, f1_ref, f2_ref, ha_ref, hb_ref, g3, u3, h3, k3):
    g3[...] = gate_ref[...].astype(F32).reshape(g3.shape)
    u3[...] = up_ref[...].astype(F32).reshape(u3.shape)
    z, c = at_ref[1], at_ref[2]
    for cr in range(NC):
        for zr in range(NZ):
            for xs in range(NX):
                j = (cr * NZ + zr) * NX + xs
                zs = z if zr == 0 else 1 - z
                cs = c if cr == 0 else 1 - c
                q = xs * (NZ * NC) + zs * NC + cs
                gate, upval = g3[q], u3[q]
                sig = jax.nn.sigmoid(gate)
                f1_ref[pl.ds(j * cap, cap), :] = upval * sig * (1.0 + gate * (1.0 - sig))
                f2_ref[pl.ds(j * cap, cap), :] = gate * sig
                h3[j] = gate * sig * upval
    ha_ref[...] = h3[...].reshape(ha_ref.shape).astype(BF16)
    a_to_b(at_ref[0], h3, k3)
    hb_ref[...] = k3[...].reshape(hb_ref.shape).astype(BF16)


def pairs_of_blocks(x):
    for cr in range(NC):
        for zr in range(NZ):
            for d in range(NX):
                yield (cr * NZ + zr) * NX + lax.rem(x + NX - d, NX), (cr * NX + d) * NZ + zr


def a_to_b(x, a3, b3):
    for ja, jb in pairs_of_blocks(x):
        b3[jb] = a3[ja]


def saved(at, gate, up, cap):
    rows, hid = gate.shape
    blocks = rows // cap
    return pl.pallas_call(
        functools.partial(saved_kernel, cap),
        in_specs=[pl.BlockSpec(memory_space=pltpu.SMEM), whole(gate.shape), whole(up.shape)],
        out_specs=[whole((rows, hid))] * 4,
        out_shape=[jax.ShapeDtypeStruct((rows, hid), t) for t in (F32, F32, BF16, BF16)],
        scratch_shapes=[pltpu.VMEM((blocks, cap, hid), F32)] * 4,
        grid=(1,),
        compiler_params=PARAMS,
        cost_estimate=LIGHT,
    )(at, gate, up)


def pack_a(place, weight, tok, start, columns):
    def compute(t, values, fixed, scalar, outs):
        rows = jnp.dot(fixed[0][...], values[0], preferred_element_type=F32)
        return [rows * fixed[1][:, 0:1]]

    out = ((place.shape[0], columns), BF16, 0)
    return over_columns(
        compute, columns, [(tok, 1, start)], [place, weight], None, [out], [], pin_out=False
    )[0]


def pack_b(place0, weight0, place1, weight1, tok0, start, tok1, cap):
    columns = tok1.shape[1]

    def compute(t, values, fixed, scalar, outs):
        rows0 = jnp.dot(fixed[0][...], values[0], preferred_element_type=F32) * fixed[1][:, 0:1]
        rows1 = jnp.dot(fixed[2][...], values[1], preferred_element_type=F32) * fixed[3][:, 0:1]
        cut = [slice(d * cap, (d + 1) * cap) for d in range(NX)]
        return [jnp.concatenate([rows0[i], rows1[i]], axis=0) for i in cut]

    out = ((NZ * cap, columns), BF16, 0)
    return over_columns(
        compute, columns, [(tok0, 1, start), (tok1, 1, 0)], [place0, weight0, place1, weight1],
        None, [out] * NX, [], pin_out=False,
    )


def use_rows(groups, w_down, hid_t, dh, grad, start, want_sum, want_grad, kernel=over_columns):
    hid, width = w_down.shape
    groups = [[e if isinstance(e, tuple) else (e, None) for e in g] for g in groups]
    columns = groups[0][0][0].shape[1]
    lengths = [sum(r[1] if r else a.shape[0] for a, r in g) for g in groups]
    rows = sum(lengths)
    tiled = [(a, 1, 0, r) if r else (a, 1, 0) for g in groups for a, r in g]
    fixed = []
    if want_sum:
        tiled.append((w_down, 1, start))
        if dh is not None:
            fixed.append(dh)
    if want_grad:
        fixed.append(hid_t)

    def compute(t, values, fixed_refs, scalar, outs):
        values, refs = list(values), list(fixed_refs)
        blocks = []
        for g in groups:
            parts = [values.pop(0) for _ in g]
            blocks.append(parts[0] if len(parts) == 1 else jnp.concatenate(parts, axis=0))
        if want_sum:
            if dh is not None:
                refs.pop(0)
            low = 0
            for block, many in zip(blocks, lengths):
                here = pl.ds(low, many)
                more = lax.dot_general(block, values[0], CONTRACT_LAST, preferred_element_type=F32)
                outs[0][here, :] += more
                low += many
        if not want_grad:
            return []
        total = None
        for i, block in enumerate(blocks):
            more = jnp.dot(refs[0][i], block, preferred_element_type=F32)
            total = more if total is None else total + more
        return [total]

    def begin(fixed_refs, outs):
        outs[0][...] = fixed_refs[0][...] if dh is not None else jnp.zeros((rows, hid), F32)

    begin = begin if want_sum else None
    sums = [((rows, hid), F32)] if want_sum else []
    if not want_grad:
        return kernel(compute, columns, tiled, fixed, None, [], sums, begin=begin)[0]
    done = over_columns(
        compute, columns, tiled, fixed, None, [((hid, width), F32, start)], sums, grad, begin=begin
    )
    return (done[1], done[0]) if want_sum else done[0]


def join(blocks):
    rows, columns = sum(b.shape[0] for b in blocks), blocks[0].shape[1]

    def compute(t, values, fixed, scalar, outs):
        return [jnp.concatenate(values, axis=0)]

    out = ((rows, columns), blocks[0].dtype, 0)
    return over_columns(compute, columns, [(b, 1, 0) for b in blocks], [], None, [out], [])[0]


def act_kernel(
    at_ref, near_ref, far0_ref, far1_ref, b0_ref, b1_ref, f1_ref, f2_ref,
    ga_ref, ua_ref, gb_ref, ub_ref, one, two,
):
    x = at_ref[0]
    half = two.shape[0] // NC
    two[pl.ds(0, half)] = b0_ref[...].reshape((half,) + two.shape[1:])
    two[pl.ds(half, half)] = b1_ref[...].reshape((half,) + two.shape[1:])
    for ja, jb in pairs_of_blocks(x):
        one[ja] = two[jb]
    many = far0_ref.shape[0]
    dh = jnp.concatenate(
        [near_ref[pl.ds(0, many), :], far0_ref[...], near_ref[pl.ds(many, many), :], far1_ref[...]],
        axis=0,
    ) + one[...].reshape(f1_ref.shape)
    dgate = dh * f1_ref[...]
    dup = dh * f2_ref[...]
    ga_ref[...] = dgate.astype(BF16)
    ua_ref[...] = dup.astype(BF16)
    for value, out_ref in ((dgate, gb_ref), (dup, ub_ref)):
        one[...] = value.reshape(one.shape)
        a_to_b(x, one, two)
        out_ref[...] = two[...].reshape(out_ref.shape).astype(BF16)


def activations(at, dhs, f1, f2, cap):
    rows, hid = f1.shape
    operands = list(dhs) + [f1, f2]
    return pl.pallas_call(
        act_kernel,
        in_specs=[pl.BlockSpec(memory_space=pltpu.SMEM)] + [whole(a.shape) for a in operands],
        out_specs=[whole((rows, hid))] * 4,
        out_shape=[jax.ShapeDtypeStruct((rows, hid), BF16)] * 4,
        scratch_shapes=[pltpu.VMEM((rows // cap, cap, hid), F32)] * 2,
        grid=(1,),
        compiler_params=PARAMS,
        cost_estimate=LIGHT,
    )(at, *operands)


def unpinned(*args):
    return over_columns(*args, pin_out=False)


def parts_of(dg, du, wg, wu, start, columns, half, other, pieces, kernel):
    many = dg.shape[0] // NC
    each = many // pieces
    tiled = [(wg, 0, start), (wu, 0, start)]
    if other is not None:
        tiled.append((other, 1, 0))

    def compute(t, values, fixed, scalar, outs):
        here = pl.ds(half * many, many)
        total = lax.dot_general(
            fixed[0][here, :], values[0], CONTRACT_LAST, preferred_element_type=F32
        )
        total += lax.dot_general(
            fixed[1][here, :], values[1], CONTRACT_LAST, preferred_element_type=F32
        )
        if other is not None:
            total += values[2].astype(F32)
        return [total[i * each : (i + 1) * each] for i in range(pieces)]

    out = ((each, columns), BF16, 0)
    return kernel(compute, columns, tiled, [dg, du], None, [out] * pieces, [])


def sum_z(a, b):
    def compute(t, values, fixed, scalar, outs):
        return [values[0].astype(F32) + values[1].astype(F32)]

    return over_columns(
        compute, a.shape[1], [(a, 1, 0), (b, 1, 0)], [], None, [(a.shape, BF16, 0)], []
    )[0]


def finish_a(place_t, tok, start, rows):
    def compute(t, values, fixed, scalar, outs):
        branch = jnp.dot(fixed[0][...], values[1], preferred_element_type=F32).astype(BF16)
        return [values[0].astype(F32) + branch.astype(F32)]

    out = ((tok.shape[0], rows.shape[1]), BF16, 0)
    return over_columns(
        compute, rows.shape[1], [(tok, 1, start), (rows, 1, 0)], [place_t], None, [out], []
    )[0]


def combine_b(keep, send, blocks):
    columns = blocks[0].shape[1]
    tokens = keep.shape[1]

    def compute(t, values, fixed, scalar, outs):
        totals = []
        for ref in fixed:
            total = None
            for d in range(NX):
                more = jnp.dot(ref[d], values[d], preferred_element_type=F32)
                total = more if total is None else total + more
            totals.append(total)
        return totals

    outs = [((tokens, columns), F32, 0), ((tokens, columns), BF16, 0)]
    return over_columns(compute, columns, [(b, 1, 0) for b in blocks], [keep, send], None, outs, [])


def finish_b(at, own, other, tok0, start, tok1):
    columns = own.shape[1]

    def compute(t, values, fixed, scalar, outs):
        branch = (values[0] + values[1].astype(F32)).astype(BF16)
        tok = jnp.where(scalar[4] == 0, values[2].astype(F32), values[3].astype(F32))
        return [tok + branch.astype(F32)]

    tiled = [(own, 1, 0), (other, 1, 0), (tok0, 1, start), (tok1, 1, 0)]
    return over_columns(compute, columns, tiled, [], at, [(own.shape, BF16, 0)], [])[0]


def place_chunk(piece, width, start, into):
    def compute(t, values, fixed, scalar, outs):
        return values

    columns = piece.shape[1]
    out = ((piece.shape[0], width), piece.dtype, start)
    return over_columns(compute, columns, [(piece, 1, 0)], [], None, [out], [], into, False)[0]


def body(pending, expert_ids, route_weight, gate_saved, up_saved, w_gate, w_up, w_down):
    own = pending[0]
    width = own.shape[1]
    rows, hid = gate_saved.shape[1:]
    cap = rows // (NX * NZ * NC)
    w_gate, w_up, w_down = w_gate[0], w_up[0], w_down[0]
    unit = width // 28
    a0, b0, a1, b1 = EARLY[0] * unit, EARLY[1] * unit, LATE[0] * unit, LATE[1] * unit
    early = a0 + b0
    at_a0, at_b0, at_a1, at_b1 = 0, a0, early, early + a1
    tie = lax.optimization_barrier

    def crossing(s):
        return s % NY == 0

    def swapped(s):
        return s % NY == NY - 1

    tok_a0 = section_move(own[:, :a0], crossing)
    info = jnp.concatenate([expert_ids[0].astype(F32), route_weight[0]], axis=1).T
    info_far = ep_move(info, dz=1)
    tok_b0 = section_move(own[:, a0:early], crossing)
    tok1 = section_move(release(own, tok_b0)[:, early:], crossing)
    section = lax.axis_index("section").astype(jnp.int32)
    position = lax.axis_index("ep").astype(jnp.int32)
    turned = (section % NY == NY - 1).astype(jnp.int32)
    last = jnp.maximum(turned, (section % NY == 0).astype(jnp.int32))
    z = (position >> 1) & 1
    at = jnp.stack([position >> 2, jnp.where(turned == 1, 1 - z, z), position & 1, turned, last])
    info0 = jnp.where(turned == 1, info_far, info)
    info1 = jnp.where(turned == 1, info, info_far)
    place, place_t, weight, place0, weight0, place1, weight1, keep_t, send_t = route(
        at, info0, info1, cap
    )

    near_a0 = x_exchange(pack_a(place, weight, tok_a0, 0, a0))
    near_a0, far_tok0, at_later = tie((near_a0, ep_move(tok_b0, dz=1), at))
    far_a0 = ep_move(near_a0, dz=1)
    sent_b0 = pack_b(place0, weight0, place1, weight1, tok_b0, 0, far_tok0, cap)
    got_b0 = x_moves(sent_b0, 1)
    f1, f2, hid_a, hid_b = saved(release(at_later, sent_b0), gate_saved[0], up_saved[0], cap)
    hid_at = hid_a.reshape(NC * NZ, -1, hid).transpose(0, 2, 1)
    hid_bt = hid_b.reshape(NC, -1, hid).transpose(0, 2, 1)
    hid_near = jnp.stack([hid_at[0], hid_at[2], hid_at[1], hid_at[3]])
    packed_a1, tok_b1 = pack_a(place, weight, tok1, 0, a1), tok1[:, a1:]
    far_a0, got_b0, packed_a1, tok_b1, f1, f2, hid_at, hid_bt, hid_near = tie(
        (far_a0, got_b0, packed_a1, tok_b1, f1, f2, hid_at, hid_bt, hid_near)
    )
    near_a1 = x_exchange(packed_a1)
    far_tok1 = ep_move(tok_b1, dz=1)
    mine0 = join([near_a0, far_a0, sent_b0[0]] + got_b0)
    near_a1, far_tok1, mine0 = tie((near_a1, far_tok1, mine0))
    far_a1 = ep_move(near_a1, dz=1)
    sent_b1 = pack_b(place0, weight0, place1, weight1, tok_b1, 0, far_tok1, cap)
    got_b1 = x_moves(sent_b1, 1)
    many = NX * cap
    theirs0 = ep_move(mine0, dc=1)
    rows_a0 = [(mine0, (0, many)), (theirs0, (0, many)), (mine0, (many, many)), (theirs0, (many, many))]
    rows_b0 = [(mine0, (2 * many, 2 * many)), (theirs0, (2 * many, 2 * many))]
    dh_a, grad = use_rows([[g] for g in rows_a0], w_down, hid_near, None, None, at_a0, True, True)
    dh_b, grad = use_rows([[g] for g in rows_b0], w_down, hid_bt, None, grad, at_b0, True, True)
    dh_near, dh_far0, dh_far1 = dh_a[: 2 * many], dh_a[2 * many : 3 * many], dh_a[3 * many :]
    dh_b0, dh_b1 = dh_b[: 2 * many], dh_b[2 * many :]

    def more_dh(groups, dh, start):
        return use_rows(groups, w_down, None, dh, None, start, True, False, at_once)

    far_a1, got_b1, dh_near, dh_far0, dh_far1, dh_b0, dh_b1, grad = tie(
        (far_a1, got_b1, dh_near, dh_far0, dh_far1, dh_b0, dh_b1, grad)
    )
    near_a1_other, far_a1_other = ep_move(near_a1, dc=1), ep_move(far_a1, dc=1)
    mine_b1 = [sent_b1[0]] + got_b1
    theirs_b1 = [ep_move(piece, dc=1) for piece in mine_b1]
    dh_b0 = more_dh([mine_b1], dh_b0, at_b1)
    dh_far0 = more_dh([[far_a1]], dh_far0, at_a1)
    dh_near = more_dh([[near_a1], [near_a1_other]], dh_near, at_a1)
    dh_b1 = more_dh([theirs_b1], dh_b1, at_b1)
    dh_far1 = more_dh([[far_a1_other]], dh_far1, at_a1)
    rows_a1 = [[near_a1], [far_a1], [near_a1_other], [far_a1_other]]
    rows_b1 = [mine_b1, theirs_b1]

    grads = activations(at, [dh_near, dh_far0, dh_far1, dh_b0, dh_b1], f1, f2, cap)

    def parts(kind, low, n, other, pieces, kernel, grads):
        dg, du = grads[:2] if kind == "A" else grads[2:]
        half = 1 if other is None else 0
        return parts_of(dg, du, w_gate, w_up, low, n, half, other, pieces, kernel)

    core_b1 = ep_move(parts("B", at_b1, b1, None, 1, at_once, grads)[0], dc=1)
    core_a1 = ep_move(parts("A", at_a1, a1, None, 1, at_once, grads)[0], dc=1)
    part_b1 = parts("B", at_b1, b1, core_b1, NX, at_once, grads)
    back_b1 = x_moves(part_b1, -1)
    keep_a1, send_a1 = parts("A", at_a1, a1, core_a1, NZ, at_once, grads)
    back_a1 = ep_move(send_a1, dz=1)
    core_b0 = ep_move(parts("B", at_b0, b0, None, 1, at_once, grads)[0], dc=1)
    core_a0 = ep_move(parts("A", at_a0, a0, None, 1, at_once, grads)[0], dc=1)
    grads = release(grads, part_b1, send_a1)
    part_b0 = parts("B", at_b0, b0, core_b0, NX, unpinned, grads)
    keep_a0, send_a0 = parts("A", at_a0, a0, core_a0, NZ, over_columns, grads)
    grad = use_rows(rows_a1, w_down, hid_at, None, release(grad, grads), at_a1, False, True)
    grad = use_rows(rows_b1, w_down, hid_bt, None, grad, at_b1, False, True)
    back_b1, back_a1, part_b0, keep_a0, send_a0, grad = tie(
        (back_b1, back_a1, part_b0, keep_a0, send_a0, grad)
    )
    back_b0 = x_moves(part_b0, -1)
    back_a0 = ep_move(send_a0, dz=1)
    keep_b1, send_b1 = combine_b(keep_t, send_t, [part_b1[0]] + back_b1)
    cross_b1 = ep_move(send_b1, dz=1)
    sum_a1 = sum_z(keep_a1, back_a1)
    cross_b1, back_b0, back_a0, sum_a1 = tie((cross_b1, back_b0, back_a0, sum_a1))
    own_a1 = x_exchange(sum_a1)
    up_b1 = section_move(finish_b(at, keep_b1, cross_b1, tok_b1, 0, far_tok1), crossing)
    keep_b0, send_b0 = combine_b(keep_t, send_t, [part_b0[0]] + back_b0)
    cross_b0 = ep_move(send_b0, dz=1)
    sum_a0 = sum_z(keep_a0, back_a0)
    done_b0 = finish_b(at, keep_b0, cross_b0, tok_b0, 0, far_tok0)
    done_b0, sum_a0, up_b1 = tie((done_b0, sum_a0, up_b1))
    up_b0 = section_move(done_b0, crossing)
    up_a1 = section_move(release(finish_a(place_t, tok1, 0, own_a1), up_b0), swapped)
    own_a0 = x_exchange(sum_a0)
    up_a0 = section_move(finish_a(place_t, tok_a0, 0, own_a0), swapped)
    out = place_chunk(up_b1, width, at_b1, None)
    out = place_chunk(up_b0, width, at_b0, out)
    out = place_chunk(up_a1, width, at_a1, out)
    out = place_chunk(up_a0, width, at_a0, out)
    return (out[None], grad[None])


def solution(mesh):
    placed = (
        P("section", "ep", None),
        P("section", "ep", None),
        P("section", "ep", None),
        P("section", None, "ep"),
        P("section", None, "ep"),
        P("section", None, "ep"),
        P("section", None, "ep"),
        P("section", "ep", None),
    )
    return jax.shard_map(
        body,
        mesh=mesh,
        in_specs=placed,
        out_specs=(P("section", "ep", None), P("section", "ep", None)),
        check_vma=False,
    )
```

```python
import functools

import jax
import jax.numpy as jnp
from jax import lax
from jax.experimental import pallas as pl
from jax.experimental.pallas import tpu as pltpu
from jax.sharding import PartitionSpec as P

NX, NZ, NC, NY = 4, 2, 2, 4
F32, BF16 = jnp.float32, jnp.bfloat16
PARAMS = pltpu.CompilerParams(vmem_limit_bytes=32 << 20)
LIGHT = pl.CostEstimate(flops=1, bytes_accessed=1, transcendentals=0)
EARLY, LATE = (5, 5), (9, 9)
ONCE_TILE = 768
CONTRACT_LAST = (((1,), (1,)), ((), ()))


def section_move(array, flip):
    sections, peers = lax.axis_size("section"), NX * NZ * NC
    pairs = []
    for s in range(sections):
        for q in range(peers):
            to = q ^ NC if flip(s) else q
            pairs.append((s * peers + q, (s - 1) % sections * peers + to))
    return lax.ppermute(array, ("section", "ep"), pairs)


def ep_move(array, dx=0, dz=0, dc=0):
    pairs = []
    for q in range(NX * NZ * NC):
        x, z, c = q // (NZ * NC), q // NC % NZ, q % NC
        pairs.append((q, (x + dx) % NX * NZ * NC + (z ^ dz) * NC + (c ^ dc)))
    return lax.ppermute(array, "ep", pairs)


def x_moves(blocks, sign):
    return [ep_move(blocks[d], dx=sign * d) for d in range(1, NX)]


def x_exchange(array):
    groups = [[x * NZ * NC + i for x in range(NX)] for i in range(NZ * NC)]
    blocks = array.reshape(NX, -1, array.shape[1])
    moved = lax.all_to_all(blocks, "ep", 0, 0, axis_index_groups=groups, tiled=True)
    return moved.reshape(array.shape)


def whole(shape):
    return pl.BlockSpec(shape, lambda *_: (0,) * len(shape))


def in_hbm(array):
    return pltpu.with_memory_space_constraint(array, pltpu.HBM)


def tile_of(columns):
    return max(t for t in range(128, 897, 128) if columns % t == 0)


def release(value, *after):
    return lax.optimization_barrier((value, after))[0]


def at_once(compute, columns, tiled, fixed, scalars, tiled_out, fixed_out, begin=None):
    n_in, n_fix, n_out = len(tiled), len(fixed), len(tiled_out)
    tile = ONCE_TILE if columns % ONCE_TILE == 0 else tile_of(columns)

    def kernel(*refs):
        ins, fixes, outs = refs[:n_in], refs[n_in : n_in + n_fix], refs[n_in + n_fix :]
        if begin is not None:
            begin(fixes, outs[n_out:])

        def step(t):
            here = pl.ds(pl.multiple_of(t * tile, 128), tile)
            values = [
                r[:, here] if axis == 1 else r[here, :] for r, (_, axis, _) in zip(ins, tiled)
            ]
            for ref, value in zip(outs, compute(t, values, fixes, None, outs[n_out:])):
                ref[:, here] = value.astype(ref.dtype)

        pl.loop(0, columns // tile)(step)

    operands, specs = [], []
    for array, axis, start in tiled:
        operands.append(array)
        if array.shape[axis] == columns:
            specs.append(whole(array.shape))
            continue
        shape = list(array.shape)
        shape[axis] = columns
        at = (0, start) if axis == 1 else (start, 0)
        specs.append(pl.BlockSpec(tuple(pl.Element(n) for n in shape), lambda *_, at=at: at))
    for array in fixed:
        operands.append(array)
        specs.append(whole(array.shape))
    shapes = [(shape, dtype) for shape, dtype, *_ in tiled_out] + list(fixed_out)
    return pl.pallas_call(
        kernel,
        in_specs=specs,
        out_specs=[whole(shape) for shape, _ in shapes],
        out_shape=[jax.ShapeDtypeStruct(shape, dtype) for shape, dtype in shapes],
        grid=(1,),
        compiler_params=PARAMS,
        cost_estimate=LIGHT,
    )(*operands)


def over_columns(
    compute, columns, tiled, fixed, scalars, tiled_out, fixed_out, into=None, pin=True,
    pin_out=True, begin=None,
):
    row_windows = [entry[3] if len(entry) > 3 else None for entry in tiled]
    tiled = [entry[:3] for entry in tiled]
    tile = tile_of(columns)
    steps = columns // tile
    n_in, n_fix, n_out = len(tiled), len(fixed), len(tiled_out)

    def kernel(*refs):
        refs = list(refs)
        take = lambda n: [refs.pop(0) for _ in range(n)]
        ins, fixes = take(n_in), take(n_fix)
        scalar = take(1)[0] if scalars is not None else None
        if into is not None:
            take(1)
        outs, fix_outs = take(n_out), take(len(fixed_out))
        in_bufs, out_bufs, fix_bufs = take(n_in), take(n_out), take(n_fix)
        in_sems, out_sems, fix_sems = take(3)

        def window(ref, axis, start, t, rows=None):
            here = pl.ds(pl.multiple_of(start + t * tile, 128), tile)
            if rows is not None:
                return ref.at[pl.ds(*rows), here]
            return ref.at[:, here] if axis == 1 else ref.at[here, :]

        def loads(t):
            return [
                pltpu.make_async_copy(
                    window(ins[i], axis, start, t, row_windows[i]),
                    window(in_bufs[i], axis, 0, t),
                    in_sems.at[i * steps + t],
                )
                for i, (_, axis, start) in enumerate(tiled)
            ]

        def stores(t):
            return [
                pltpu.make_async_copy(
                    window(out_bufs[i], 1, 0, t),
                    window(outs[i], 1, tiled_out[i][2], t),
                    out_sems.at[i * steps + t],
                )
                for i in range(n_out)
            ]

        whole_loads = [
            pltpu.make_async_copy(fixes[i], fix_bufs[i], fix_sems.at[i]) for i in range(n_fix)
        ]
        for copy in whole_loads:
            copy.start()
        for t in range(steps):
            for copy in loads(t):
                copy.start()
        for copy in whole_loads:
            copy.wait()

        def step(t):
            for copy in loads(t):
                copy.wait()
            values = [
                window(in_bufs[i], axis, 0, t)[...] for i, (_, axis, _) in enumerate(tiled)
            ]
            results = compute(t, values, fix_bufs, scalar, fix_outs)
            for i, value in enumerate(results):
                window(out_bufs[i], 1, 0, t)[...] = value.astype(out_bufs[i].dtype)
            for copy in stores(t):
                copy.start()

        if begin is not None:
            begin(fix_bufs, fix_outs)
        pl.loop(0, steps)(step)
        for t in range(steps):
            for copy in stores(t):
                copy.wait()

    hbm = pl.BlockSpec(memory_space=pl.ANY)
    operands = [in_hbm(a) if pin else a for a in [a for a, _, _ in tiled] + list(fixed)]
    specs = [hbm] * (n_in + n_fix)
    if scalars is not None:
        operands.append(scalars)
        specs.append(pl.BlockSpec(memory_space=pltpu.SMEM))
    aliases = {}
    if into is not None:
        aliases[len(operands)] = 0
        operands.append(in_hbm(into))
        specs.append(hbm)
    buffers = [
        pltpu.VMEM(
            (r[1] if r else a.shape[0], columns) if axis == 1 else (columns, a.shape[1]), a.dtype
        )
        for (a, axis, _), r in zip(tiled, row_windows)
    ] + [pltpu.VMEM((shape[0], columns), dtype) for shape, dtype, _ in tiled_out]
    buffers += [pltpu.VMEM(a.shape, a.dtype) for a in fixed]
    return pl.pallas_call(
        kernel,
        in_specs=specs,
        out_specs=[hbm] * n_out + [pl.BlockSpec(memory_space=pltpu.VMEM)] * len(fixed_out),
        out_shape=[
            (pltpu.HBM if pin_out else jax.ShapeDtypeStruct)(shape, dtype)
            for shape, dtype, _ in tiled_out
        ]
        + [jax.ShapeDtypeStruct(shape, dtype) for shape, dtype in fixed_out],
        scratch_shapes=buffers
        + [
            pltpu.SemaphoreType.DMA((max(1, n_in * steps),)),
            pltpu.SemaphoreType.DMA((max(1, n_out * steps),)),
            pltpu.SemaphoreType.DMA((max(1, n_fix),)),
        ],
        input_output_aliases=aliases,
        compiler_params=PARAMS,
        cost_estimate=LIGHT,
    )(*operands)


def tables_of(cap, info_ref, first_x):
    tokens = info_ref.shape[1]
    row = lax.broadcasted_iota(jnp.int32, (tokens, tokens), 0)
    col = lax.broadcasted_iota(jnp.int32, (tokens, tokens), 1)
    before = (row < col).astype(F32).astype(BF16)
    slot_of = lax.broadcasted_iota(jnp.int32, (cap, tokens), 0).astype(F32)
    places, weights = [], []
    for d in range(NX):
        expert = lax.rem(first_x + d, NX).astype(F32)
        first = info_ref[0:1, :] == expert
        second = info_ref[1:2, :] == expert
        named = jnp.where(first | second, 1.0, 0.0)
        prob = jnp.where(first, info_ref[2:3, :], jnp.where(second, info_ref[3:4, :], 0.0))
        rank = jnp.dot(
            jnp.broadcast_to(named, (8, tokens)).astype(BF16), before, preferred_element_type=F32
        )[0:1]
        placed = jnp.where((slot_of == rank) & (named > 0.0), 1.0, 0.0)
        places.append(placed)
        weights.append(
            jnp.broadcast_to(jnp.sum(placed * prob, axis=1, keepdims=True), (cap, 128))
        )
    return places, weights


def transposed(block):
    tokens = block.shape[1]
    row = lax.broadcasted_iota(jnp.int32, (tokens, tokens), 0)
    col = lax.broadcasted_iota(jnp.int32, (tokens, tokens), 1)
    eye = (row == col).astype(F32).astype(BF16)
    return lax.dot_general(eye, block.astype(BF16), CONTRACT_LAST, preferred_element_type=F32)


def route_kernel(
    cap, at_ref, info0_ref, info1_ref, pa_ref, pat_ref, wa_ref, p0_ref, w0_ref, p1_ref, w1_ref,
    keep_ref, send_ref,
):
    x, last = at_ref[0], at_ref[4].astype(F32)
    places, weights = tables_of(cap, info0_ref, jnp.int32(0))
    pa_ref[...] = jnp.concatenate(places, axis=0).astype(BF16)
    pat_ref[...] = transposed(jnp.concatenate(places, axis=0)).astype(BF16)
    wa_ref[...] = jnp.concatenate(weights, axis=0)
    places0, weights0 = tables_of(cap, info0_ref, x)
    places1, weights1 = tables_of(cap, info1_ref, x)
    p0_ref[...] = jnp.concatenate(places0, axis=0).astype(BF16)
    w0_ref[...] = jnp.concatenate(weights0, axis=0)
    p1_ref[...] = jnp.concatenate(places1, axis=0).astype(BF16)
    w1_ref[...] = jnp.concatenate(weights1, axis=0)
    for d in range(NX):
        keep = jnp.concatenate([places0[d] * (1.0 - last), places1[d] * last], axis=0)
        send = jnp.concatenate([places0[d] * last, places1[d] * (1.0 - last)], axis=0)
        keep_ref[d] = transposed(keep).astype(BF16)
        send_ref[d] = transposed(send).astype(BF16)


def route(at, info0, info1, cap):
    tokens = info0.shape[1]
    slots = NX * cap
    place, weight = (slots, tokens), (slots, 128)
    back = (NX, tokens, NZ * cap)
    shapes = [(place, BF16), ((tokens, slots), BF16), (weight, F32), (place, BF16), (weight, F32)]
    shapes += [(place, BF16), (weight, F32), (back, BF16), (back, BF16)]
    return pl.pallas_call(
        functools.partial(route_kernel, cap),
        in_specs=[pl.BlockSpec(memory_space=pltpu.SMEM), whole(info0.shape), whole(info1.shape)],
        out_specs=[whole(s) for s, _ in shapes],
        out_shape=[pltpu.HBM(s, t) for s, t in shapes],
        grid=(1,),
        compiler_params=PARAMS,
        cost_estimate=LIGHT,
    )(at, info0, info1)


def saved_kernel(cap, at_ref, gate_ref, up_ref, f1_ref, f2_ref, ha_ref, hb_ref, g3, u3, h3, k3):
    g3[...] = gate_ref[...].astype(F32).reshape(g3.shape)
    u3[...] = up_ref[...].astype(F32).reshape(u3.shape)
    z, c = at_ref[1], at_ref[2]
    for cr in range(NC):
        for zr in range(NZ):
            for xs in range(NX):
                j = (cr * NZ + zr) * NX + xs
                zs = z if zr == 0 else 1 - z
                cs = c if cr == 0 else 1 - c
                q = xs * (NZ * NC) + zs * NC + cs
                gate, upval = g3[q], u3[q]
                sig = jax.nn.sigmoid(gate)
                f1_ref[pl.ds(j * cap, cap), :] = upval * sig * (1.0 + gate * (1.0 - sig))
                f2_ref[pl.ds(j * cap, cap), :] = gate * sig
                h3[j] = gate * sig * upval
    ha_ref[...] = h3[...].reshape(ha_ref.shape).astype(BF16)
    a_to_b(at_ref[0], h3, k3)
    hb_ref[...] = k3[...].reshape(hb_ref.shape).astype(BF16)


def pairs_of_blocks(x):
    for cr in range(NC):
        for zr in range(NZ):
            for d in range(NX):
                yield (cr * NZ + zr) * NX + lax.rem(x + NX - d, NX), (cr * NX + d) * NZ + zr


def a_to_b(x, a3, b3):
    for ja, jb in pairs_of_blocks(x):
        b3[jb] = a3[ja]


def saved(at, gate, up, cap):
    rows, hid = gate.shape
    blocks = rows // cap
    return pl.pallas_call(
        functools.partial(saved_kernel, cap),
        in_specs=[pl.BlockSpec(memory_space=pltpu.SMEM), whole(gate.shape), whole(up.shape)],
        out_specs=[whole((rows, hid))] * 4,
        out_shape=[jax.ShapeDtypeStruct((rows, hid), t) for t in (F32, F32, BF16, BF16)],
        scratch_shapes=[pltpu.VMEM((blocks, cap, hid), F32)] * 4,
        grid=(1,),
        compiler_params=PARAMS,
        cost_estimate=LIGHT,
    )(at, gate, up)


def pack_a(place, weight, tok, start, columns):
    def compute(t, values, fixed, scalar, outs):
        rows = jnp.dot(fixed[0][...], values[0], preferred_element_type=F32)
        return [rows * fixed[1][:, 0:1]]

    out = ((place.shape[0], columns), BF16, 0)
    return over_columns(
        compute, columns, [(tok, 1, start)], [place, weight], None, [out], [], pin_out=False
    )[0]


def pack_b(place0, weight0, place1, weight1, tok0, start, tok1, cap):
    columns = tok1.shape[1]

    def compute(t, values, fixed, scalar, outs):
        rows0 = jnp.dot(fixed[0][...], values[0], preferred_element_type=F32) * fixed[1][:, 0:1]
        rows1 = jnp.dot(fixed[2][...], values[1], preferred_element_type=F32) * fixed[3][:, 0:1]
        cut = [slice(d * cap, (d + 1) * cap) for d in range(NX)]
        return [jnp.concatenate([rows0[i], rows1[i]], axis=0) for i in cut]

    out = ((NZ * cap, columns), BF16, 0)
    return over_columns(
        compute, columns, [(tok0, 1, start), (tok1, 1, 0)], [place0, weight0, place1, weight1],
        None, [out] * NX, [], pin_out=False,
    )


def use_rows(groups, w_down, hid_t, dh, grad, start, want_sum, want_grad, kernel=over_columns):
    hid, width = w_down.shape
    groups = [[e if isinstance(e, tuple) else (e, None) for e in g] for g in groups]
    columns = groups[0][0][0].shape[1]
    lengths = [sum(r[1] if r else a.shape[0] for a, r in g) for g in groups]
    rows = sum(lengths)
    tiled = [(a, 1, 0, r) if r else (a, 1, 0) for g in groups for a, r in g]
    fixed = []
    if want_sum:
        tiled.append((w_down, 1, start))
        if dh is not None:
            fixed.append(dh)
    if want_grad:
        fixed.append(hid_t)

    def compute(t, values, fixed_refs, scalar, outs):
        values, refs = list(values), list(fixed_refs)
        blocks = []
        for g in groups:
            parts = [values.pop(0) for _ in g]
            blocks.append(parts[0] if len(parts) == 1 else jnp.concatenate(parts, axis=0))
        if want_sum:
            if dh is not None:
                refs.pop(0)
            low = 0
            for block, many in zip(blocks, lengths):
                here = pl.ds(low, many)
                more = lax.dot_general(block, values[0], CONTRACT_LAST, preferred_element_type=F32)
                outs[0][here, :] += more
                low += many
        if not want_grad:
            return []
        total = None
        for i, block in enumerate(blocks):
            more = jnp.dot(refs[0][i], block, preferred_element_type=F32)
            total = more if total is None else total + more
        return [total]

    def begin(fixed_refs, outs):
        outs[0][...] = fixed_refs[0][...] if dh is not None else jnp.zeros((rows, hid), F32)

    begin = begin if want_sum else None
    sums = [((rows, hid), F32)] if want_sum else []
    if not want_grad:
        return kernel(compute, columns, tiled, fixed, None, [], sums, begin=begin)[0]
    done = over_columns(
        compute, columns, tiled, fixed, None, [((hid, width), F32, start)], sums, grad, begin=begin
    )
    return (done[1], done[0]) if want_sum else done[0]


def join(blocks):
    rows, columns = sum(b.shape[0] for b in blocks), blocks[0].shape[1]

    def compute(t, values, fixed, scalar, outs):
        return [jnp.concatenate(values, axis=0)]

    out = ((rows, columns), blocks[0].dtype, 0)
    return over_columns(compute, columns, [(b, 1, 0) for b in blocks], [], None, [out], [])[0]


def act_kernel(
    at_ref, near_ref, far0_ref, far1_ref, b0_ref, b1_ref, f1_ref, f2_ref,
    ga_ref, ua_ref, gb_ref, ub_ref, one, two,
):
    x = at_ref[0]
    half = two.shape[0] // NC
    two[pl.ds(0, half)] = b0_ref[...].reshape((half,) + two.shape[1:])
    two[pl.ds(half, half)] = b1_ref[...].reshape((half,) + two.shape[1:])
    for ja, jb in pairs_of_blocks(x):
        one[ja] = two[jb]
    many = far0_ref.shape[0]
    dh = jnp.concatenate(
        [near_ref[pl.ds(0, many), :], far0_ref[...], near_ref[pl.ds(many, many), :], far1_ref[...]],
        axis=0,
    ) + one[...].reshape(f1_ref.shape)
    dgate = dh * f1_ref[...]
    dup = dh * f2_ref[...]
    ga_ref[...] = dgate.astype(BF16)
    ua_ref[...] = dup.astype(BF16)
    for value, out_ref in ((dgate, gb_ref), (dup, ub_ref)):
        one[...] = value.reshape(one.shape)
        a_to_b(x, one, two)
        out_ref[...] = two[...].reshape(out_ref.shape).astype(BF16)


def activations(at, dhs, f1, f2, cap):
    rows, hid = f1.shape
    operands = list(dhs) + [f1, f2]
    return pl.pallas_call(
        act_kernel,
        in_specs=[pl.BlockSpec(memory_space=pltpu.SMEM)] + [whole(a.shape) for a in operands],
        out_specs=[whole((rows, hid))] * 4,
        out_shape=[jax.ShapeDtypeStruct((rows, hid), BF16)] * 4,
        scratch_shapes=[pltpu.VMEM((rows // cap, cap, hid), F32)] * 2,
        grid=(1,),
        compiler_params=PARAMS,
        cost_estimate=LIGHT,
    )(at, *operands)


def unpinned(*args):
    return over_columns(*args, pin_out=False)


def parts_of(dg, du, wg, wu, start, columns, half, other, pieces, kernel):
    many = dg.shape[0] // NC
    each = many // pieces
    tiled = [(wg, 0, start), (wu, 0, start)]
    if other is not None:
        tiled.append((other, 1, 0))

    def compute(t, values, fixed, scalar, outs):
        here = pl.ds(half * many, many)
        total = lax.dot_general(
            fixed[0][here, :], values[0], CONTRACT_LAST, preferred_element_type=F32
        )
        total += lax.dot_general(
            fixed[1][here, :], values[1], CONTRACT_LAST, preferred_element_type=F32
        )
        if other is not None:
            total += values[2].astype(F32)
        return [total[i * each : (i + 1) * each] for i in range(pieces)]

    out = ((each, columns), BF16, 0)
    return kernel(compute, columns, tiled, [dg, du], None, [out] * pieces, [])


def sum_z(a, b):
    def compute(t, values, fixed, scalar, outs):
        return [values[0].astype(F32) + values[1].astype(F32)]

    return over_columns(
        compute, a.shape[1], [(a, 1, 0), (b, 1, 0)], [], None, [(a.shape, BF16, 0)], []
    )[0]


def finish_a(place_t, tok, start, rows):
    def compute(t, values, fixed, scalar, outs):
        branch = jnp.dot(fixed[0][...], values[1], preferred_element_type=F32).astype(BF16)
        return [values[0].astype(F32) + branch.astype(F32)]

    out = ((tok.shape[0], rows.shape[1]), BF16, 0)
    return over_columns(
        compute, rows.shape[1], [(tok, 1, start), (rows, 1, 0)], [place_t], None, [out], []
    )[0]


def combine_b(keep, send, blocks):
    columns = blocks[0].shape[1]
    tokens = keep.shape[1]

    def compute(t, values, fixed, scalar, outs):
        totals = []
        for ref in fixed:
            total = None
            for d in range(NX):
                more = jnp.dot(ref[d], values[d], preferred_element_type=F32)
                total = more if total is None else total + more
            totals.append(total)
        return totals

    outs = [((tokens, columns), F32, 0), ((tokens, columns), BF16, 0)]
    return over_columns(compute, columns, [(b, 1, 0) for b in blocks], [keep, send], None, outs, [])


def finish_b(at, own, other, tok0, start, tok1):
    columns = own.shape[1]

    def compute(t, values, fixed, scalar, outs):
        branch = (values[0] + values[1].astype(F32)).astype(BF16)
        tok = jnp.where(scalar[4] == 0, values[2].astype(F32), values[3].astype(F32))
        return [tok + branch.astype(F32)]

    tiled = [(own, 1, 0), (other, 1, 0), (tok0, 1, start), (tok1, 1, 0)]
    return over_columns(compute, columns, tiled, [], at, [(own.shape, BF16, 0)], [])[0]


def place_chunk(piece, width, start, into):
    def compute(t, values, fixed, scalar, outs):
        return values

    columns = piece.shape[1]
    out = ((piece.shape[0], width), piece.dtype, start)
    return over_columns(compute, columns, [(piece, 1, 0)], [], None, [out], [], into, False)[0]


def body(pending, expert_ids, route_weight, gate_saved, up_saved, w_gate, w_up, w_down):
    own = pending[0]
    width = own.shape[1]
    rows, hid = gate_saved.shape[1:]
    cap = rows // (NX * NZ * NC)
    w_gate, w_up, w_down = w_gate[0], w_up[0], w_down[0]
    unit = width // 28
    a0, b0, a1, b1 = EARLY[0] * unit, EARLY[1] * unit, LATE[0] * unit, LATE[1] * unit
    early = a0 + b0
    at_a0, at_b0, at_a1, at_b1 = 0, a0, early, early + a1
    tie = lax.optimization_barrier

    def crossing(s):
        return s % NY == 0

    def swapped(s):
        return s % NY == NY - 1

    tok_a0 = section_move(own[:, :a0], crossing)
    info = jnp.concatenate([expert_ids[0].astype(F32), route_weight[0]], axis=1).T
    info_far = ep_move(info, dz=1)
    tok_b0 = section_move(own[:, a0:early], crossing)
    tok1 = section_move(release(own, tok_b0)[:, early:], crossing)
    section = lax.axis_index("section").astype(jnp.int32)
    position = lax.axis_index("ep").astype(jnp.int32)
    turned = (section % NY == NY - 1).astype(jnp.int32)
    last = jnp.maximum(turned, (section % NY == 0).astype(jnp.int32))
    z = (position >> 1) & 1
    at = jnp.stack([position >> 2, jnp.where(turned == 1, 1 - z, z), position & 1, turned, last])
    info0 = jnp.where(turned == 1, info_far, info)
    info1 = jnp.where(turned == 1, info, info_far)
    place, place_t, weight, place0, weight0, place1, weight1, keep_t, send_t = route(
        at, info0, info1, cap
    )

    near_a0 = x_exchange(pack_a(place, weight, tok_a0, 0, a0))
    near_a0, far_tok0, at_later = tie((near_a0, ep_move(tok_b0, dz=1), at))
    far_a0 = ep_move(near_a0, dz=1)
    sent_b0 = pack_b(place0, weight0, place1, weight1, tok_b0, 0, far_tok0, cap)
    got_b0 = x_moves(sent_b0, 1)
    f1, f2, hid_a, hid_b = saved(release(at_later, sent_b0), gate_saved[0], up_saved[0], cap)
    hid_at = hid_a.reshape(NC * NZ, -1, hid).transpose(0, 2, 1)
    hid_bt = hid_b.reshape(NC, -1, hid).transpose(0, 2, 1)
    hid_near = jnp.stack([hid_at[0], hid_at[2], hid_at[1], hid_at[3]])
    packed_a1, tok_b1 = pack_a(place, weight, tok1, 0, a1), tok1[:, a1:]
    far_a0, got_b0, packed_a1, tok_b1, f1, f2, hid_at, hid_bt, hid_near = tie(
        (far_a0, got_b0, packed_a1, tok_b1, f1, f2, hid_at, hid_bt, hid_near)
    )
    near_a1 = x_exchange(packed_a1)
    far_tok1 = ep_move(tok_b1, dz=1)
    mine0 = join([near_a0, far_a0, sent_b0[0]] + got_b0)
    near_a1, far_tok1, mine0 = tie((near_a1, far_tok1, mine0))
    far_a1 = ep_move(near_a1, dz=1)
    sent_b1 = pack_b(place0, weight0, place1, weight1, tok_b1, 0, far_tok1, cap)
    got_b1 = x_moves(sent_b1, 1)
    many = NX * cap
    theirs0 = ep_move(mine0, dc=1)
    rows_a0 = [(mine0, (0, many)), (theirs0, (0, many)), (mine0, (many, many)), (theirs0, (many, many))]
    rows_b0 = [(mine0, (2 * many, 2 * many)), (theirs0, (2 * many, 2 * many))]
    dh_a, grad = use_rows([[g] for g in rows_a0], w_down, hid_near, None, None, at_a0, True, True)
    dh_b, grad = use_rows([[g] for g in rows_b0], w_down, hid_bt, None, grad, at_b0, True, True)
    dh_near, dh_far0, dh_far1 = dh_a[: 2 * many], dh_a[2 * many : 3 * many], dh_a[3 * many :]
    dh_b0, dh_b1 = dh_b[: 2 * many], dh_b[2 * many :]

    def more_dh(groups, dh, start):
        return use_rows(groups, w_down, None, dh, None, start, True, False, at_once)

    far_a1, got_b1, dh_near, dh_far0, dh_far1, dh_b0, dh_b1, grad = tie(
        (far_a1, got_b1, dh_near, dh_far0, dh_far1, dh_b0, dh_b1, grad)
    )
    near_a1_other, far_a1_other = ep_move(near_a1, dc=1), ep_move(far_a1, dc=1)
    mine_b1 = [sent_b1[0]] + got_b1
    theirs_b1 = [ep_move(piece, dc=1) for piece in mine_b1]
    dh_b0 = more_dh([mine_b1], dh_b0, at_b1)
    dh_far0 = more_dh([[far_a1]], dh_far0, at_a1)
    dh_near = more_dh([[near_a1], [near_a1_other]], dh_near, at_a1)
    dh_b1 = more_dh([theirs_b1], dh_b1, at_b1)
    dh_far1 = more_dh([[far_a1_other]], dh_far1, at_a1)
    rows_a1 = [[near_a1], [far_a1], [near_a1_other], [far_a1_other]]
    rows_b1 = [mine_b1, theirs_b1]

    grads = activations(at, [dh_near, dh_far0, dh_far1, dh_b0, dh_b1], f1, f2, cap)

    def parts(kind, low, n, other, pieces, kernel, grads):
        dg, du = grads[:2] if kind == "A" else grads[2:]
        half = 1 if other is None else 0
        return parts_of(dg, du, w_gate, w_up, low, n, half, other, pieces, kernel)

    core_b1 = ep_move(parts("B", at_b1, b1, None, 1, at_once, grads)[0], dc=1)
    core_a1 = ep_move(parts("A", at_a1, a1, None, 1, at_once, grads)[0], dc=1)
    part_b1 = parts("B", at_b1, b1, core_b1, NX, at_once, grads)
    back_b1 = x_moves(part_b1, -1)
    keep_a1, send_a1 = parts("A", at_a1, a1, core_a1, NZ, at_once, grads)
    back_a1 = ep_move(send_a1, dz=1)
    core_b0 = ep_move(parts("B", at_b0, b0, None, 1, at_once, grads)[0], dc=1)
    core_a0 = ep_move(parts("A", at_a0, a0, None, 1, at_once, grads)[0], dc=1)
    grads = release(grads, part_b1, send_a1)
    part_b0 = parts("B", at_b0, b0, core_b0, NX, unpinned, grads)
    keep_a0, send_a0 = parts("A", at_a0, a0, core_a0, NZ, over_columns, grads)
    grad = use_rows(rows_a1, w_down, hid_at, None, release(grad, grads), at_a1, False, True)
    grad = use_rows(rows_b1, w_down, hid_bt, None, grad, at_b1, False, True)
    back_b1, back_a1, part_b0, keep_a0, send_a0, grad = tie(
        (back_b1, back_a1, part_b0, keep_a0, send_a0, grad)
    )
    back_b0 = x_moves(part_b0, -1)
    keep_b1, send_b1 = combine_b(keep_t, send_t, [part_b1[0]] + back_b1)
    cross_b1 = ep_move(send_b1, dz=1)
    back_a0 = ep_move(release(send_a0, cross_b1), dz=1)
    done_b1 = finish_b(at, keep_b1, cross_b1, tok_b1, 0, far_tok1)
    up_b1 = section_move(done_b1, crossing)
    own_a1 = x_exchange(release(sum_z(keep_a1, back_a1), back_b0, done_b1))
    sum_a0 = sum_z(keep_a0, back_a0)
    keep_b0, send_b0 = combine_b(keep_t, send_t, [part_b0[0]] + back_b0)
    cross_b0 = ep_move(send_b0, dz=1)
    done_a1 = finish_a(place_t, tok1, 0, release(own_a1, send_b0))
    up_a1 = section_move(release(done_a1, up_b1), swapped)
    cross_b0 = release(cross_b0, done_a1, sum_a0)
    done_b0 = finish_b(at, keep_b0, cross_b0, tok_b0, 0, far_tok0)
    up_b0 = section_move(release(done_b0, up_a1), crossing)
    own_a0 = x_exchange(release(sum_a0, cross_b0))
    up_a0 = section_move(finish_a(place_t, tok_a0, 0, own_a0), swapped)
    out = place_chunk(up_b1, width, at_b1, None)
    out = place_chunk(up_a1, width, at_a1, out)
    out = place_chunk(up_b0, width, at_b0, out)
    out = place_chunk(up_a0, width, at_a0, out)
    return (out[None], grad[None])


def solution(mesh):
    placed = (
        P("section", "ep", None),
        P("section", "ep", None),
        P("section", "ep", None),
        P("section", None, "ep"),
        P("section", None, "ep"),
        P("section", None, "ep"),
        P("section", None, "ep"),
        P("section", "ep", None),
    )
    return jax.shard_map(
        body,
        mesh=mesh,
        in_specs=placed,
        out_specs=(P("section", "ep", None), P("section", "ep", None)),
        check_vma=False,
    )
```

```python
import functools

import jax
import jax.numpy as jnp
from jax import lax
from jax.experimental import pallas as pl
from jax.experimental.pallas import tpu as pltpu
from jax.sharding import PartitionSpec as P

NX, NZ, NC, NY = 4, 2, 2, 4
F32, BF16 = jnp.float32, jnp.bfloat16
PARAMS = pltpu.CompilerParams(vmem_limit_bytes=32 << 20)
LIGHT = pl.CostEstimate(flops=1, bytes_accessed=1, transcendentals=0)
EARLY, LATE = (5, 5), (9, 9)
ONCE_TILE = 768
CONTRACT_LAST = (((1,), (1,)), ((), ()))


def section_move(array, flip):
    sections, peers = lax.axis_size("section"), NX * NZ * NC
    pairs = []
    for s in range(sections):
        for q in range(peers):
            to = q ^ NC if flip(s) else q
            pairs.append((s * peers + q, (s - 1) % sections * peers + to))
    return lax.ppermute(array, ("section", "ep"), pairs)


def ep_move(array, dx=0, dz=0, dc=0):
    pairs = []
    for q in range(NX * NZ * NC):
        x, z, c = q // (NZ * NC), q // NC % NZ, q % NC
        pairs.append((q, (x + dx) % NX * NZ * NC + (z ^ dz) * NC + (c ^ dc)))
    return lax.ppermute(array, "ep", pairs)


def x_moves(blocks, sign):
    return [ep_move(blocks[d], dx=sign * d) for d in range(1, NX)]


def x_exchange(array):
    groups = [[x * NZ * NC + i for x in range(NX)] for i in range(NZ * NC)]
    blocks = array.reshape(NX, -1, array.shape[1])
    moved = lax.all_to_all(blocks, "ep", 0, 0, axis_index_groups=groups, tiled=True)
    return moved.reshape(array.shape)


def whole(shape):
    return pl.BlockSpec(shape, lambda *_: (0,) * len(shape))


def in_hbm(array):
    return pltpu.with_memory_space_constraint(array, pltpu.HBM)


def tile_of(columns):
    return max(t for t in range(128, 897, 128) if columns % t == 0)


def release(value, *after):
    return lax.optimization_barrier((value, after))[0]


def at_once(compute, columns, tiled, fixed, scalars, tiled_out, fixed_out, begin=None):
    n_in, n_fix, n_out = len(tiled), len(fixed), len(tiled_out)
    tile = ONCE_TILE if columns % ONCE_TILE == 0 else tile_of(columns)

    def kernel(*refs):
        ins, fixes, outs = refs[:n_in], refs[n_in : n_in + n_fix], refs[n_in + n_fix :]
        if begin is not None:
            begin(fixes, outs[n_out:])

        def step(t):
            here = pl.ds(pl.multiple_of(t * tile, 128), tile)
            values = [
                r[:, here] if axis == 1 else r[here, :] for r, (_, axis, _) in zip(ins, tiled)
            ]
            for ref, value in zip(outs, compute(t, values, fixes, None, outs[n_out:])):
                ref[:, here] = value.astype(ref.dtype)

        pl.loop(0, columns // tile)(step)

    operands, specs = [], []
    for array, axis, start in tiled:
        operands.append(array)
        if array.shape[axis] == columns:
            specs.append(whole(array.shape))
            continue
        shape = list(array.shape)
        shape[axis] = columns
        at = (0, start) if axis == 1 else (start, 0)
        specs.append(pl.BlockSpec(tuple(pl.Element(n) for n in shape), lambda *_, at=at: at))
    for array in fixed:
        operands.append(array)
        specs.append(whole(array.shape))
    shapes = [(shape, dtype) for shape, dtype, *_ in tiled_out] + list(fixed_out)
    return pl.pallas_call(
        kernel,
        in_specs=specs,
        out_specs=[whole(shape) for shape, _ in shapes],
        out_shape=[jax.ShapeDtypeStruct(shape, dtype) for shape, dtype in shapes],
        grid=(1,),
        compiler_params=PARAMS,
        cost_estimate=LIGHT,
    )(*operands)


def over_columns(
    compute, columns, tiled, fixed, scalars, tiled_out, fixed_out, into=None, pin=True,
    pin_out=True, begin=None,
):
    row_windows = [entry[3] if len(entry) > 3 else None for entry in tiled]
    tiled = [entry[:3] for entry in tiled]
    tile = tile_of(columns)
    steps = columns // tile
    n_in, n_fix, n_out = len(tiled), len(fixed), len(tiled_out)

    def kernel(*refs):
        refs = list(refs)
        take = lambda n: [refs.pop(0) for _ in range(n)]
        ins, fixes = take(n_in), take(n_fix)
        scalar = take(1)[0] if scalars is not None else None
        if into is not None:
            take(1)
        outs, fix_outs = take(n_out), take(len(fixed_out))
        in_bufs, out_bufs, fix_bufs = take(n_in), take(n_out), take(n_fix)
        in_sems, out_sems, fix_sems = take(3)

        def window(ref, axis, start, t, rows=None):
            here = pl.ds(pl.multiple_of(start + t * tile, 128), tile)
            if rows is not None:
                return ref.at[pl.ds(*rows), here]
            return ref.at[:, here] if axis == 1 else ref.at[here, :]

        def loads(t):
            return [
                pltpu.make_async_copy(
                    window(ins[i], axis, start, t, row_windows[i]),
                    window(in_bufs[i], axis, 0, t),
                    in_sems.at[i * steps + t],
                )
                for i, (_, axis, start) in enumerate(tiled)
            ]

        def stores(t):
            return [
                pltpu.make_async_copy(
                    window(out_bufs[i], 1, 0, t),
                    window(outs[i], 1, tiled_out[i][2], t),
                    out_sems.at[i * steps + t],
                )
                for i in range(n_out)
            ]

        whole_loads = [
            pltpu.make_async_copy(fixes[i], fix_bufs[i], fix_sems.at[i]) for i in range(n_fix)
        ]
        for copy in whole_loads:
            copy.start()
        for t in range(steps):
            for copy in loads(t):
                copy.start()
        for copy in whole_loads:
            copy.wait()

        def step(t):
            for copy in loads(t):
                copy.wait()
            values = [
                window(in_bufs[i], axis, 0, t)[...] for i, (_, axis, _) in enumerate(tiled)
            ]
            results = compute(t, values, fix_bufs, scalar, fix_outs)
            for i, value in enumerate(results):
                window(out_bufs[i], 1, 0, t)[...] = value.astype(out_bufs[i].dtype)
            for copy in stores(t):
                copy.start()

        if begin is not None:
            begin(fix_bufs, fix_outs)
        pl.loop(0, steps)(step)
        for t in range(steps):
            for copy in stores(t):
                copy.wait()

    hbm = pl.BlockSpec(memory_space=pl.ANY)
    operands = [in_hbm(a) if pin else a for a in [a for a, _, _ in tiled] + list(fixed)]
    specs = [hbm] * (n_in + n_fix)
    if scalars is not None:
        operands.append(scalars)
        specs.append(pl.BlockSpec(memory_space=pltpu.SMEM))
    aliases = {}
    if into is not None:
        aliases[len(operands)] = 0
        operands.append(in_hbm(into))
        specs.append(hbm)
    buffers = [
        pltpu.VMEM(
            (r[1] if r else a.shape[0], columns) if axis == 1 else (columns, a.shape[1]), a.dtype
        )
        for (a, axis, _), r in zip(tiled, row_windows)
    ] + [pltpu.VMEM((shape[0], columns), dtype) for shape, dtype, _ in tiled_out]
    buffers += [pltpu.VMEM(a.shape, a.dtype) for a in fixed]
    return pl.pallas_call(
        kernel,
        in_specs=specs,
        out_specs=[hbm] * n_out + [pl.BlockSpec(memory_space=pltpu.VMEM)] * len(fixed_out),
        out_shape=[
            (pltpu.HBM if pin_out else jax.ShapeDtypeStruct)(shape, dtype)
            for shape, dtype, _ in tiled_out
        ]
        + [jax.ShapeDtypeStruct(shape, dtype) for shape, dtype in fixed_out],
        scratch_shapes=buffers
        + [
            pltpu.SemaphoreType.DMA((max(1, n_in * steps),)),
            pltpu.SemaphoreType.DMA((max(1, n_out * steps),)),
            pltpu.SemaphoreType.DMA((max(1, n_fix),)),
        ],
        input_output_aliases=aliases,
        compiler_params=PARAMS,
        cost_estimate=LIGHT,
    )(*operands)


def tables_of(cap, info_ref, first_x):
    tokens = info_ref.shape[1]
    row = lax.broadcasted_iota(jnp.int32, (tokens, tokens), 0)
    col = lax.broadcasted_iota(jnp.int32, (tokens, tokens), 1)
    before = (row < col).astype(F32).astype(BF16)
    slot_of = lax.broadcasted_iota(jnp.int32, (cap, tokens), 0).astype(F32)
    places, weights = [], []
    for d in range(NX):
        expert = lax.rem(first_x + d, NX).astype(F32)
        first = info_ref[0:1, :] == expert
        second = info_ref[1:2, :] == expert
        named = jnp.where(first | second, 1.0, 0.0)
        prob = jnp.where(first, info_ref[2:3, :], jnp.where(second, info_ref[3:4, :], 0.0))
        rank = jnp.dot(
            jnp.broadcast_to(named, (8, tokens)).astype(BF16), before, preferred_element_type=F32
        )[0:1]
        placed = jnp.where((slot_of == rank) & (named > 0.0), 1.0, 0.0)
        places.append(placed)
        weights.append(
            jnp.broadcast_to(jnp.sum(placed * prob, axis=1, keepdims=True), (cap, 128))
        )
    return places, weights


def transposed(block):
    tokens = block.shape[1]
    row = lax.broadcasted_iota(jnp.int32, (tokens, tokens), 0)
    col = lax.broadcasted_iota(jnp.int32, (tokens, tokens), 1)
    eye = (row == col).astype(F32).astype(BF16)
    return lax.dot_general(eye, block.astype(BF16), CONTRACT_LAST, preferred_element_type=F32)


def route_kernel(
    cap, at_ref, info0_ref, info1_ref, pa_ref, pat_ref, wa_ref, p0_ref, w0_ref, p1_ref, w1_ref,
    keep_ref, send_ref,
):
    x, last = at_ref[0], at_ref[4].astype(F32)
    places, weights = tables_of(cap, info0_ref, jnp.int32(0))
    pa_ref[...] = jnp.concatenate(places, axis=0).astype(BF16)
    pat_ref[...] = transposed(jnp.concatenate(places, axis=0)).astype(BF16)
    wa_ref[...] = jnp.concatenate(weights, axis=0)
    places0, weights0 = tables_of(cap, info0_ref, x)
    places1, weights1 = tables_of(cap, info1_ref, x)
    p0_ref[...] = jnp.concatenate(places0, axis=0).astype(BF16)
    w0_ref[...] = jnp.concatenate(weights0, axis=0)
    p1_ref[...] = jnp.concatenate(places1, axis=0).astype(BF16)
    w1_ref[...] = jnp.concatenate(weights1, axis=0)
    for d in range(NX):
        keep = jnp.concatenate([places0[d] * (1.0 - last), places1[d] * last], axis=0)
        send = jnp.concatenate([places0[d] * last, places1[d] * (1.0 - last)], axis=0)
        keep_ref[d] = transposed(keep).astype(BF16)
        send_ref[d] = transposed(send).astype(BF16)


def route(at, info0, info1, cap):
    tokens = info0.shape[1]
    slots = NX * cap
    place, weight = (slots, tokens), (slots, 128)
    back = (NX, tokens, NZ * cap)
    shapes = [(place, BF16), ((tokens, slots), BF16), (weight, F32), (place, BF16), (weight, F32)]
    shapes += [(place, BF16), (weight, F32), (back, BF16), (back, BF16)]
    return pl.pallas_call(
        functools.partial(route_kernel, cap),
        in_specs=[pl.BlockSpec(memory_space=pltpu.SMEM), whole(info0.shape), whole(info1.shape)],
        out_specs=[whole(s) for s, _ in shapes],
        out_shape=[pltpu.HBM(s, t) for s, t in shapes],
        grid=(1,),
        compiler_params=PARAMS,
        cost_estimate=LIGHT,
    )(at, info0, info1)


def saved_kernel(cap, at_ref, gate_ref, up_ref, f1_ref, f2_ref, ha_ref, hb_ref, g3, u3, h3, k3):
    g3[...] = gate_ref[...].astype(F32).reshape(g3.shape)
    u3[...] = up_ref[...].astype(F32).reshape(u3.shape)
    z, c = at_ref[1], at_ref[2]
    for cr in range(NC):
        for zr in range(NZ):
            for xs in range(NX):
                j = (cr * NZ + zr) * NX + xs
                zs = z if zr == 0 else 1 - z
                cs = c if cr == 0 else 1 - c
                q = xs * (NZ * NC) + zs * NC + cs
                gate, upval = g3[q], u3[q]
                sig = jax.nn.sigmoid(gate)
                f1_ref[pl.ds(j * cap, cap), :] = upval * sig * (1.0 + gate * (1.0 - sig))
                f2_ref[pl.ds(j * cap, cap), :] = gate * sig
                h3[j] = gate * sig * upval
    ha_ref[...] = h3[...].reshape(ha_ref.shape).astype(BF16)
    a_to_b(at_ref[0], h3, k3)
    hb_ref[...] = k3[...].reshape(hb_ref.shape).astype(BF16)


def pairs_of_blocks(x):
    for cr in range(NC):
        for zr in range(NZ):
            for d in range(NX):
                yield (cr * NZ + zr) * NX + lax.rem(x + NX - d, NX), (cr * NX + d) * NZ + zr


def a_to_b(x, a3, b3):
    for ja, jb in pairs_of_blocks(x):
        b3[jb] = a3[ja]


def saved(at, gate, up, cap):
    rows, hid = gate.shape
    blocks = rows // cap
    return pl.pallas_call(
        functools.partial(saved_kernel, cap),
        in_specs=[pl.BlockSpec(memory_space=pltpu.SMEM), whole(gate.shape), whole(up.shape)],
        out_specs=[whole((rows, hid))] * 4,
        out_shape=[jax.ShapeDtypeStruct((rows, hid), t) for t in (F32, F32, BF16, BF16)],
        scratch_shapes=[pltpu.VMEM((blocks, cap, hid), F32)] * 4,
        grid=(1,),
        compiler_params=PARAMS,
        cost_estimate=LIGHT,
    )(at, gate, up)


def pack_a(place, weight, tok, start, columns):
    def compute(t, values, fixed, scalar, outs):
        rows = jnp.dot(fixed[0][...], values[0], preferred_element_type=F32)
        return [rows * fixed[1][:, 0:1]]

    out = ((place.shape[0], columns), BF16, 0)
    return over_columns(
        compute, columns, [(tok, 1, start)], [place, weight], None, [out], [], pin_out=False
    )[0]


def pack_b(place0, weight0, place1, weight1, tok0, start, tok1, cap):
    columns = tok1.shape[1]

    def compute(t, values, fixed, scalar, outs):
        rows0 = jnp.dot(fixed[0][...], values[0], preferred_element_type=F32) * fixed[1][:, 0:1]
        rows1 = jnp.dot(fixed[2][...], values[1], preferred_element_type=F32) * fixed[3][:, 0:1]
        cut = [slice(d * cap, (d + 1) * cap) for d in range(NX)]
        return [jnp.concatenate([rows0[i], rows1[i]], axis=0) for i in cut]

    out = ((NZ * cap, columns), BF16, 0)
    return over_columns(
        compute, columns, [(tok0, 1, start), (tok1, 1, 0)], [place0, weight0, place1, weight1],
        None, [out] * NX, [], pin_out=False,
    )


def use_rows(groups, w_down, hid_t, dh, grad, start, want_sum, want_grad, kernel=over_columns):
    hid, width = w_down.shape
    groups = [[e if isinstance(e, tuple) else (e, None) for e in g] for g in groups]
    columns = groups[0][0][0].shape[1]
    lengths = [sum(r[1] if r else a.shape[0] for a, r in g) for g in groups]
    rows = sum(lengths)
    tiled = [(a, 1, 0, r) if r else (a, 1, 0) for g in groups for a, r in g]
    fixed = []
    if want_sum:
        tiled.append((w_down, 1, start))
        if dh is not None:
            fixed.append(dh)
    if want_grad:
        fixed.append(hid_t)

    def compute(t, values, fixed_refs, scalar, outs):
        values, refs = list(values), list(fixed_refs)
        blocks = []
        for g in groups:
            parts = [values.pop(0) for _ in g]
            blocks.append(parts[0] if len(parts) == 1 else jnp.concatenate(parts, axis=0))
        if want_sum:
            if dh is not None:
                refs.pop(0)
            low = 0
            for block, many in zip(blocks, lengths):
                here = pl.ds(low, many)
                more = lax.dot_general(block, values[0], CONTRACT_LAST, preferred_element_type=F32)
                outs[0][here, :] += more
                low += many
        if not want_grad:
            return []
        total = None
        for i, block in enumerate(blocks):
            more = jnp.dot(refs[0][i], block, preferred_element_type=F32)
            total = more if total is None else total + more
        return [total]

    def begin(fixed_refs, outs):
        outs[0][...] = fixed_refs[0][...] if dh is not None else jnp.zeros((rows, hid), F32)

    begin = begin if want_sum else None
    sums = [((rows, hid), F32)] if want_sum else []
    if not want_grad:
        return kernel(compute, columns, tiled, fixed, None, [], sums, begin=begin)[0]
    done = over_columns(
        compute, columns, tiled, fixed, None, [((hid, width), F32, start)], sums, grad, begin=begin
    )
    return (done[1], done[0]) if want_sum else done[0]


def join(blocks):
    rows, columns = sum(b.shape[0] for b in blocks), blocks[0].shape[1]

    def compute(t, values, fixed, scalar, outs):
        return [jnp.concatenate(values, axis=0)]

    out = ((rows, columns), blocks[0].dtype, 0)
    return over_columns(compute, columns, [(b, 1, 0) for b in blocks], [], None, [out], [])[0]


def act_kernel(
    at_ref, near_ref, far0_ref, far1_ref, b0_ref, b1_ref, f1_ref, f2_ref,
    ga_ref, ua_ref, gb_ref, ub_ref, one, two,
):
    x = at_ref[0]
    half = two.shape[0] // NC
    two[pl.ds(0, half)] = b0_ref[...].reshape((half,) + two.shape[1:])
    two[pl.ds(half, half)] = b1_ref[...].reshape((half,) + two.shape[1:])
    for ja, jb in pairs_of_blocks(x):
        one[ja] = two[jb]
    many = far0_ref.shape[0]
    dh = jnp.concatenate(
        [near_ref[pl.ds(0, many), :], far0_ref[...], near_ref[pl.ds(many, many), :], far1_ref[...]],
        axis=0,
    ) + one[...].reshape(f1_ref.shape)
    dgate = dh * f1_ref[...]
    dup = dh * f2_ref[...]
    ga_ref[...] = dgate.astype(BF16)
    ua_ref[...] = dup.astype(BF16)
    for value, out_ref in ((dgate, gb_ref), (dup, ub_ref)):
        one[...] = value.reshape(one.shape)
        a_to_b(x, one, two)
        out_ref[...] = two[...].reshape(out_ref.shape).astype(BF16)


def activations(at, dhs, f1, f2, cap):
    rows, hid = f1.shape
    operands = list(dhs) + [f1, f2]
    return pl.pallas_call(
        act_kernel,
        in_specs=[pl.BlockSpec(memory_space=pltpu.SMEM)] + [whole(a.shape) for a in operands],
        out_specs=[whole((rows, hid))] * 4,
        out_shape=[jax.ShapeDtypeStruct((rows, hid), BF16)] * 4,
        scratch_shapes=[pltpu.VMEM((rows // cap, cap, hid), F32)] * 2,
        grid=(1,),
        compiler_params=PARAMS,
        cost_estimate=LIGHT,
    )(at, *operands)


def unpinned(*args):
    return over_columns(*args, pin_out=False)


def parts_of(dg, du, wg, wu, start, columns, half, other, pieces, kernel):
    many = dg.shape[0] // NC
    each = many // pieces
    tiled = [(wg, 0, start), (wu, 0, start)]
    if other is not None:
        tiled.append((other, 1, 0))

    def compute(t, values, fixed, scalar, outs):
        here = pl.ds(half * many, many)
        total = lax.dot_general(
            fixed[0][here, :], values[0], CONTRACT_LAST, preferred_element_type=F32
        )
        total += lax.dot_general(
            fixed[1][here, :], values[1], CONTRACT_LAST, preferred_element_type=F32
        )
        if other is not None:
            total += values[2].astype(F32)
        return [total[i * each : (i + 1) * each] for i in range(pieces)]

    out = ((each, columns), BF16, 0)
    return kernel(compute, columns, tiled, [dg, du], None, [out] * pieces, [])


def sum_z(a, b):
    def compute(t, values, fixed, scalar, outs):
        return [values[0].astype(F32) + values[1].astype(F32)]

    return over_columns(
        compute, a.shape[1], [(a, 1, 0), (b, 1, 0)], [], None, [(a.shape, BF16, 0)], []
    )[0]


def finish_a(place_t, tok, start, rows):
    def compute(t, values, fixed, scalar, outs):
        branch = jnp.dot(fixed[0][...], values[1], preferred_element_type=F32).astype(BF16)
        return [values[0].astype(F32) + branch.astype(F32)]

    out = ((tok.shape[0], rows.shape[1]), BF16, 0)
    return over_columns(
        compute, rows.shape[1], [(tok, 1, start), (rows, 1, 0)], [place_t], None, [out], []
    )[0]


def combine_b(keep, send, blocks):
    columns = blocks[0].shape[1]
    tokens = keep.shape[1]

    def compute(t, values, fixed, scalar, outs):
        totals = []
        for ref in fixed:
            total = None
            for d in range(NX):
                more = jnp.dot(ref[d], values[d], preferred_element_type=F32)
                total = more if total is None else total + more
            totals.append(total)
        return totals

    outs = [((tokens, columns), F32, 0), ((tokens, columns), BF16, 0)]
    return over_columns(compute, columns, [(b, 1, 0) for b in blocks], [keep, send], None, outs, [])


def finish_b(at, own, other, tok0, start, tok1):
    columns = own.shape[1]

    def compute(t, values, fixed, scalar, outs):
        branch = (values[0] + values[1].astype(F32)).astype(BF16)
        tok = jnp.where(scalar[4] == 0, values[2].astype(F32), values[3].astype(F32))
        return [tok + branch.astype(F32)]

    tiled = [(own, 1, 0), (other, 1, 0), (tok0, 1, start), (tok1, 1, 0)]
    return over_columns(compute, columns, tiled, [], at, [(own.shape, BF16, 0)], [])[0]


def place_chunk(piece, width, start, into):
    def compute(t, values, fixed, scalar, outs):
        return values

    columns = piece.shape[1]
    out = ((piece.shape[0], width), piece.dtype, start)
    return over_columns(compute, columns, [(piece, 1, 0)], [], None, [out], [], into, False)[0]


def body(pending, expert_ids, route_weight, gate_saved, up_saved, w_gate, w_up, w_down):
    own = pending[0]
    width = own.shape[1]
    rows, hid = gate_saved.shape[1:]
    cap = rows // (NX * NZ * NC)
    w_gate, w_up, w_down = w_gate[0], w_up[0], w_down[0]
    unit = width // 28
    a0, b0, a1, b1 = EARLY[0] * unit, EARLY[1] * unit, LATE[0] * unit, LATE[1] * unit
    early = a0 + b0
    at_a0, at_b0, at_a1, at_b1 = 0, a0, early, early + a1
    tie = lax.optimization_barrier

    def crossing(s):
        return s % NY == 0

    def swapped(s):
        return s % NY == NY - 1

    tok_a0 = section_move(own[:, :a0], crossing)
    info = jnp.concatenate([expert_ids[0].astype(F32), route_weight[0]], axis=1).T
    info_far = ep_move(info, dz=1)
    tok_b0 = section_move(own[:, a0:early], crossing)
    tok1 = section_move(release(own, tok_b0)[:, early:], crossing)
    section = lax.axis_index("section").astype(jnp.int32)
    position = lax.axis_index("ep").astype(jnp.int32)
    turned = (section % NY == NY - 1).astype(jnp.int32)
    last = jnp.maximum(turned, (section % NY == 0).astype(jnp.int32))
    z = (position >> 1) & 1
    at = jnp.stack([position >> 2, jnp.where(turned == 1, 1 - z, z), position & 1, turned, last])
    info0 = jnp.where(turned == 1, info_far, info)
    info1 = jnp.where(turned == 1, info, info_far)
    place, place_t, weight, place0, weight0, place1, weight1, keep_t, send_t = route(
        at, info0, info1, cap
    )

    near_a0 = x_exchange(pack_a(place, weight, tok_a0, 0, a0))
    near_a0, far_tok0, at_later = tie((near_a0, ep_move(tok_b0, dz=1), at))
    far_a0 = ep_move(near_a0, dz=1)
    sent_b0 = pack_b(place0, weight0, place1, weight1, tok_b0, 0, far_tok0, cap)
    got_b0 = x_moves(sent_b0, 1)
    f1, f2, hid_a, hid_b = saved(release(at_later, sent_b0), gate_saved[0], up_saved[0], cap)
    hid_at = hid_a.reshape(NC * NZ, -1, hid).transpose(0, 2, 1)
    hid_bt = hid_b.reshape(NC, -1, hid).transpose(0, 2, 1)
    hid_near = jnp.stack([hid_at[0], hid_at[2], hid_at[1], hid_at[3]])
    packed_a1, tok_b1 = pack_a(place, weight, tok1, 0, a1), tok1[:, a1:]
    far_a0, got_b0, packed_a1, tok_b1, f1, f2, hid_at, hid_bt, hid_near = tie(
        (far_a0, got_b0, packed_a1, tok_b1, f1, f2, hid_at, hid_bt, hid_near)
    )
    near_a1 = x_exchange(packed_a1)
    far_tok1 = ep_move(tok_b1, dz=1)
    mine0 = join([near_a0, far_a0, sent_b0[0]] + got_b0)
    near_a1, far_tok1, mine0 = tie((near_a1, far_tok1, mine0))
    far_a1 = ep_move(near_a1, dz=1)
    sent_b1 = pack_b(place0, weight0, place1, weight1, tok_b1, 0, far_tok1, cap)
    got_b1 = x_moves(sent_b1, 1)
    many = NX * cap
    theirs0 = ep_move(mine0, dc=1)
    rows_a0 = [(mine0, (0, many)), (theirs0, (0, many)), (mine0, (many, many)), (theirs0, (many, many))]
    rows_b0 = [(mine0, (2 * many, 2 * many)), (theirs0, (2 * many, 2 * many))]
    dh_a, grad = use_rows([[g] for g in rows_a0], w_down, hid_near, None, None, at_a0, True, True)
    dh_b, grad = use_rows([[g] for g in rows_b0], w_down, hid_bt, None, grad, at_b0, True, True)
    dh_near, dh_far0, dh_far1 = dh_a[: 2 * many], dh_a[2 * many : 3 * many], dh_a[3 * many :]
    dh_b0, dh_b1 = dh_b[: 2 * many], dh_b[2 * many :]

    def more_dh(groups, dh, start):
        return use_rows(groups, w_down, None, dh, None, start, True, False, at_once)

    far_a1, got_b1, dh_near, dh_far0, dh_far1, dh_b0, dh_b1, grad = tie(
        (far_a1, got_b1, dh_near, dh_far0, dh_far1, dh_b0, dh_b1, grad)
    )
    near_a1_other, far_a1_other = ep_move(near_a1, dc=1), ep_move(far_a1, dc=1)
    mine_b1 = [sent_b1[0]] + got_b1
    theirs_b1 = [ep_move(piece, dc=1) for piece in mine_b1]
    dh_b0 = more_dh([mine_b1], dh_b0, at_b1)
    dh_far0 = more_dh([[far_a1]], dh_far0, at_a1)
    dh_near = more_dh([[near_a1], [near_a1_other]], dh_near, at_a1)
    dh_b1 = more_dh([theirs_b1], dh_b1, at_b1)
    dh_far1 = more_dh([[far_a1_other]], dh_far1, at_a1)
    rows_a1 = [[near_a1], [far_a1], [near_a1_other], [far_a1_other]]
    rows_b1 = [mine_b1, theirs_b1]

    grads = activations(at, [dh_near, dh_far0, dh_far1, dh_b0, dh_b1], f1, f2, cap)

    def parts(kind, low, n, other, pieces, kernel, grads):
        dg, du = grads[:2] if kind == "A" else grads[2:]
        half = 1 if other is None else 0
        return parts_of(dg, du, w_gate, w_up, low, n, half, other, pieces, kernel)

    core_b1 = ep_move(parts("B", at_b1, b1, None, 1, at_once, grads)[0], dc=1)
    core_a1 = ep_move(parts("A", at_a1, a1, None, 1, at_once, grads)[0], dc=1)
    part_b1 = parts("B", at_b1, b1, core_b1, NX, at_once, grads)
    back_b1 = x_moves(part_b1, -1)
    keep_a1, send_a1 = parts("A", at_a1, a1, core_a1, NZ, at_once, grads)
    back_a1 = ep_move(send_a1, dz=1)
    core_b0 = ep_move(parts("B", at_b0, b0, None, 1, at_once, grads)[0], dc=1)
    core_a0 = ep_move(parts("A", at_a0, a0, None, 1, at_once, grads)[0], dc=1)
    grads = release(grads, part_b1, send_a1)
    part_b0 = parts("B", at_b0, b0, core_b0, NX, unpinned, grads)
    keep_a0, send_a0 = parts("A", at_a0, a0, core_a0, NZ, over_columns, grads)
    grad = use_rows(rows_a1, w_down, hid_at, None, release(grad, grads), at_a1, False, True)
    grad = use_rows(rows_b1, w_down, hid_bt, None, grad, at_b1, False, True)
    back_b1, back_a1, part_b0, keep_a0, send_a0, grad = tie(
        (back_b1, back_a1, part_b0, keep_a0, send_a0, grad)
    )
    back_b0 = x_moves(part_b0, -1)
    back_a0 = ep_move(send_a0, dz=1)
    keep_b1, send_b1 = combine_b(keep_t, send_t, [part_b1[0]] + back_b1)
    cross_b1 = ep_move(send_b1, dz=1)
    sum_a1 = sum_z(keep_a1, back_a1)
    keep_b0, send_b0 = combine_b(keep_t, send_t, [part_b0[0]] + back_b0)
    cross_b1, send_b0, back_a0, sum_a1 = tie((cross_b1, send_b0, back_a0, sum_a1))
    done_b1 = finish_b(at, keep_b1, cross_b1, tok_b1, 0, far_tok1)
    up_b1 = section_move(done_b1, crossing)
    own_a1 = x_exchange(release(sum_a1, done_b1))
    cross_b0 = ep_move(send_b0, dz=1)
    sum_a0 = sum_z(keep_a0, back_a0)
    done_b0 = finish_b(at, keep_b0, cross_b0, tok_b0, 0, far_tok0)
    done_b0, sum_a0, up_b1 = tie((done_b0, sum_a0, up_b1))
    up_b0 = section_move(done_b0, crossing)
    up_a1 = section_move(release(finish_a(place_t, tok1, 0, own_a1), up_b0), swapped)
    own_a0 = x_exchange(sum_a0)
    up_a0 = section_move(finish_a(place_t, tok_a0, 0, own_a0), swapped)
    out = place_chunk(up_b1, width, at_b1, None)
    out = place_chunk(up_b0, width, at_b0, out)
    out = place_chunk(up_a1, width, at_a1, out)
    out = place_chunk(up_a0, width, at_a0, out)
    return (out[None], grad[None])


def solution(mesh):
    placed = (
        P("section", "ep", None),
        P("section", "ep", None),
        P("section", "ep", None),
        P("section", None, "ep"),
        P("section", None, "ep"),
        P("section", None, "ep"),
        P("section", None, "ep"),
        P("section", "ep", None),
    )
    return jax.shard_map(
        body,
        mesh=mesh,
        in_specs=placed,
        out_specs=(P("section", "ep", None), P("section", "ep", None)),
        check_vma=False,
    )
```
